32 devices in a mesh: slab: 2 (over y), docs: 4 (over x, core), blk: 4 (over z).
Axes of the slice: x: 2, y: 2, z: 4, core: 2. Of those that a mesh axis runs over, the one named last changes fastest.
Arguments:
- pooled: bfloat16 [16384, 768], P(('slab', 'docs', 'blk')), parts along dimension 0, may hold values from -6 to 6
- proj_weight: bfloat16 [768, 768], replicated, may hold values from -0.21875 to 0.21875
- cluster: int32 [16384], P(('slab', 'docs', 'blk')), parts along dimension 0, may hold values from 0 to 143, as said below
Outputs:
- best_sim: float32 [16384], P(('slab', 'docs', 'blk')), parts along dimension 0
The draws below stay inside these ranges and needn't reach their ends.
There are 2 independent parts, one for each index of `slab`. The reference program is written for one: setup_inputs(seed, part) draws one part's arguments, and reference() takes and returns one part's arrays. A program takes and returns all parts, laid end to end along the dimension named above; an argument that names none is the same for every part. Nothing has to cross between parts.
Inputs may be any that keep to these rules, and one draw needn't show every extreme that they name: Clusters below 16 are large, the others small. The documents of one device hold exactly 128 of large clusters and 384 of small ones. Among one device's documents at most 64 of large clusters share the value of cluster modulo the size of docs, and at most 48 of small clusters share the value of (cluster - 16) modulo the number of devices of docs and blk; in every draw one value of each kind holds exactly that many on every device.
All inputs are finite; a program needn't handle non-finite values.
Results may differ from the reference program's by a relative error of at most 0.0012.
Values may be sent and summed in bfloat16 or wider, within the bound.
No kernel may reach another device: no remote copies, remote signals or barrier semaphores. Data moves between devices by JAX's collectives and lax.ppermute only.
A program may use at most 64 MiB of HBM per device.

```python
import jax
import jax.numpy as jnp
from jax import lax

D = 768
BIG_OWN = 4
SMALL_OWN = 8
BIG_DEV = 128
SMALL_DEV = 384
LARGE_CL = 16
CAPB = 64
CAPS = 48
DOCS = 8192
N_DOCS = 4
N_BLK = 4


def draw_cluster(key, part):
    devices = N_DOCS * N_BLK
    hot_owner = jax.random.randint(jax.random.fold_in(key, 11), (), 0, N_DOCS).astype(jnp.int32)
    hot_target = jax.random.randint(jax.random.fold_in(key, 12), (), 0, devices).astype(jnp.int32)
    device_keys = jax.random.split(jax.random.fold_in(key, 13), devices)

    def one_device(device_key):
        subkeys = jax.random.split(device_key, 7)
        big_slots = N_DOCS * CAPB
        big_owner = jnp.arange(big_slots, dtype=jnp.int32) // CAPB
        big_pri = jnp.where(big_owner == hot_owner, 0, 1) * big_slots + jax.random.permutation(subkeys[0], big_slots).astype(jnp.int32)
        chosen = jnp.argsort(big_pri)[:BIG_DEV]
        owners = big_owner[chosen]
        big_rank = jnp.minimum(jax.random.randint(subkeys[1], (BIG_DEV,), 0, BIG_OWN), jax.random.randint(subkeys[2], (BIG_DEV,), 0, BIG_OWN))
        big_ids = owners + N_DOCS * big_rank
        small_slots = devices * CAPS
        small_target = jnp.arange(small_slots, dtype=jnp.int32) // CAPS
        small_pri = jnp.where(small_target == hot_target, 0, 1) * small_slots + jax.random.permutation(subkeys[3], small_slots).astype(jnp.int32)
        picked = jnp.argsort(small_pri)[:SMALL_DEV]
        targets = small_target[picked]
        small_rank = jnp.minimum(jax.random.randint(subkeys[4], (SMALL_DEV,), 0, SMALL_OWN), jax.random.randint(subkeys[5], (SMALL_DEV,), 0, SMALL_OWN))
        small_ids = LARGE_CL + targets + devices * small_rank
        all_ids = jnp.concatenate([big_ids, small_ids]).astype(jnp.int32)
        return jax.random.permutation(subkeys[6], all_ids)
    return jax.vmap(one_device)(device_keys).reshape(-1).astype(jnp.int32)


def block_scale(own_key, shape, cuts, smallest, top_value):
    level, own = 1.0, jax.random.fold_in(own_key, 6)
    for axis_at, shards_of in cuts:
        steps = jnp.exp(jax.random.uniform(jax.random.fold_in(own, axis_at), (shards_of,), jnp.float32, smallest / len(cuts), top_value / len(cuts)))
        level = level * jnp.repeat(steps, shape[axis_at] // shards_of).reshape([-1 if axis == axis_at else 1 for axis in range(len(shape))])
    return level


def bell_draw(stream_key, shape, width, reach, shards=(), held_as=jnp.bfloat16):
    drawn = jax.random.normal(stream_key, shape, jnp.float32) * width
    if len(shards) > 0:
        drawn = block_scale(stream_key, shape, shards, -0.22, 0.18) * drawn
    return jnp.clip(drawn, min=-reach, max=reach).astype(held_as)


def setup_inputs(seed: int = 0, part: int = 0) -> dict:
    arg_keys = jax.random.split(jax.random.key(seed), 4)
    part_splits = jax.random.split(jax.random.fold_in(arg_keys[3], part), 4)
    return {
        "pooled": bell_draw(part_splits[0], (DOCS, D), 1.0, 6.0, ((0, 16),)),
        "proj_weight": bell_draw(arg_keys[1], (D, D), D ** -0.5, 0.21875),
        "cluster": draw_cluster(jax.random.fold_in(jax.random.fold_in(arg_keys[3], part), 71), part),
    }


def group_best(embedded, cluster, group_of, groups, capacity):
    total_rows = embedded.shape[0]
    feature = embedded.shape[1]
    positions = jnp.arange(total_rows, dtype=jnp.int32)
    group_key = jnp.where(group_of >= 0, group_of, groups).astype(jnp.int32)
    sort_order = jnp.argsort(group_key * total_rows + positions).astype(jnp.int32)
    sorted_key = group_key[sort_order]
    group_sizes = jax.ops.segment_sum(jnp.ones((total_rows,), jnp.int32), group_key, num_segments=groups + 1)
    starts = (jnp.cumsum(group_sizes) - group_sizes).astype(jnp.int32)
    sorted_rank = positions - starts[sorted_key]
    slot_rank = jnp.zeros((total_rows,), jnp.int32).at[sort_order].set(sorted_rank)
    slot = jnp.where(group_of >= 0, group_key * capacity + slot_rank, groups * capacity).astype(jnp.int32)
    padded = jnp.zeros((groups * capacity, feature), embedded.dtype).at[slot].set(embedded, mode='drop')
    padded_ids = jnp.full((groups * capacity,), -1, jnp.int32).at[slot].set(cluster, mode='drop')
    padded = padded.reshape(groups, capacity, feature)
    padded_ids = padded_ids.reshape(groups, capacity)

    def group_scan(operands):
        block_rows, block_ids = operands
        scores = jnp.dot(block_rows, block_rows.T, preferred_element_type=jnp.float32)
        inside = jnp.arange(capacity, dtype=jnp.int32)
        allowed = (block_ids[:, None] == block_ids[None, :]) & (block_ids[:, None] >= 0) & (inside[:, None] != inside[None, :])
        return lax.optimization_barrier(jnp.max(jnp.where(allowed, scores, -1.0), axis=1))
    best_all = lax.map(group_scan, (padded, padded_ids)).reshape(-1)
    return best_all[jnp.minimum(slot, groups * capacity - 1)]

def reference(pooled, proj_weight, cluster):
    projected = jnp.dot(pooled, proj_weight, preferred_element_type=jnp.float32)
    embedded = (projected / jnp.sqrt(lax.optimization_barrier(jnp.sum(projected * projected, axis=1, keepdims=True)) + 1e-06)).astype(jnp.bfloat16)
    is_big = cluster < LARGE_CL
    big_group = jnp.where(is_big, cluster % N_DOCS, -1).astype(jnp.int32)
    small_group = jnp.where(is_big, -1, (cluster - LARGE_CL) % (N_DOCS * N_BLK)).astype(jnp.int32)
    best_big = group_best(embedded, cluster, big_group, N_DOCS, N_DOCS * N_BLK * CAPB)
    best_small = group_best(embedded, cluster, small_group, N_DOCS * N_BLK, N_DOCS * N_BLK * CAPS)
    return jnp.where(is_big, best_big, best_small)
```

```python
import functools

import jax
import jax.numpy as jnp
from jax import lax
from jax.experimental import pallas as pl
from jax.experimental.pallas import tpu as pltpu
from jax.sharding import PartitionSpec as P

BIG_OWN = 4
LANES = 128
VMEM = pl.BlockSpec(memory_space=pltpu.VMEM)
SMEM = pl.BlockSpec(memory_space=pltpu.SMEM)


def modulo(x, n):
    return x & (n - 1) if n & (n - 1) == 0 else lax.rem(x, jnp.int32(n))


def quotient(x, n):
    if n & (n - 1) == 0:
        return lax.shift_right_logical(x, jnp.int32(n.bit_length() - 1))
    return lax.div(x, jnp.int32(n))


def iota(shape, axis):
    return lax.broadcasted_iota(jnp.int32, shape, axis)


def dot_nt(a, b):
    return lax.dot_general(a, b, (((1,), (1,)), ((), ())), preferred_element_type=jnp.float32)


def tile_of(rows, most=256):
    tile = most
    while rows % tile:
        tile //= 2
    return tile


def home_of(docs, blocks):
    return max(blocks // 2 - 1, 0) + (docs % 2) * (1 if blocks > 1 else 0)


def arrive_kernel(shards, blocks, cap_big, cap_small, pooled_ref, weight_ref, cluster_ref,
                  small_ref, big_ref, ids_ref, where_ref, rows_ref):
    docs = pooled_ref.shape[0]
    devices = shards * blocks
    limit = BIG_OWN * shards
    small_slots = devices * cap_small
    slots = small_slots + shards * cap_big
    buckets = devices + shards

    projected = jnp.dot(pooled_ref[...], weight_ref[...], preferred_element_type=jnp.float32)
    squares = jnp.sum(projected * projected, axis=1, keepdims=True)
    rows_ref[...] = (projected / jnp.sqrt(squares + 1e-06)).astype(jnp.bfloat16)

    cluster = cluster_ref[...]
    is_big = cluster < limit
    owner = modulo(cluster, shards)
    past = jnp.maximum(cluster - limit, 0)
    target = modulo(past, devices)
    bucket = jnp.where(is_big, devices + owner, target)
    quota = jnp.where(is_big, quotient(cluster, shards), quotient(past, devices)) + 1

    padded = -(-buckets // 16) * 16
    hot = (iota((padded, docs), 0) == bucket).astype(jnp.float32)
    earlier = (iota((docs, docs), 0) < iota((docs, docs), 1)).astype(jnp.bfloat16)
    before = jnp.dot(hot.astype(jnp.bfloat16), earlier, preferred_element_type=jnp.float32)
    rank = jnp.sum(before * hot, axis=0, keepdims=True).astype(jnp.int32)
    slot = jnp.where(is_big, small_slots + owner * cap_big + rank, target * cap_small + rank)

    home = max(blocks // 2 - 1, 0) + (modulo(owner, 2) if blocks > 1 else 0)
    where_ref[0:1, :] = jnp.where(is_big, owner * blocks + home, target)
    where_ref[1:2, :] = jnp.where(is_big, cap_small + rank, rank)

    quotas = jnp.broadcast_to(quota.astype(jnp.float32), (8, docs)).astype(jnp.bfloat16)
    for ref, first in ((small_ref, 0), (big_ref, small_slots)):
        tile = tile_of(ref.shape[0])
        for at in range(0, ref.shape[0], tile):
            pick = (iota((tile, docs), 0) + (first + at) == slot).astype(jnp.float32).astype(jnp.bfloat16)
            ref[at:at + tile, :] = jnp.dot(
                pick, rows_ref[...], preferred_element_type=jnp.float32).astype(jnp.bfloat16)
            ids = dot_nt(quotas, pick)
            for lane in range(0, tile, LANES):
                ids_ref[0, (first + at + lane) // LANES:(first + at + lane) // LANES + 1, :] = ids[0:1, lane:lane + LANES]


def ids_kernel(shards, blocks, cap_big, cap_small, me_ref, all_ref, big_from_ref,
               small_row_ref, small_col_ref, big_row_ref, big_col_ref):
    devices = shards * blocks
    small_slots = devices * cap_small
    groups = all_ref.shape[1]
    me = me_ref[0] * blocks + me_ref[1]

    small = small_row_ref.shape[1]
    big = big_row_ref.shape[1]
    small_at = iota((1, small), 1)
    small_from = small_at // cap_small
    small_want = me * cap_small + lax.rem(small_at, jnp.int32(cap_small))
    big_want = small_slots + me_ref[0] * cap_big + lax.rem(iota((1, big), 1), jnp.int32(cap_big))
    small_sum = jnp.zeros((devices, small), jnp.float32)
    big_sum = jnp.zeros((devices, big), jnp.float32)
    for group in range(groups):
        values = all_ref[:, group, :].astype(jnp.bfloat16)
        low, high = group * LANES, (group + 1) * LANES
        if low < small_slots:
            pick = (iota((LANES, small), 0) + low == small_want).astype(jnp.float32).astype(jnp.bfloat16)
            small_sum += jnp.dot(values, pick, preferred_element_type=jnp.float32)
        if high > small_slots:
            pick = (iota((LANES, big), 0) + low == big_want).astype(jnp.float32).astype(jnp.bfloat16)
            big_sum += jnp.dot(values, pick, preferred_element_type=jnp.float32)
    small_row = jnp.sum(
        jnp.where(iota((devices, small), 0) == small_from, small_sum, 0.0), axis=0, keepdims=True)
    big_row = jnp.sum(
        jnp.where(iota((devices, big), 0) == big_from_ref[...], big_sum, 0.0), axis=0, keepdims=True)
    small_row_ref[...] = small_row
    big_row_ref[...] = big_row
    small_col_ref[...] = jnp.broadcast_to(small_row, (LANES, small)).T
    big_col_ref[...] = jnp.broadcast_to(big_row, (LANES, big)).T


def block_best(queries, col_ids, first_row, others, row_ids, first_col):
    scores = dot_nt(queries, others)
    allowed = (col_ids == row_ids) & (row_ids > 0.0)
    if first_row is not None:
        allowed &= (iota(scores.shape, 0) + first_row) != (iota(scores.shape, 1) + first_col)
    return jnp.max(jnp.where(allowed, scores, -1.0), axis=0, keepdims=True)


def small_kernel(rows_ref, row_ref, col_ref, best_ref):
    total = rows_ref.shape[0]
    tile = tile_of(total)
    best = jnp.full((1, total), -1.0, jnp.float32)
    for at in range(0, total, tile):
        best = jnp.maximum(best, block_best(
            rows_ref[at:at + tile, :], col_ref[at:at + tile, 0:1], at, rows_ref[...], row_ref[...], 0))
    best_ref[...] = best


def big_kernel(cap_big, cap_small, parts, *refs):
    blocks = refs[:parts]
    row_ref, col_ref, from_ref, small_ref, back_ref = refs[parts:]
    size = blocks[0].shape[0]
    devices = back_ref.shape[0]
    bests = []
    for col in range(parts):
        best = jnp.full((1, size), -1.0, jnp.float32)
        for row in range(parts):
            same = 0 if row == col else None
            best = jnp.maximum(best, block_best(
                blocks[row][...], col_ref[row * size:(row + 1) * size, 0:1], same,
                blocks[col][...], row_ref[:, col * size:(col + 1) * size], same))
        bests.append(best)
    best_big = jnp.concatenate(bests, axis=1)
    best_small = small_ref[...]

    def spread(best, sources, lane):
        total = best.shape[1]
        mine = jnp.where(iota((devices, total), 0) == sources, best, 0.0)
        place = (iota((total, LANES), 1) == lane).astype(jnp.float32)
        return jnp.dot(mine, place, precision=lax.Precision.HIGHEST, preferred_element_type=jnp.float32)

    small_total = best_small.shape[1]
    big_total = best_big.shape[1]
    back = spread(best_small, iota((1, small_total), 1) // cap_small,
                  lax.rem(iota((small_total, 1), 0), jnp.int32(cap_small)))
    back += spread(best_big, from_ref[...],
                   cap_small + lax.rem(iota((big_total, 1), 0), jnp.int32(cap_big)))
    for device in range(devices):
        back_ref[device, 0:1, :] = back[device:device + 1, :]


def finish_kernel(back_ref, where_ref, out_ref):
    devices = back_ref.shape[0]
    docs = where_ref.shape[1]
    values = jnp.concatenate([back_ref[device, 0:1, :] for device in range(devices)], axis=0)
    pick = (iota((devices, docs), 0) == where_ref[0:1, :]).astype(jnp.float32)
    found = lax.dot_general(values, pick, (((0,), (0,)), ((), ())),
                            precision=lax.Precision.HIGHEST, preferred_element_type=jnp.float32)
    out_ref[...] = jnp.sum(
        jnp.where(iota((LANES, docs), 0) == where_ref[1:2, :], found, 0.0), axis=0, keepdims=True)


def call(kernel, out_shape, in_specs, flops, moved, limit=16, scratch=()):
    multiple = isinstance(out_shape, (tuple, list))
    return pl.pallas_call(
        kernel,
        out_shape=out_shape,
        in_specs=in_specs,
        out_specs=tuple(VMEM for _ in out_shape) if multiple else VMEM,
        scratch_shapes=scratch,
        cost_estimate=pl.CostEstimate(flops=flops, bytes_accessed=moved, transcendentals=0),
        compiler_params=pltpu.CompilerParams(vmem_limit_bytes=limit << 20),
    )


def body(pooled, proj_weight, cluster):
    shards = lax.axis_size("docs")
    blocks = lax.axis_size("blk")
    devices = shards * blocks
    docs = pooled.shape[0]
    feature = proj_weight.shape[1]
    big_count = docs // 4
    small_count = docs - big_count
    cap_big = 2 * big_count // shards
    cap_small = 2 * small_count // devices
    small_slots = devices * cap_small
    slots = small_slots + shards * cap_big
    sizes = (shards, blocks, cap_big, cap_small)
    f32, bf16, i32 = jnp.float32, jnp.bfloat16, jnp.int32
    shape = jax.ShapeDtypeStruct

    send_small, send_big, slot_ids, where = call(
        functools.partial(arrive_kernel, *sizes),
        (shape((small_slots, feature), bf16), shape((shards * cap_big, feature), bf16),
         shape((1, slots // LANES, LANES), f32), shape((8, docs), i32)),
        (VMEM, VMEM, VMEM),
        2 * docs * feature * (pooled.shape[1] + slots), 4 << 20, 32,
        (pltpu.VMEM((docs, feature), bf16),),
    )(pooled, proj_weight, cluster.reshape(1, docs))

    got_small = lax.all_to_all(
        send_small.reshape(devices, cap_small, feature), ("docs", "blk"),
        split_axis=0, concat_axis=0, tiled=True).reshape(small_slots, feature)
    all_ids = lax.all_gather(slot_ids, ("docs", "blk"), axis=0, tiled=True)
    got_big = lax.all_to_all(
        send_big.reshape(shards, cap_big, feature), "docs",
        split_axis=0, concat_axis=0, tiled=True).reshape(shards * cap_big, feature)

    my_docs, my_blk = lax.axis_index("docs"), lax.axis_index("blk")
    others = [[blk for blk in range(blocks) if blk != home_of(d, blocks)] for d in range(shards)]
    parts = [got_big]
    for step in range(blocks - 1):
        pairs = [(d * blocks + others[d][step], d * blocks + home_of(d, blocks)) for d in range(shards)]
        parts.append(lax.ppermute(got_big, ("docs", "blk"), pairs))

    big_total = blocks * shards * cap_big
    order = jnp.asarray([[home_of(d, blocks)] + others[d] for d in range(2)], i32)[my_docs % 2]
    from_blk = jnp.repeat(order, shards * cap_big)
    from_docs = (jnp.arange(big_total, dtype=i32) // cap_big) % shards
    big_from = (from_docs * blocks + from_blk).reshape(1, big_total)

    small_row, small_col, big_row, big_col = call(
        functools.partial(ids_kernel, *sizes),
        (shape((1, small_slots), f32), shape((small_slots, LANES), f32),
         shape((1, big_total), f32), shape((big_total, LANES), f32)),
        (SMEM, VMEM, VMEM),
        2 * devices * slots * slots, 1 << 20,
    )(jnp.stack([my_docs, my_blk]).astype(i32), all_ids, big_from)

    best_small = call(
        small_kernel, shape((1, small_slots), f32), (VMEM, VMEM, VMEM),
        2 * small_slots * small_slots * feature, 2 << 20,
    )(got_small, small_row, small_col)

    back = call(
        functools.partial(big_kernel, cap_big, cap_small, blocks),
        shape((devices, 1, LANES), f32), (VMEM,) * (blocks + 4),
        2 * big_total * big_total * feature, 2 << 20,
    )(*parts, big_row, big_col, big_from, best_small)

    returned = lax.all_to_all(back, ("docs", "blk"), split_axis=0, concat_axis=0, tiled=True)
    out = call(
        finish_kernel, shape((1, docs), f32), (VMEM, VMEM),
        2 * docs * LANES * devices, 1 << 16,
    )(returned, where)
    return out.reshape(docs)


def solution(mesh):
    in_specs = (P(("slab", "docs", "blk"), None), P(), P(("slab", "docs", "blk")))
    out_specs = P(("slab", "docs", "blk"))
    return jax.shard_map(body, mesh=mesh, in_specs=in_specs, out_specs=out_specs, check_vma=False)
```

```python
import functools

import jax
import jax.numpy as jnp
from jax import lax
from jax.experimental import pallas as pl
from jax.experimental.pallas import tpu as pltpu
from jax.sharding import PartitionSpec as P

BIG_OWN = 4
LANES = 128


def modulo(x, n):
    return x & (n - 1) if n & (n - 1) == 0 else lax.rem(x, jnp.int32(n))


def quotient(x, n):
    if n & (n - 1) == 0:
        return lax.shift_right_logical(x, jnp.int32(n.bit_length() - 1))
    return lax.div(x, jnp.int32(n))


def iota(shape, axis):
    return lax.broadcasted_iota(jnp.int32, shape, axis)


def dot_nt(a, b):
    return lax.dot_general(a, b, (((1,), (1,)), ((), ())), preferred_element_type=jnp.float32)


def tile_of(rows, most=256):
    tile = most
    while rows % tile:
        tile //= 2
    return tile


def home_of(docs, blocks):
    return max(blocks // 2 - 1, 0) + (docs & min(blocks - 1, 1))


def sort_kernel(shards, blocks, cap_big, cap_small, pooled_hbm, weight_hbm, cluster_hbm,
                small_hbm, rows_ref, info_ref, pooled_ref, weight_ref, cluster_ref, stage_ref, sems, out_sems):
    docs = pooled_ref.shape[0]
    devices = shards * blocks
    limit = BIG_OWN * shards
    small_slots = devices * cap_small
    buckets = devices + shards

    fetches = [pltpu.make_async_copy(source, target, sems.at[n]) for n, (source, target) in enumerate(
        ((cluster_hbm, cluster_ref), (weight_hbm, weight_ref), (pooled_hbm, pooled_ref)))]
    for fetch in fetches:
        fetch.start()
    fetches[0].wait()

    cluster = cluster_ref[...]
    is_big = cluster < limit
    owner = modulo(cluster, shards)
    past = jnp.maximum(cluster - limit, 0)
    target = modulo(past, devices)
    bucket = jnp.where(is_big, devices + owner, target)
    quota = jnp.where(is_big, quotient(cluster, shards), quotient(past, devices)) + 1

    padded = -(-buckets // 16) * 16
    hot = (iota((padded, docs), 0) == bucket).astype(jnp.float32)
    earlier = (iota((docs, docs), 0) < iota((docs, docs), 1)).astype(jnp.float32).astype(jnp.bfloat16)
    before = jnp.dot(hot.astype(jnp.bfloat16), earlier, preferred_element_type=jnp.float32)
    rank = jnp.sum(before * hot, axis=0, keepdims=True).astype(jnp.int32)
    slot = jnp.where(is_big, small_slots + owner * cap_big + rank, target * cap_small + rank)

    home = home_of(owner, blocks)
    info_ref[0:1, :] = jnp.where(is_big, owner * blocks + home, target)
    info_ref[1:2, :] = jnp.where(is_big, cap_small + rank, rank)
    info_ref[2:3, :] = slot
    info_ref[3:4, :] = quota
    info_ref[4:5, :] = bucket

    for fetch in fetches[1:]:
        fetch.wait()
    projected = jnp.dot(pooled_ref[...], weight_ref[...], preferred_element_type=jnp.float32)
    squares = jnp.sum(projected * projected, axis=1, keepdims=True)
    rows_ref[...] = (projected / jnp.sqrt(squares + 1e-06)).astype(jnp.bfloat16)
    place_rows(rows_ref, slot, 0, stage_ref, small_hbm, out_sems)


def place_rows(rows_ref, slot, first, stage_ref, out_hbm, sems):
    total, docs = stage_ref.shape[0], rows_ref.shape[0]
    tile = total // sems.shape[0]
    sends = []
    for part in range(sems.shape[0]):
        at = part * tile
        pick = (iota((tile, docs), 0) + (first + at) == slot).astype(jnp.float32).astype(jnp.bfloat16)
        stage_ref[at:at + tile, :] = jnp.dot(
            pick, rows_ref[...], preferred_element_type=jnp.float32).astype(jnp.bfloat16)
        send = pltpu.make_async_copy(
            stage_ref.at[pl.ds(at, tile)], out_hbm.at[pl.ds(at, tile)], sems.at[part])
        send.start()
        sends.append(send)
    for send in sends:
        send.wait()


def sort_big_kernel(shards, blocks, cap_big, cap_small, rows_ref, info_ref, big_hbm, ids_hbm,
                    stage_ref, lanes_ref, out_sems, ids_sem):
    docs = rows_ref.shape[0]
    devices = shards * blocks
    lane, slot = info_ref[1:2, :], info_ref[2:3, :]
    quota, bucket = info_ref[3:4, :], info_ref[4:5, :]
    to = iota((devices, docs), 0)
    mine = (to == bucket) | (quotient(to, blocks) + devices == bucket)
    values = jnp.where(mine, quota.astype(jnp.float32), 0.0).astype(jnp.bfloat16)
    place = (iota((LANES, docs), 0) == lane).astype(jnp.float32).astype(jnp.bfloat16)
    store_rows(dot_nt(values, place), lanes_ref)
    send = pltpu.make_async_copy(lanes_ref, ids_hbm, ids_sem)
    send.start()
    place_rows(rows_ref, slot, devices * cap_small, stage_ref, big_hbm, out_sems)
    send.wait()


def store_rows(values, ref):
    for device in range(ref.shape[0]):
        ref[device, 0:1, :] = values[device:device + 1, :]


def load_rows(ref):
    return jnp.concatenate([ref[device, 0:1, :] for device in range(ref.shape[0])], axis=0)


def small_sources(total, cap_small):
    at = iota((1, total), 1)
    return at // cap_small, lax.rem(at, jnp.int32(cap_small))


def big_sources(total, my_docs, shards, blocks, cap_big, cap_small):
    at = iota((1, total), 1)
    part = at // (shards * cap_big)
    home = home_of(my_docs, blocks)
    blk = jnp.where(part == 0, home, jnp.where(part - 1 >= home, part, part - 1))
    docs = modulo(at // cap_big, shards)
    return docs * blocks + blk, cap_small + lax.rem(at, jnp.int32(cap_big))


def ids_kernel(shards, blocks, cap_big, cap_small, me_ref, ids_ref, small_ref, big_ref):
    devices = shards * blocks
    values = load_rows(ids_ref).astype(jnp.bfloat16)
    for ref, (source, lane) in (
        (small_ref, small_sources(small_ref.shape[1], cap_small)),
        (big_ref, big_sources(big_ref.shape[1], me_ref[0], shards, blocks, cap_big, cap_small)),
    ):
        total = ref.shape[1]
        pick = (iota((LANES, total), 0) == lane).astype(jnp.float32).astype(jnp.bfloat16)
        found = jnp.dot(values, pick, preferred_element_type=jnp.float32)
        ref[...] = jnp.sum(
            jnp.where(iota((devices, total), 0) == source, found, 0.0), axis=0, keepdims=True)


def as_column(row):
    return jnp.broadcast_to(row, (LANES, row.shape[1])).T[:, 0:1]


def block_best(queries, col_ids, first_row, others, row_ids, first_col):
    scores = dot_nt(queries, others)
    allowed = (col_ids == row_ids) & (row_ids > 0.0)
    if first_row is not None:
        allowed &= (iota(scores.shape, 0) + first_row) != (iota(scores.shape, 1) + first_col)
    return jnp.max(jnp.where(allowed, scores, -1.0), axis=0, keepdims=True)


def small_kernel(rows_ref, row_ref, best_ref):
    total = rows_ref.shape[0]
    tile = tile_of(total)
    best = jnp.full((1, total), -1.0, jnp.float32)
    for at in range(0, total, tile):
        best = jnp.maximum(best, block_best(
            rows_ref[at:at + tile, :], as_column(row_ref[:, at:at + tile]), at, rows_ref[...], row_ref[...], 0))
    best_ref[...] = best


def big_kernel(shards, blocks, cap_big, cap_small, me_ref, *refs):
    held = refs[:blocks]
    row_ref, small_ref, back_hbm, lanes_ref, sem = refs[blocks:]
    size = held[0].shape[0]
    devices = shards * blocks
    bests = [jnp.full((1, size), -1.0, jnp.float32) for _ in range(blocks)]
    for row in range(blocks):
        col_ids = as_column(row_ref[:, row * size:(row + 1) * size])
        for col in range(blocks):
            same = 0 if row == col else None
            bests[col] = jnp.maximum(bests[col], block_best(
                held[row][...], col_ids, same, held[col][...], row_ref[:, col * size:(col + 1) * size], same))
    best_big = jnp.concatenate(bests, axis=1)
    best_small = small_ref[...]

    def spread(best, source, lane):
        total = best.shape[1]
        mine = jnp.where(iota((devices, total), 0) == source, best, 0.0)
        place = (iota((LANES, total), 0) == lane).astype(jnp.float32)
        return lax.dot_general(mine, place, (((1,), (1,)), ((), ())),
                               precision=lax.Precision.HIGHEST, preferred_element_type=jnp.float32)

    back = spread(best_small, *small_sources(best_small.shape[1], cap_small))
    back += spread(best_big, *big_sources(best_big.shape[1], me_ref[0], shards, blocks, cap_big, cap_small))
    store_rows(back, lanes_ref)
    send = pltpu.make_async_copy(lanes_ref, back_hbm, sem)
    send.start()
    send.wait()


def finish_kernel(back_ref, where_ref, out_ref):
    devices = back_ref.shape[0]
    docs = where_ref.shape[1]
    values = load_rows(back_ref)
    pick = (iota((devices, docs), 0) == where_ref[0:1, :]).astype(jnp.float32)
    found = lax.dot_general(values, pick, (((0,), (0,)), ((), ())),
                            precision=lax.Precision.HIGHEST, preferred_element_type=jnp.float32)
    out_ref[...] = jnp.sum(
        jnp.where(iota((LANES, docs), 0) == where_ref[1:2, :], found, 0.0), axis=0, keepdims=True)


def call(kernel, outs, ins, flops, moved, limit=16, scratch=()):
    specs = [pl.BlockSpec(memory_space=space) for _, _, space in outs]
    return pl.pallas_call(
        kernel,
        out_shape=[space(shape, dtype) if space is pltpu.HBM else jax.ShapeDtypeStruct(shape, dtype)
                   for shape, dtype, space in outs],
        in_specs=[pl.BlockSpec(memory_space=space) for space in ins],
        out_specs=specs,
        scratch_shapes=scratch,
        cost_estimate=pl.CostEstimate(flops=flops, bytes_accessed=moved, transcendentals=0),
        compiler_params=pltpu.CompilerParams(vmem_limit_bytes=limit << 20),
    )


def body(pooled, proj_weight, cluster):
    shards = lax.axis_size("docs")
    blocks = lax.axis_size("blk")
    devices = shards * blocks
    docs = pooled.shape[0]
    feature = proj_weight.shape[1]
    big_count = docs // 4
    small_count = docs - big_count
    cap_big = 2 * big_count // shards
    cap_small = 2 * small_count // devices
    small_slots = devices * cap_small
    big_slots = shards * cap_big
    big_total = blocks * big_slots
    sizes = (shards, blocks, cap_big, cap_small)
    f32, bf16, i32 = jnp.float32, jnp.bfloat16, jnp.int32
    vmem, hbm, smem, dma = pltpu.VMEM, pltpu.HBM, pltpu.SMEM, pltpu.SemaphoreType.DMA

    send_small, rows, info = call(
        functools.partial(sort_kernel, *sizes),
        [((small_slots, feature), bf16, hbm), ((docs, feature), bf16, vmem), ((8, docs), i32, vmem)],
        [hbm, hbm, hbm],
        2 * docs * feature * (pooled.shape[1] + small_slots), 4 << 20, 32,
        [vmem(pooled.shape, bf16), vmem(proj_weight.shape, bf16), vmem((1, docs), i32),
         vmem((small_slots, feature), bf16), dma((3,)), dma((3,))],
    )(pooled, proj_weight, cluster.reshape(1, docs))

    got_small = lax.all_to_all(
        send_small.reshape(devices, cap_small, feature), ("docs", "blk"),
        split_axis=0, concat_axis=0, tiled=True).reshape(small_slots, feature)

    send_big, send_ids = call(
        functools.partial(sort_big_kernel, *sizes),
        [((big_slots, feature), bf16, hbm), ((devices, 1, LANES), f32, hbm)],
        [vmem, vmem],
        2 * docs * feature * big_slots, 2 << 20, 16,
        [vmem((big_slots, feature), bf16), vmem((devices, 1, LANES), f32), dma((1,)), dma],
    )(rows, info)
    got_big = lax.all_to_all(
        send_big.reshape(shards, cap_big, feature), "docs",
        split_axis=0, concat_axis=0, tiled=True).reshape(big_slots, feature)
    got_ids = lax.all_to_all(send_ids, ("docs", "blk"), split_axis=0, concat_axis=0, tiled=True)

    me = lax.axis_index("docs").astype(i32).reshape(1)
    held = [got_big]
    for step in range(blocks - 1):
        homes = [home_of(d, blocks) for d in range(shards)]
        pairs = [(d * blocks + (step if step < homes[d] else step + 1), d * blocks + homes[d])
                 for d in range(shards)]
        held.append(lax.ppermute(got_big, ("docs", "blk"), pairs))

    small_ids, big_ids = call(
        functools.partial(ids_kernel, *sizes),
        [((1, small_slots), f32, vmem), ((1, big_total), f32, vmem)],
        [smem, vmem],
        2 * devices * LANES * (small_slots + big_total), 1 << 16,
    )(me, got_ids)

    best_small, = call(
        small_kernel, [((1, small_slots), f32, vmem)], [vmem, vmem],
        2 * small_slots * small_slots * feature, 2 << 20,
    )(got_small, small_ids)

    back, = call(
        functools.partial(big_kernel, *sizes),
        [((devices, 1, LANES), f32, hbm)],
        [smem] + [vmem] * (blocks + 2),
        2 * big_total * big_total * feature, 2 << 20, 16,
        [vmem((devices, 1, LANES), f32), dma],
    )(me, *held, big_ids, best_small)

    returned = lax.all_to_all(back, ("docs", "blk"), split_axis=0, concat_axis=0, tiled=True)
    out, = call(
        finish_kernel, [((1, docs), f32, vmem)], [vmem, vmem],
        2 * docs * LANES * devices, 1 << 16,
    )(returned, info)
    return out.reshape(docs)


def solution(mesh):
    in_specs = (P(("slab", "docs", "blk"), None), P(), P(("slab", "docs", "blk")))
    out_specs = P(("slab", "docs", "blk"))
    return jax.shard_map(body, mesh=mesh, in_specs=in_specs, out_specs=out_specs, check_vma=False)
```

```python
import functools

import jax
import jax.numpy as jnp
from jax import lax
from jax.experimental import pallas as pl
from jax.experimental.pallas import tpu as pltpu
from jax.sharding import PartitionSpec as P

BIG_OWN = 4
LANES = 128


def modulo(x, n):
    return x & (n - 1) if n & (n - 1) == 0 else lax.rem(x, jnp.int32(n))


def quotient(x, n):
    if n & (n - 1) == 0:
        return lax.shift_right_logical(x, jnp.int32(n.bit_length() - 1))
    return lax.div(x, jnp.int32(n))


def iota(shape, axis):
    return lax.broadcasted_iota(jnp.int32, shape, axis)


def dot_nt(a, b):
    return lax.dot_general(a, b, (((1,), (1,)), ((), ())), preferred_element_type=jnp.float32)


def tile_of(rows, most=256):
    tile = most
    while rows % tile:
        tile //= 2
    return tile


def home_of(docs, blocks):
    return max(blocks // 2 - 1, 0) + (docs & min(blocks - 1, 1))


def sort_kernel(shards, blocks, cap_big, cap_small, pooled_hbm, weight_hbm, cluster_hbm,
                small_hbm, rows_hbm, info_hbm, pooled_ref, weight_ref, cluster_ref, stage_ref, rows_ref, info_ref,
                sems, out_sems):
    docs = pooled_ref.shape[0]
    devices = shards * blocks
    limit = BIG_OWN * shards
    small_slots = devices * cap_small
    buckets = devices + shards

    fetches = [pltpu.make_async_copy(source, target, sems.at[n]) for n, (source, target) in enumerate(
        ((cluster_hbm, cluster_ref), (weight_hbm, weight_ref), (pooled_hbm, pooled_ref)))]
    for fetch in fetches:
        fetch.start()
    fetches[0].wait()

    cluster = cluster_ref[...]
    is_big = cluster < limit
    owner = modulo(cluster, shards)
    past = jnp.maximum(cluster - limit, 0)
    target = modulo(past, devices)
    bucket = jnp.where(is_big, devices + owner, target)
    quota = jnp.where(is_big, quotient(cluster, shards), quotient(past, devices)) + 1

    padded = -(-buckets // 16) * 16
    hot = (iota((padded, docs), 0) == bucket).astype(jnp.float32)
    earlier = (iota((docs, docs), 0) < iota((docs, docs), 1)).astype(jnp.float32).astype(jnp.bfloat16)
    before = jnp.dot(hot.astype(jnp.bfloat16), earlier, preferred_element_type=jnp.float32)
    rank = jnp.sum(before * hot, axis=0, keepdims=True).astype(jnp.int32)
    slot = jnp.where(is_big, small_slots + owner * cap_big + rank, target * cap_small + rank)

    home = home_of(owner, blocks)
    info_ref[0:1, :] = jnp.where(is_big, owner * blocks + home, target)
    info_ref[1:2, :] = jnp.where(is_big, cap_small + rank, rank)
    info_ref[2:3, :] = slot
    info_ref[3:4, :] = quota
    info_ref[4:5, :] = bucket
    info_ref[5:8, :] = jnp.zeros((3, docs), jnp.int32)
    keeps = [pltpu.make_async_copy(info_ref, info_hbm, sems.at[3]),
             pltpu.make_async_copy(rows_ref, rows_hbm, sems.at[4])]
    keeps[0].start()

    for fetch in fetches[1:]:
        fetch.wait()
    projected = jnp.dot(pooled_ref[...], weight_ref[...], preferred_element_type=jnp.float32)
    squares = jnp.sum(projected * projected, axis=1, keepdims=True)
    rows_ref[...] = (projected / jnp.sqrt(squares + 1e-06)).astype(jnp.bfloat16)
    keeps[1].start()

    tile = small_slots // out_sems.shape[0]
    for part in range(out_sems.shape[0]):
        at = part * tile
        stage_ref[at:at + tile, :] = picked_rows(rows_ref, slot, at, tile)
        keeps.append(pltpu.make_async_copy(
            stage_ref.at[pl.ds(at, tile)], small_hbm.at[pl.ds(at, tile)], out_sems.at[part]))
        keeps[-1].start()
    for keep in keeps:
        keep.wait()


def picked_rows(rows_ref, slot, first, count):
    docs = rows_ref.shape[0]
    pick = (iota((count, docs), 0) + first == slot).astype(jnp.float32).astype(jnp.bfloat16)
    return jnp.dot(pick, rows_ref[...], preferred_element_type=jnp.float32).astype(jnp.bfloat16)


def sort_big_kernel(shards, blocks, cap_big, cap_small, me_ref, rows_ref, info_ref, *out_refs):
    docs = rows_ref.shape[0]
    devices = shards * blocks
    lane, slot = info_ref[1:2, :], info_ref[2:3, :]
    quota, bucket = info_ref[3:4, :].astype(jnp.float32), info_ref[4:5, :]
    place = (iota((LANES, docs), 0) == lane).astype(jnp.float32).astype(jnp.bfloat16)
    for shift, ref in enumerate(out_refs):
        to = modulo(me_ref[0] + shift, shards)
        ref[0:cap_big, :] = picked_rows(rows_ref, slot, devices * cap_small + to * cap_big, cap_big)
        table = ref.shape[0] - cap_big
        blk = iota((table, docs), 0)
        mine = (blk < blocks) & ((blk + to * blocks == bucket) | (bucket == devices + to))
        values = jnp.where(mine, quota, 0.0).astype(jnp.bfloat16)
        ref[cap_big:, 0:LANES] = dot_nt(values, place).astype(jnp.bfloat16)
        ref[cap_big:, LANES:] = jnp.zeros((table, ref.shape[1] - LANES), jnp.bfloat16)


def group_kernel(shards, blocks, cap_big, me_ref, *refs):
    held, group_ref, ids_refs = refs[:shards], refs[shards], refs[shards + 1:]
    tables = []
    for shift, ref in enumerate(held):
        group_ref[shift * cap_big:(shift + 1) * cap_big, :] = ref[0:cap_big, :]
        tables.append(ref[cap_big:, 0:LANES].astype(jnp.float32))
    for step, ref in enumerate(ids_refs):
        to = modulo(me_ref[1] + step, blocks)
        ref[...] = jnp.zeros(ref.shape, jnp.float32)
        for shift, table in enumerate(tables):
            ref[shift:shift + 1, :] = jnp.sum(
                jnp.where(iota(table.shape, 0) == to, table, 0.0), axis=0, keepdims=True)


def store_rows(values, ref):
    for device in range(ref.shape[0]):
        ref[device, 0:1, :] = values[device:device + 1, :]


def load_rows(ref):
    return jnp.concatenate([ref[device, 0:1, :] for device in range(ref.shape[0])], axis=0)


def small_sources(total, blocks, cap_small):
    at = iota((1, total), 1)
    source = at // cap_small
    return source // blocks, modulo(source, blocks), lax.rem(at, jnp.int32(cap_small))


def big_sources(total, my_docs, shards, blocks, cap_big, cap_small):
    at = iota((1, total), 1)
    part = at // (shards * cap_big)
    home = home_of(my_docs, blocks)
    blk = jnp.where(part == 0, home, jnp.where(part - 1 >= home, part, part - 1))
    docs = modulo(my_docs + shards - modulo(at // cap_big, shards), shards)
    return docs, blk, cap_small + lax.rem(at, jnp.int32(cap_big))


def ids_kernel(shards, blocks, cap_big, cap_small, me_ref, *refs):
    tables, small_ref, big_ref = refs[:blocks], refs[blocks], refs[blocks + 1]
    high = tables[0].shape[0]
    values = jnp.concatenate([table[...] for table in tables], axis=0)
    values = jnp.concatenate([values, jnp.zeros_like(values)], axis=0).astype(jnp.bfloat16)
    for ref, (docs, blk, lane) in (
        (small_ref, small_sources(small_ref.shape[1], blocks, cap_small)),
        (big_ref, big_sources(big_ref.shape[1], me_ref[0], shards, blocks, cap_big, cap_small)),
    ):
        total = ref.shape[1]
        pick = (iota((LANES, total), 0) == lane).astype(jnp.float32).astype(jnp.bfloat16)
        found = jnp.dot(values, pick, preferred_element_type=jnp.float32)
        row = modulo(me_ref[1] + blocks - blk, blocks) * high + modulo(me_ref[0] + shards - docs, shards)
        ref[...] = jnp.sum(jnp.where(iota(found.shape, 0) == row, found, 0.0), axis=0, keepdims=True)


def as_column(row):
    return jnp.broadcast_to(row, (8, row.shape[1])).T[:, 0:1]


def block_best(queries, col_ids, first_row, others, row_ids, first_col):
    scores = dot_nt(queries, others)
    allowed = (col_ids == row_ids) & (row_ids > 0.0)
    if first_row is not None:
        allowed &= (iota(scores.shape, 0) + first_row) != (iota(scores.shape, 1) + first_col)
    return jnp.max(jnp.where(allowed, scores, -1.0), axis=0, keepdims=True)


def big_kernel(*refs):
    held, row_ref, best_ref = refs[:-2], refs[-2], refs[-1]
    size = held[0].shape[0]
    col_ids = as_column(row_ref[...])
    bests = [jnp.full((1, size), -1.0, jnp.float32) for _ in held]
    for row, queries in enumerate(held):
        for col, others in enumerate(held):
            same = 0 if row == col else None
            bests[col] = jnp.maximum(bests[col], block_best(
                queries[...], col_ids[row * size:(row + 1) * size], same,
                others[...], row_ref[:, col * size:(col + 1) * size], same))
    for col, best in enumerate(bests):
        best_ref[:, col * size:(col + 1) * size] = best


def small_kernel(shards, blocks, cap_big, cap_small, me_ref, rows_ref, row_ref, big_ref,
                 back_hbm, lanes_ref, sem):
    devices = shards * blocks
    total = rows_ref.shape[0]

    def spread(best, docs, blk, lane):
        mine = jnp.where(iota((devices, best.shape[1]), 0) == docs * blocks + blk, best, 0.0)
        place = (iota((LANES, best.shape[1]), 0) == lane).astype(jnp.float32)
        return lax.dot_general(mine, place, (((1,), (1,)), ((), ())),
                               precision=lax.Precision.HIGHEST, preferred_element_type=jnp.float32)

    back = spread(big_ref[...], *big_sources(big_ref.shape[1], me_ref[0], shards, blocks, cap_big, cap_small))
    col_ids = as_column(row_ref[...])
    tile = tile_of(total)
    best = jnp.full((1, total), -1.0, jnp.float32)
    for at in range(0, total, tile):
        best = jnp.maximum(best, block_best(
            rows_ref[at:at + tile, :], col_ids[at:at + tile], at, rows_ref[...], row_ref[...], 0))
    back += spread(best, *small_sources(total, blocks, cap_small))
    store_rows(back, lanes_ref)
    send = pltpu.make_async_copy(lanes_ref, back_hbm, sem)
    send.start()
    send.wait()


def masks_kernel(info_ref, device_ref, lane_ref):
    device_ref[...] = (iota(device_ref.shape, 0) == info_ref[0:1, :]).astype(jnp.float32)
    lane_ref[...] = (iota(lane_ref.shape, 0) == info_ref[1:2, :]).astype(jnp.float32)


def finish_kernel(back_ref, device_ref, lane_ref, out_ref):
    found = lax.dot_general(load_rows(back_ref), device_ref[...], (((0,), (0,)), ((), ())),
                            precision=lax.Precision.HIGHEST, preferred_element_type=jnp.float32)
    out_ref[...] = jnp.sum(jnp.where(lane_ref[...] > 0.0, found, 0.0), axis=0, keepdims=True)


def call(kernel, outs, ins, flops, moved, limit=16, scratch=()):
    specs = [pl.BlockSpec(memory_space=space) for _, _, space in outs]
    return pl.pallas_call(
        kernel,
        out_shape=[space(shape, dtype) if space is pltpu.HBM else jax.ShapeDtypeStruct(shape, dtype)
                   for shape, dtype, space in outs],
        in_specs=[pl.BlockSpec(memory_space=space) for space in ins],
        out_specs=specs,
        scratch_shapes=scratch,
        cost_estimate=pl.CostEstimate(flops=flops, bytes_accessed=moved, transcendentals=0),
        compiler_params=pltpu.CompilerParams(vmem_limit_bytes=limit << 20),
    )


def body(pooled, proj_weight, cluster):
    shards = lax.axis_size("docs")
    blocks = lax.axis_size("blk")
    devices = shards * blocks
    docs = pooled.shape[0]
    feature = proj_weight.shape[1]
    big_count = docs // 4
    small_count = docs - big_count
    cap_big = 2 * big_count // shards
    cap_small = 2 * small_count // devices
    small_slots = devices * cap_small
    big_slots = shards * cap_big
    big_total = blocks * big_slots
    sizes = (shards, blocks, cap_big, cap_small)
    f32, bf16, i32 = jnp.float32, jnp.bfloat16, jnp.int32
    vmem, hbm, smem, dma = pltpu.VMEM, pltpu.HBM, pltpu.SMEM, pltpu.SemaphoreType.DMA

    send_small, rows, info = call(
        functools.partial(sort_kernel, *sizes),
        [((small_slots, feature), bf16, hbm), ((docs, feature), bf16, hbm), ((8, docs), i32, hbm)],
        [hbm, hbm, hbm],
        2 * docs * feature * (pooled.shape[1] + small_slots), 4 << 20, 60,
        [vmem(pooled.shape, bf16), vmem(proj_weight.shape, bf16), vmem((1, docs), i32),
         vmem((small_slots, feature), bf16), vmem((docs, feature), bf16), vmem((8, docs), i32),
         dma((5,)), dma((3,))],
    )(pooled, proj_weight, cluster.reshape(1, docs))

    got_small = lax.all_to_all(
        send_small.reshape(devices, cap_small, feature), ("docs", "blk"),
        split_axis=0, concat_axis=0, tiled=True).reshape(small_slots, feature)

    def along(x, axis, count, by):
        return lax.ppermute(x, axis, [(i, (i + by) % count) for i in range(count)])

    me = jnp.stack([lax.axis_index("docs"), lax.axis_index("blk")]).astype(i32)
    table = -(-blocks // 16) * 16
    sent = call(
        functools.partial(sort_big_kernel, *sizes),
        [((cap_big + table, feature), bf16, vmem)] * shards,
        [smem, vmem, vmem],
        2 * docs * feature * big_slots, 2 << 20,
    )(me, rows, info)
    held = [sent[0]] + [along(sent[by], "docs", shards, by) for by in range(1, shards)]

    high = -(-shards // 8) * 8
    group, *tables = call(
        functools.partial(group_kernel, shards, blocks, cap_big),
        [((big_slots, feature), bf16, vmem)] + [((high, LANES), f32, vmem)] * blocks,
        [smem] + [vmem] * shards,
        big_slots * feature, 1 << 20,
    )(me, *held)

    parts = [group]
    for step in range(blocks - 1):
        homes = [home_of(d, blocks) for d in range(shards)]
        pairs = [(d * blocks + (step if step < homes[d] else step + 1), d * blocks + homes[d])
                 for d in range(shards)]
        parts.append(lax.ppermute(group, ("docs", "blk"), pairs))
    tables = [tables[0]] + [along(tables[by], "blk", blocks, by) for by in range(1, blocks)]

    small_ids, big_ids = call(
        functools.partial(ids_kernel, *sizes),
        [((1, small_slots), f32, vmem), ((1, big_total), f32, vmem)],
        [smem] + [vmem] * blocks,
        2 * high * blocks * LANES * (small_slots + big_total), 1 << 16,
    )(me, *tables)

    best_big, = call(
        big_kernel, [((1, big_total), f32, vmem)], [vmem] * (blocks + 1),
        2 * big_total * big_total * feature, 2 << 20,
    )(*parts, big_ids)

    back, = call(
        functools.partial(small_kernel, *sizes),
        [((devices, 1, LANES), f32, hbm)], [smem, vmem, vmem, vmem],
        2 * small_slots * small_slots * feature, 2 << 20, 16,
        [vmem((devices, 1, LANES), f32), dma],
    )(me, got_small, small_ids, best_big)

    returned = lax.all_to_all(back, ("docs", "blk"), split_axis=0, concat_axis=0, tiled=True)
    masks = call(
        masks_kernel, [((devices, docs), f32, vmem), ((LANES, docs), f32, vmem)], [vmem],
        docs * LANES, 1 << 18,
    )(info)
    out, = call(
        finish_kernel, [((1, docs), f32, vmem)], [vmem, vmem, vmem],
        2 * docs * LANES * devices, 1 << 18,
    )(returned, *masks)
    return out.reshape(docs)


def solution(mesh):
    in_specs = (P(("slab", "docs", "blk"), None), P(), P(("slab", "docs", "blk")))
    out_specs = P(("slab", "docs", "blk"))
    return jax.shard_map(body, mesh=mesh, in_specs=in_specs, out_specs=out_specs, check_vma=False)
```

```python
import functools

import jax
import jax.numpy as jnp
from jax import lax
from jax.experimental import pallas as pl
from jax.experimental.pallas import tpu as pltpu
from jax.sharding import PartitionSpec as P

BIG_OWN = 4
LANES = 128


def modulo(x, n):
    return x & (n - 1) if n & (n - 1) == 0 else lax.rem(x, jnp.int32(n))


def quotient(x, n):
    if n & (n - 1) == 0:
        return lax.shift_right_logical(x, jnp.int32(n.bit_length() - 1))
    return lax.div(x, jnp.int32(n))


def iota(shape, axis):
    return lax.broadcasted_iota(jnp.int32, shape, axis)


def dot_nt(a, b):
    return lax.dot_general(a, b, (((1,), (1,)), ((), ())), preferred_element_type=jnp.float32)


def tile_of(rows, most=256):
    tile = most
    while rows % tile:
        tile //= 2
    return tile


def home_of(docs, blocks):
    return max(blocks // 2 - 1, 0) + (docs & min(blocks - 1, 1))


def sort_kernel(shards, blocks, cap_big, cap_small, relative, me_ref, pooled_hbm, weight_hbm, cluster_hbm, *refs):
    devices = shards * blocks
    (pooled_ref, weight_ref, cluster_ref, rows_ref, info_ref, small_ref, big_ref, sems, small_sems, big_sems) = refs[-10:]
    info_hbm, outs = refs[0], refs[1:-10]
    small_hbm, big_hbm = outs[:-shards], outs[-shards:]
    docs, feature = rows_ref.shape
    limit = BIG_OWN * shards
    small_slots = devices * cap_small
    buckets = devices + shards
    my_docs, my_blk = me_ref[0], me_ref[1]

    fetches = [pltpu.make_async_copy(source, target, sems.at[n]) for n, (source, target) in enumerate(
        ((cluster_hbm, cluster_ref), (weight_hbm, weight_ref), (pooled_hbm, pooled_ref)))]
    for fetch in fetches:
        fetch.start()
    fetches[0].wait()

    cluster = cluster_ref[...]
    is_big = cluster < limit
    owner = modulo(cluster, shards)
    past = jnp.maximum(cluster - limit, 0)
    target = modulo(past, devices)
    bucket = jnp.where(is_big, devices + owner, target)
    quota = (jnp.where(is_big, quotient(cluster, shards), quotient(past, devices)) + 1).astype(jnp.float32)

    padded = -(-buckets // 16) * 16
    hot = (iota((padded, docs), 0) == bucket).astype(jnp.float32)
    earlier = (iota((docs, docs), 0) < iota((docs, docs), 1)).astype(jnp.float32).astype(jnp.bfloat16)
    before = jnp.dot(hot.astype(jnp.bfloat16), earlier, preferred_element_type=jnp.float32)
    rank = jnp.sum(before * hot, axis=0, keepdims=True).astype(jnp.int32)
    lane = jnp.where(is_big, cap_small + rank, rank)

    info_ref[0:1, :] = jnp.where(is_big, owner * blocks + home_of(owner, blocks), target)
    info_ref[1:2, :] = lane
    info_ref[2:8, :] = jnp.zeros((6, docs), jnp.int32)
    sends = [pltpu.make_async_copy(info_ref, info_hbm, sems.at[3])]
    sends[0].start()

    place = (iota((LANES, docs), 0) == lane).astype(jnp.float32).astype(jnp.bfloat16)
    high = big_ref.shape[0] // shards
    table = high - cap_big
    for shift in range(shards):
        to = modulo(my_docs + shift, shards)
        blk = iota((table, docs), 0)
        mine = (blk < blocks) & ((blk + to * blocks == bucket) | (bucket == devices + to))
        values = jnp.where(mine, quota, 0.0).astype(jnp.bfloat16)
        at = shift * high + cap_big
        big_ref[at:at + table, 0:LANES] = dot_nt(values, place).astype(jnp.bfloat16)
        big_ref[at:at + table, LANES:] = jnp.zeros((table, feature - LANES), jnp.bfloat16)

    big_at = modulo(owner + shards - my_docs, shards)
    small_at = target
    if relative:
        small_at = (modulo(quotient(target, blocks) + shards - my_docs, shards) * blocks
                    + modulo(modulo(target, blocks) + blocks - my_blk, blocks))
    big_slot = jnp.where(is_big, big_at * cap_big + rank, -1)
    small_slot = jnp.where(is_big, -1, small_at * cap_small + rank)

    for fetch in fetches[1:]:
        fetch.wait()
    projected = jnp.dot(pooled_ref[...], weight_ref[...], preferred_element_type=jnp.float32)
    squares = jnp.sum(projected * projected, axis=1, keepdims=True)
    rows_ref[...] = (projected / jnp.sqrt(squares + 1e-06)).astype(jnp.bfloat16)

    def picked_rows(slot, first, count):
        pick = (iota((count, docs), 0) + first == slot).astype(jnp.float32).astype(jnp.bfloat16)
        return jnp.dot(pick, rows_ref[...], preferred_element_type=jnp.float32).astype(jnp.bfloat16)

    picked = picked_rows(big_slot, 0, shards * cap_big)
    for shift, out in enumerate(big_hbm):
        big_ref[shift * high:shift * high + cap_big, :] = picked[shift * cap_big:(shift + 1) * cap_big, :]
        sends.append(pltpu.make_async_copy(big_ref.at[pl.ds(shift * high, high)], out, big_sems.at[shift]))
        sends[-1].start()

    rows = small_slots // len(small_hbm)
    tile = rows * (-(-len(small_hbm) // 4)) if relative else rows
    for at in range(0, small_slots, tile):
        small_ref[at:at + tile, :] = picked_rows(small_slot, at, tile)
        for part in range(at // rows, (at + tile) // rows):
            sends.append(pltpu.make_async_copy(
                small_ref.at[pl.ds(part * rows, rows)], small_hbm[part], small_sems.at[part]))
            sends[-1].start()
    for send in sends:
        send.wait()


def group_kernel(shards, blocks, cap_big, me_ref, *refs):
    held, group_ref, ids_refs = refs[:shards], refs[shards], refs[shards + 1:]
    tables = []
    for shift, ref in enumerate(held):
        group_ref[shift * cap_big:(shift + 1) * cap_big, :] = ref[0:cap_big, :]
        tables.append(ref[cap_big:, 0:LANES].astype(jnp.float32))
    for step, ref in enumerate(ids_refs):
        to = modulo(me_ref[1] + step, blocks)
        ref[...] = jnp.zeros(ref.shape, jnp.float32)
        for shift, table in enumerate(tables):
            ref[shift:shift + 1, :] = jnp.sum(
                jnp.where(iota(table.shape, 0) == to, table, 0.0), axis=0, keepdims=True)


def store_rows(values, ref):
    for device in range(ref.shape[0]):
        ref[device, 0:1, :] = values[device:device + 1, :]


def load_rows(ref):
    return jnp.concatenate([ref[device, 0:1, :] for device in range(ref.shape[0])], axis=0)


def small_sources(total, me_ref, shards, blocks, cap_small, relative):
    at = iota((1, total), 1)
    source = at // cap_small
    docs, blk = source // blocks, modulo(source, blocks)
    if relative:
        docs, blk = modulo(me_ref[0] + shards - docs, shards), modulo(me_ref[1] + blocks - blk, blocks)
    return docs, blk, lax.rem(at, jnp.int32(cap_small))


def big_sources(total, my_docs, shards, blocks, cap_big, cap_small):
    at = iota((1, total), 1)
    part = at // (shards * cap_big)
    home = home_of(my_docs, blocks)
    blk = jnp.where(part == 0, home, jnp.where(part - 1 >= home, part, part - 1))
    docs = modulo(my_docs + shards - modulo(at // cap_big, shards), shards)
    return docs, blk, cap_small + lax.rem(at, jnp.int32(cap_big))


def ids_kernel(shards, blocks, cap_big, cap_small, relative, me_ref, *refs):
    tables, small_ref, big_ref = refs[:blocks], refs[blocks], refs[blocks + 1]
    high = tables[0].shape[0]
    values = jnp.concatenate([table[...] for table in tables], axis=0)
    values = jnp.concatenate([values, jnp.zeros_like(values)], axis=0).astype(jnp.bfloat16)
    for ref, (docs, blk, lane) in (
        (small_ref, small_sources(small_ref.shape[1], me_ref, shards, blocks, cap_small, relative)),
        (big_ref, big_sources(big_ref.shape[1], me_ref[0], shards, blocks, cap_big, cap_small)),
    ):
        total = ref.shape[1]
        pick = (iota((LANES, total), 0) == lane).astype(jnp.float32).astype(jnp.bfloat16)
        found = jnp.dot(values, pick, preferred_element_type=jnp.float32)
        row = modulo(me_ref[1] + blocks - blk, blocks) * high + modulo(me_ref[0] + shards - docs, shards)
        ref[...] = jnp.sum(jnp.where(iota(found.shape, 0) == row, found, 0.0), axis=0, keepdims=True)


def as_column(row):
    return jnp.broadcast_to(row, (8, row.shape[1])).T[:, 0:1]


def block_best(queries, col_ids, first_row, others, row_ids, first_col):
    scores = dot_nt(queries, others)
    allowed = (col_ids == row_ids) & (row_ids > 0.0)
    if first_row is not None:
        allowed &= (iota(scores.shape, 0) + first_row) != (iota(scores.shape, 1) + first_col)
    return jnp.max(jnp.where(allowed, scores, -1.0), axis=0, keepdims=True)


def spread(best, docs, blk, lane, shards, blocks):
    total, devices = best.shape[1], shards * blocks
    mine = jnp.where(iota((devices, total), 0) == docs * blocks + blk, best, 0.0)
    place = (iota((LANES, total), 0) == lane).astype(jnp.float32).astype(jnp.bfloat16)
    found = dot_nt(thirds(mine), place)
    return found[:devices] + found[devices:2 * devices] + found[2 * devices:]


def thirds(values):
    high = values.astype(jnp.bfloat16)
    rest = values - high.astype(jnp.float32)
    middle = rest.astype(jnp.bfloat16)
    low = (rest - middle.astype(jnp.float32)).astype(jnp.bfloat16)
    return jnp.concatenate([high, middle, low], axis=0)


def big_kernel(shards, blocks, cap_big, cap_small, me_ref, *refs):
    held, row_ref, back_ref = refs[:-2], refs[-2], refs[-1]
    size = held[0].shape[0]
    col_ids = as_column(row_ref[...])
    bests = [jnp.full((1, size), -1.0, jnp.float32) for _ in held]
    for row, queries in enumerate(held):
        for col, others in enumerate(held):
            same = 0 if row == col else None
            bests[col] = jnp.maximum(bests[col], block_best(
                queries[...], col_ids[row * size:(row + 1) * size], same,
                others[...], row_ref[:, col * size:(col + 1) * size], same))
    best = jnp.concatenate(bests, axis=1)
    back_ref[...] = spread(
        best, *big_sources(best.shape[1], me_ref[0], shards, blocks, cap_big, cap_small), shards, blocks)


def small_kernel(shards, blocks, cap_small, relative, me_ref, *refs):
    parts, (row_ref, big_ref, back_hbm, rows_ref, lanes_ref, sem) = refs[:-6], refs[-6:]
    total = rows_ref.shape[0]
    size = parts[0].shape[0]
    for at, part in enumerate(parts):
        rows_ref[at * size:(at + 1) * size, :] = part[...]
    col_ids = as_column(row_ref[...])
    tile = tile_of(total)
    best = jnp.full((1, total), -1.0, jnp.float32)
    for at in range(0, total, tile):
        best = jnp.maximum(best, block_best(
            rows_ref[at:at + tile, :], col_ids[at:at + tile], at, rows_ref[...], row_ref[...], 0))
    back = spread(best, *small_sources(total, me_ref, shards, blocks, cap_small, relative), shards, blocks)
    store_rows(big_ref[...] + back, lanes_ref)
    send = pltpu.make_async_copy(lanes_ref, back_hbm, sem)
    send.start()
    send.wait()


def masks_kernel(info_ref, device_ref, lane_ref):
    device = (iota((device_ref.shape[0] // 3, device_ref.shape[1]), 0) == info_ref[0:1, :]).astype(jnp.float32)
    device_ref[...] = jnp.concatenate([device] * 3, axis=0).astype(jnp.bfloat16)
    lane_ref[...] = (iota(lane_ref.shape, 0) == info_ref[1:2, :]).astype(jnp.float32)


def finish_kernel(back_ref, device_ref, lane_ref, out_ref):
    found = lax.dot_general(thirds(load_rows(back_ref)), device_ref[...], (((0,), (0,)), ((), ())),
                            preferred_element_type=jnp.float32)
    out_ref[...] = jnp.sum(jnp.where(lane_ref[...] > 0.0, found, 0.0), axis=0, keepdims=True)


def call(kernel, outs, ins, flops, moved, limit=16, scratch=()):
    specs = [pl.BlockSpec(memory_space=space) for _, _, space in outs]
    return pl.pallas_call(
        kernel,
        out_shape=[space(shape, dtype) if space is pltpu.HBM else jax.ShapeDtypeStruct(shape, dtype)
                   for shape, dtype, space in outs],
        in_specs=[pl.BlockSpec(memory_space=space) for space in ins],
        out_specs=specs,
        scratch_shapes=scratch,
        cost_estimate=pl.CostEstimate(flops=flops, bytes_accessed=moved, transcendentals=0),
        compiler_params=pltpu.CompilerParams(vmem_limit_bytes=limit << 20),
    )


def body(pooled, proj_weight, cluster):
    shards = lax.axis_size("docs")
    blocks = lax.axis_size("blk")
    devices = shards * blocks
    docs = pooled.shape[0]
    feature = proj_weight.shape[1]
    big_count = docs // 4
    small_count = docs - big_count
    cap_big = 2 * big_count // shards
    cap_small = 2 * small_count // devices
    small_slots = devices * cap_small
    big_slots = shards * cap_big
    big_total = blocks * big_slots
    sizes = (shards, blocks, cap_big, cap_small)
    f32, bf16, i32 = jnp.float32, jnp.bfloat16, jnp.int32
    vmem, hbm, smem, dma = pltpu.VMEM, pltpu.HBM, pltpu.SMEM, pltpu.SemaphoreType.DMA

    me = jnp.stack([lax.axis_index("docs"), lax.axis_index("blk")]).astype(i32)
    table = -(-blocks // 16) * 16
    relative = devices <= 16
    pieces = devices if relative else 1
    info, *sent = call(
        functools.partial(sort_kernel, *sizes, relative),
        [((8, docs), i32, hbm)] + [((small_slots // pieces, feature), bf16, hbm)] * pieces
        + [((cap_big + table, feature), bf16, hbm)] * shards,
        [smem, hbm, hbm, hbm],
        2 * docs * feature * (pooled.shape[1] + small_slots + big_slots), 5 << 20, 60,
        [vmem(pooled.shape, bf16), vmem(proj_weight.shape, bf16), vmem((1, docs), i32),
         vmem((docs, feature), bf16), vmem((8, docs), i32), vmem((small_slots, feature), bf16),
         vmem((shards * (cap_big + table), feature), bf16), dma((4,)), dma((pieces,)), dma((shards,))],
    )(me, pooled, proj_weight, cluster.reshape(1, docs))
    small_sent, big_sent = sent[:pieces], sent[pieces:]

    def along(x, axis, count, by):
        return lax.ppermute(x, axis, [(i, (i + by) % count) for i in range(count)])

    held = [big_sent[0]] + [along(big_sent[by], "docs", shards, by) for by in range(1, shards)]

    if relative:
        small_got = [None] * devices
        small_got[0] = small_sent[0]
        far_first = sorted(range(blocks), key=lambda by: -min(by, blocks - by))
        for by_blk in far_first:
            for by_docs in range(shards):
                pairs = [(d * blocks + b, (d + by_docs) % shards * blocks + (b + by_blk) % blocks)
                         for d in range(shards) for b in range(blocks)]
                piece = by_docs * blocks + by_blk
                if piece:
                    small_got[piece] = lax.ppermute(small_sent[piece], ("docs", "blk"), pairs)
    else:
        small_got = [lax.all_to_all(
            small_sent[0].reshape(devices, cap_small, feature), ("docs", "blk"),
            split_axis=0, concat_axis=0, tiled=True).reshape(small_slots, feature)]

    high = -(-shards // 8) * 8
    group, *tables = call(
        functools.partial(group_kernel, shards, blocks, cap_big),
        [((big_slots, feature), bf16, vmem)] + [((high, LANES), f32, vmem)] * blocks,
        [smem] + [vmem] * shards,
        big_slots * feature, 1 << 20,
    )(me, *held)

    parts = [group]
    for step in range(blocks - 1):
        homes = [home_of(d, blocks) for d in range(shards)]
        pairs = [(d * blocks + (step if step < homes[d] else step + 1), d * blocks + homes[d])
                 for d in range(shards)]
        parts.append(lax.ppermute(group, ("docs", "blk"), pairs))
    tables = [tables[0]] + [along(tables[by], "blk", blocks, by) for by in range(1, blocks)]

    small_ids, big_ids = call(
        functools.partial(ids_kernel, *sizes, relative),
        [((1, small_slots), f32, vmem), ((1, big_total), f32, vmem)],
        [smem] + [vmem] * blocks,
        2 * high * blocks * LANES * (small_slots + big_total), 1 << 16,
    )(me, *tables)

    back_big, = call(
        functools.partial(big_kernel, *sizes),
        [((devices, LANES), f32, vmem)], [smem] + [vmem] * (blocks + 1),
        2 * big_total * big_total * feature, 2 << 20,
    )(me, *parts, big_ids)

    back, = call(
        functools.partial(small_kernel, shards, blocks, cap_small, relative),
        [((devices, 1, LANES), f32, hbm)], [smem] + [vmem] * (pieces + 2),
        2 * small_slots * small_slots * feature, 2 << 20, 16,
        [vmem((small_slots, feature), bf16), vmem((devices, 1, LANES), f32), dma],
    )(me, *small_got, small_ids, back_big)

    returned = lax.all_to_all(back, ("docs", "blk"), split_axis=0, concat_axis=0, tiled=True)
    masks = call(
        masks_kernel, [((3 * devices, docs), bf16, vmem), ((LANES, docs), f32, vmem)], [vmem],
        docs * LANES, 1 << 18,
    )(info)
    out, = call(
        finish_kernel, [((1, docs), f32, vmem)], [vmem, vmem, vmem],
        2 * docs * LANES * devices, 1 << 18,
    )(returned, *masks)
    return out.reshape(docs)


def solution(mesh):
    in_specs = (P(("slab", "docs", "blk"), None), P(), P(("slab", "docs", "blk")))
    out_specs = P(("slab", "docs", "blk"))
    return jax.shard_map(body, mesh=mesh, in_specs=in_specs, out_specs=out_specs, check_vma=False)
```

```python
import functools

import jax
import jax.numpy as jnp
from jax import lax
from jax.experimental import pallas as pl
from jax.experimental.pallas import tpu as pltpu
from jax.sharding import PartitionSpec as P

BIG_OWN = 4
LANES = 128


def modulo(x, n):
    return x & (n - 1) if n & (n - 1) == 0 else lax.rem(x, jnp.int32(n))


def quotient(x, n):
    if n & (n - 1) == 0:
        return lax.shift_right_logical(x, jnp.int32(n.bit_length() - 1))
    return lax.div(x, jnp.int32(n))


def iota(shape, axis):
    return lax.broadcasted_iota(jnp.int32, shape, axis)


def dot_nt(a, b):
    return lax.dot_general(a, b, (((1,), (1,)), ((), ())), preferred_element_type=jnp.float32)


def tile_of(rows, most=256):
    tile = most
    while rows % tile:
        tile //= 2
    return tile


def home_of(docs, blocks):
    return max(blocks // 2 - 1, 0) + (docs & min(blocks - 1, 1))


def picked_rows(rows_ref, slot, first, count):
    pick = (iota((count, rows_ref.shape[0]), 0) + first == slot).astype(jnp.float32).astype(jnp.bfloat16)
    return jnp.dot(pick, rows_ref[...], preferred_element_type=jnp.float32).astype(jnp.bfloat16)


def sort_kernel(shards, blocks, cap_big, cap_small, me_ref, pooled_hbm, weight_hbm, cluster_hbm, *refs):
    pooled_ref, weight_ref, cluster_ref, rows_ref, info_ref, big_ref, sems, big_sems = refs[-8:]
    rows_hbm, info_hbm, big_hbm = refs[0], refs[1], refs[2:-8]
    docs = rows_ref.shape[0]
    devices = shards * blocks
    limit = BIG_OWN * shards
    buckets = devices + shards

    fetches = [pltpu.make_async_copy(source, target, sems.at[n]) for n, (source, target) in enumerate(
        ((cluster_hbm, cluster_ref), (weight_hbm, weight_ref), (pooled_hbm, pooled_ref)))]
    for fetch in fetches:
        fetch.start()
    fetches[0].wait()

    cluster = cluster_ref[...]
    is_big = cluster < limit
    owner = modulo(cluster, shards)
    past = jnp.maximum(cluster - limit, 0)
    target = modulo(past, devices)
    bucket = jnp.where(is_big, devices + owner, target)

    padded = -(-buckets // 16) * 16
    hot = (iota((padded, docs), 0) == bucket).astype(jnp.float32)
    earlier = (iota((docs, docs), 0) < iota((docs, docs), 1)).astype(jnp.float32).astype(jnp.bfloat16)
    before = jnp.dot(hot.astype(jnp.bfloat16), earlier, preferred_element_type=jnp.float32)
    rank = jnp.sum(before * hot, axis=0, keepdims=True).astype(jnp.int32)

    info_ref[0:1, :] = jnp.where(is_big, owner * blocks + home_of(owner, blocks), target)
    info_ref[1:2, :] = jnp.where(is_big, cap_small + rank, rank)
    info_ref[2:3, :] = jnp.where(is_big, -1, target * cap_small + rank)
    info_ref[3:4, :] = jnp.where(is_big, quotient(cluster, shards), quotient(past, devices)) + 1
    info_ref[4:5, :] = bucket
    info_ref[5:8, :] = jnp.zeros((3, docs), jnp.int32)
    sends = [pltpu.make_async_copy(info_ref, info_hbm, sems.at[3])]
    sends[0].start()

    for fetch in fetches[1:]:
        fetch.wait()
    projected = jnp.dot(pooled_ref[...], weight_ref[...], preferred_element_type=jnp.float32)
    squares = jnp.sum(projected * projected, axis=1, keepdims=True)
    rows_ref[...] = (projected / jnp.sqrt(squares + 1e-06)).astype(jnp.bfloat16)
    sends.append(pltpu.make_async_copy(rows_ref, rows_hbm, sems.at[4]))
    sends[-1].start()

    kinds = 2 if blocks > 1 and shards > 1 else 1
    half = shards // kinds * cap_big
    place = modulo(owner, kinds) * half + owner // kinds * cap_big + rank
    big_ref[...] = picked_rows(rows_ref, jnp.where(is_big, place, -1), 0, shards * cap_big)
    for step, out in enumerate(big_hbm):
        kind = kind_of(me_ref[1] - step + blocks, blocks, kinds)
        sends.append(pltpu.make_async_copy(
            big_ref.at[pl.ds(pl.multiple_of(kind * half, half), half)], out, big_sems.at[step]))
        sends[-1].start()
    for send in sends:
        send.wait()


def kind_of(blk, blocks, kinds):
    return jnp.where(modulo(blk, blocks) == home_of(1, blocks), kinds - 1, 0)


def sort_small_kernel(shards, blocks, cap_small, me_ref, rows_ref, info_ref, small_hbm, *refs):
    ids_refs, (small_ref, sems) = refs[:-2], refs[-2:]
    docs = rows_ref.shape[0]
    devices = shards * blocks
    slot = info_ref[2:3, :]
    tile = small_ref.shape[0] // sems.shape[0]
    sends = []
    for part in range(sems.shape[0]):
        small_ref[part * tile:(part + 1) * tile, :] = picked_rows(rows_ref, slot, part * tile, tile)
        sends.append(pltpu.make_async_copy(
            small_ref.at[pl.ds(part * tile, tile)], small_hbm.at[pl.ds(part * tile, tile)], sems.at[part]))
        sends[-1].start()
    quota, bucket = info_ref[3:4, :].astype(jnp.float32), info_ref[4:5, :]
    place = (iota((LANES, docs), 0) == info_ref[1:2, :]).astype(jnp.float32).astype(jnp.bfloat16)
    for shift, ref in enumerate(ids_refs):
        to = modulo(me_ref[0] + shift, shards)
        blk = iota((2 * ref.shape[0], docs), 0)
        mine = (blk < blocks) & ((blk + to * blocks == bucket) | (bucket == devices + to))
        values = jnp.where(mine, quota, 0.0).astype(jnp.bfloat16)
        ref[...] = dot_nt(values, place)[0:ref.shape[0], :]
    for send in sends:
        send.wait()


def group_kernel(shards, blocks, cap_big, me_ref, *refs):
    held, outs = refs[:blocks], refs[blocks:]
    kinds = 2 if blocks > 1 and shards > 1 else 1
    for shift, out in enumerate(outs):
        at = pl.multiple_of(modulo(me_ref[0] + shards - shift, shards) // kinds * cap_big, cap_big)
        for step, block in enumerate(held):
            out[step * cap_big:(step + 1) * cap_big, :] = block[pl.ds(at, cap_big), :]


def turn_kernel(blocks, me_ref, *refs):
    held, outs = refs[:-blocks], refs[-blocks:]
    for step, out in enumerate(outs):
        to = modulo(me_ref[1] + step, blocks)
        out[...] = jnp.zeros(out.shape, jnp.float32)
        for shift, table in enumerate(held):
            out[shift:shift + 1, :] = jnp.sum(
                jnp.where(iota(table.shape, 0) == to, table[...], 0.0), axis=0, keepdims=True)


def store_rows(values, ref):
    for device in range(ref.shape[0]):
        ref[device, 0:1, :] = values[device:device + 1, :]


def load_rows(ref):
    return jnp.concatenate([ref[device, 0:1, :] for device in range(ref.shape[0])], axis=0)


def small_sources(total, blocks, cap_small):
    at = iota((1, total), 1)
    source = at // cap_small
    return source // blocks, modulo(source, blocks), lax.rem(at, jnp.int32(cap_small))


def big_sources(total, me_ref, shards, blocks, cap_big, cap_small):
    at = iota((1, total), 1)
    part, step = at // (blocks * cap_big), modulo(at // cap_big, blocks)
    return (modulo(me_ref[0] + part, shards), modulo(me_ref[1] + step, blocks),
            cap_small + lax.rem(at, jnp.int32(cap_big)))


def ids_kernel(shards, blocks, cap_big, cap_small, me_ref, *refs):
    tables, small_ref, big_ref = refs[:blocks], refs[blocks], refs[blocks + 1]
    high = tables[0].shape[0]
    values = jnp.concatenate([table[...] for table in tables], axis=0)
    values = jnp.concatenate([values, jnp.zeros_like(values)], axis=0).astype(jnp.bfloat16)
    for ref, (docs, blk, lane) in (
        (small_ref, small_sources(small_ref.shape[1], blocks, cap_small)),
        (big_ref, big_sources(big_ref.shape[1], me_ref, shards, blocks, cap_big, cap_small)),
    ):
        total = ref.shape[1]
        pick = (iota((LANES, total), 0) == lane).astype(jnp.float32).astype(jnp.bfloat16)
        found = jnp.dot(values, pick, preferred_element_type=jnp.float32)
        row = modulo(me_ref[1] + blocks - blk, blocks) * high + modulo(me_ref[0] + shards - docs, shards)
        ref[...] = jnp.sum(jnp.where(iota(found.shape, 0) == row, found, 0.0), axis=0, keepdims=True)


def as_column(row):
    return jnp.broadcast_to(row, (8, row.shape[1])).T[:, 0:1]


def block_best(queries, col_ids, first_row, others, row_ids, first_col):
    scores = dot_nt(queries, others)
    allowed = (col_ids == row_ids) & (row_ids > 0.0)
    if first_row is not None:
        allowed &= (iota(scores.shape, 0) + first_row) != (iota(scores.shape, 1) + first_col)
    return jnp.max(jnp.where(allowed, scores, -1.0), axis=0, keepdims=True)


def spread(best, docs, blk, lane, shards, blocks):
    total, devices = best.shape[1], shards * blocks
    mine = jnp.where(iota((devices, total), 0) == docs * blocks + blk, best, 0.0)
    place = (iota((LANES, total), 0) == lane).astype(jnp.float32).astype(jnp.bfloat16)
    found = dot_nt(thirds(mine), place)
    return found[:devices] + found[devices:2 * devices] + found[2 * devices:]


def thirds(values):
    high = values.astype(jnp.bfloat16)
    rest = values - high.astype(jnp.float32)
    middle = rest.astype(jnp.bfloat16)
    low = (rest - middle.astype(jnp.float32)).astype(jnp.bfloat16)
    return jnp.concatenate([high, middle, low], axis=0)


def big_kernel(shards, blocks, cap_big, cap_small, me_ref, *refs):
    held, row_ref, back_ref = refs[:-2], refs[-2], refs[-1]
    size = held[0].shape[0]
    col_ids = as_column(row_ref[...])
    bests = [jnp.full((1, size), -1.0, jnp.float32) for _ in held]
    for row, queries in enumerate(held):
        for col, others in enumerate(held):
            same = 0 if row == col else None
            bests[col] = jnp.maximum(bests[col], block_best(
                queries[...], col_ids[row * size:(row + 1) * size], same,
                others[...], row_ref[:, col * size:(col + 1) * size], same))
    best = jnp.concatenate(bests, axis=1)
    back_ref[...] = spread(
        best, *big_sources(best.shape[1], me_ref, shards, blocks, cap_big, cap_small), shards, blocks)


def small_kernel(shards, blocks, cap_small, rows_ref, row_ref, big_ref, back_hbm, lanes_ref, sem):
    total = rows_ref.shape[0]
    col_ids = as_column(row_ref[...])
    tile = tile_of(total)
    best = jnp.full((1, total), -1.0, jnp.float32)
    for at in range(0, total, tile):
        best = jnp.maximum(best, block_best(
            rows_ref[at:at + tile, :], col_ids[at:at + tile], at, rows_ref[...], row_ref[...], 0))
    back = spread(best, *small_sources(total, blocks, cap_small), shards, blocks)
    store_rows(big_ref[...] + back, lanes_ref)
    send = pltpu.make_async_copy(lanes_ref, back_hbm, sem)
    send.start()
    send.wait()


def masks_kernel(info_ref, device_ref, lane_ref):
    device = (iota((device_ref.shape[0] // 3, device_ref.shape[1]), 0) == info_ref[0:1, :]).astype(jnp.float32)
    device_ref[...] = jnp.concatenate([device] * 3, axis=0).astype(jnp.bfloat16)
    lane_ref[...] = (iota(lane_ref.shape, 0) == info_ref[1:2, :]).astype(jnp.float32)


def finish_kernel(back_ref, device_ref, lane_ref, out_ref):
    found = lax.dot_general(thirds(load_rows(back_ref)), device_ref[...], (((0,), (0,)), ((), ())),
                            preferred_element_type=jnp.float32)
    out_ref[...] = jnp.sum(jnp.where(lane_ref[...] > 0.0, found, 0.0), axis=0, keepdims=True)


def call(kernel, outs, ins, flops, moved, limit=16, scratch=()):
    specs = [pl.BlockSpec(memory_space=space) for _, _, space in outs]
    return pl.pallas_call(
        kernel,
        out_shape=[space(shape, dtype) if space is pltpu.HBM else jax.ShapeDtypeStruct(shape, dtype)
                   for shape, dtype, space in outs],
        in_specs=[pl.BlockSpec(memory_space=space) for space in ins],
        out_specs=specs,
        scratch_shapes=scratch,
        cost_estimate=pl.CostEstimate(flops=flops, bytes_accessed=moved, transcendentals=0),
        compiler_params=pltpu.CompilerParams(vmem_limit_bytes=limit << 20),
    )


def body(pooled, proj_weight, cluster):
    shards = lax.axis_size("docs")
    blocks = lax.axis_size("blk")
    devices = shards * blocks
    docs = pooled.shape[0]
    feature = proj_weight.shape[1]
    big_count = docs // 4
    small_count = docs - big_count
    cap_big = 2 * big_count // shards
    cap_small = 2 * small_count // devices
    small_slots = devices * cap_small
    big_slots = shards * cap_big
    big_total = blocks * big_slots
    sizes = (shards, blocks, cap_big, cap_small)
    f32, bf16, i32 = jnp.float32, jnp.bfloat16, jnp.int32
    vmem, hbm, smem, dma = pltpu.VMEM, pltpu.HBM, pltpu.SMEM, pltpu.SemaphoreType.DMA

    me = jnp.stack([lax.axis_index("docs"), lax.axis_index("blk")]).astype(i32)
    kinds = 2 if blocks > 1 and shards > 1 else 1
    half = big_slots // kinds
    rows, info, *big_sent = call(
        functools.partial(sort_kernel, *sizes),
        [((docs, feature), bf16, hbm), ((8, docs), i32, hbm)] + [((half, feature), bf16, hbm)] * blocks,
        [smem, hbm, hbm, hbm],
        2 * docs * feature * (pooled.shape[1] + big_slots), 4 << 20, 60,
        [vmem(pooled.shape, bf16), vmem(proj_weight.shape, bf16), vmem((1, docs), i32),
         vmem((docs, feature), bf16), vmem((8, docs), i32), vmem((big_slots, feature), bf16),
         dma((5,)), dma((blocks,))],
    )(me, pooled, proj_weight, cluster.reshape(1, docs))

    homes = [home_of(d, blocks) for d in range(kinds)]
    big_held = [big_sent[0]]
    for step in range(1, blocks):
        pairs = [(d * blocks + (home + step) % blocks, d * blocks + home) for d in range(shards) for home in homes]
        big_held.append(lax.ppermute(big_sent[step], ("docs", "blk"), pairs))

    table = -(-blocks // 8) * 8
    small_sent, *tables = call(
        functools.partial(sort_small_kernel, shards, blocks, cap_small),
        [((small_slots, feature), bf16, hbm)] + [((table, LANES), f32, vmem)] * shards,
        [smem, vmem, vmem],
        2 * docs * feature * small_slots, 2 << 20, 16,
        [vmem((small_slots, feature), bf16), dma((3,))],
    )(me, rows, info)

    got_small = lax.all_to_all(
        small_sent.reshape(devices, cap_small, feature), ("docs", "blk"),
        split_axis=0, concat_axis=0, tiled=True).reshape(small_slots, feature)

    def along(x, axis, count, by):
        return lax.ppermute(x, axis, [(i, (i + by) % count) for i in range(count)])

    tables = [tables[0]] + [along(tables[by], "docs", shards, by) for by in range(1, shards)]

    grouped = call(
        functools.partial(group_kernel, shards, blocks, cap_big),
        [((blocks * cap_big, feature), bf16, vmem)] * shards,
        [smem] + [vmem] * blocks,
        shards * blocks * cap_big * feature, 4 << 20,
    )(me, *big_held)
    parts = [grouped[0]]
    for shift in range(1, shards):
        pairs = [((d + shift) % shards * blocks + home_of(d, blocks), d * blocks + home_of(d, blocks))
                 for d in range(shards)]
        parts.append(lax.ppermute(grouped[shift], ("docs", "blk"), pairs))

    high = -(-shards // 8) * 8
    tables = call(
        functools.partial(turn_kernel, blocks),
        [((high, LANES), f32, vmem)] * blocks, [smem] + [vmem] * shards,
        shards * blocks * LANES, 1 << 16,
    )(me, *tables)
    tables = [tables[0]] + [along(tables[by], "blk", blocks, by) for by in range(1, blocks)]

    small_ids, big_ids = call(
        functools.partial(ids_kernel, *sizes),
        [((1, small_slots), f32, vmem), ((1, big_total), f32, vmem)],
        [smem] + [vmem] * blocks,
        2 * high * blocks * LANES * (small_slots + big_total), 1 << 16,
    )(me, *tables)

    back_big, = call(
        functools.partial(big_kernel, *sizes),
        [((devices, LANES), f32, vmem)], [smem] + [vmem] * (shards + 1),
        2 * big_total * big_total * feature, 2 << 20,
    )(me, *parts, big_ids)

    back, = call(
        functools.partial(small_kernel, shards, blocks, cap_small),
        [((devices, 1, LANES), f32, hbm)], [vmem, vmem, vmem],
        2 * small_slots * small_slots * feature, 2 << 20, 16,
        [vmem((devices, 1, LANES), f32), dma],
    )(got_small, small_ids, back_big)

    returned = lax.all_to_all(back, ("docs", "blk"), split_axis=0, concat_axis=0, tiled=True)
    masks = call(
        masks_kernel, [((3 * devices, docs), bf16, vmem), ((LANES, docs), f32, vmem)], [vmem],
        docs * LANES, 1 << 18,
    )(info)
    out, = call(
        finish_kernel, [((1, docs), f32, vmem)], [vmem, vmem, vmem],
        2 * docs * LANES * devices, 1 << 18,
    )(returned, *masks)
    return out.reshape(docs)


def solution(mesh):
    in_specs = (P(("slab", "docs", "blk"), None), P(), P(("slab", "docs", "blk")))
    out_specs = P(("slab", "docs", "blk"))
    return jax.shard_map(body, mesh=mesh, in_specs=in_specs, out_specs=out_specs, check_vma=False)
```

```python
import functools

import jax
import jax.numpy as jnp
from jax import lax
from jax.experimental import pallas as pl
from jax.experimental.pallas import tpu as pltpu
from jax.sharding import PartitionSpec as P

BIG_OWN = 4
LANES = 128


def modulo(x, n):
    return x & (n - 1) if n & (n - 1) == 0 else lax.rem(x, jnp.int32(n))


def quotient(x, n):
    if n & (n - 1) == 0:
        return lax.shift_right_logical(x, jnp.int32(n.bit_length() - 1))
    return lax.div(x, jnp.int32(n))


def iota(shape, axis):
    return lax.broadcasted_iota(jnp.int32, shape, axis)


def dot_nt(a, b):
    return lax.dot_general(a, b, (((1,), (1,)), ((), ())), preferred_element_type=jnp.float32)


def tile_of(rows, most=256):
    tile = most
    while rows % tile:
        tile //= 2
    return tile


def home_of(docs, blocks):
    return max(blocks // 2 - 1, 0) + (docs & min(blocks - 1, 1))


def picked_rows(rows_ref, slot, first, count):
    pick = (iota((count, rows_ref.shape[0]), 0) + first == slot).astype(jnp.float32).astype(jnp.bfloat16)
    return jnp.dot(pick, rows_ref[...], preferred_element_type=jnp.float32).astype(jnp.bfloat16)


def sort_kernel(shards, blocks, cap_big, cap_small, docs_at, blk_at, pooled_hbm, weight_hbm, cluster_hbm, *refs):
    pooled_ref, weight_ref, cluster_ref, rows_ref, info_ref, big_ref, ids_ref, sems, big_sems, ids_sems = refs[-10:]
    rows_hbm, info_hbm, big_hbm, ids_hbm = refs[0], refs[1], refs[2:2 + blocks], refs[2 + blocks:-10]
    docs = rows_ref.shape[0]
    devices = shards * blocks
    limit = BIG_OWN * shards
    buckets = devices + shards

    fetches = [pltpu.make_async_copy(source, target, sems.at[n]) for n, (source, target) in enumerate(
        ((cluster_hbm, cluster_ref), (weight_hbm, weight_ref), (pooled_hbm, pooled_ref)))]
    for fetch in fetches:
        fetch.start()
    fetches[0].wait()

    cluster = cluster_ref[...]
    is_big = cluster < limit
    owner = modulo(cluster, shards)
    past = jnp.maximum(cluster - limit, 0)
    target = modulo(past, devices)
    bucket = jnp.where(is_big, devices + owner, target)

    padded = -(-buckets // 16) * 16
    hot = (iota((padded, docs), 0) == bucket).astype(jnp.float32)
    earlier = (iota((docs, docs), 0) < iota((docs, docs), 1)).astype(jnp.float32).astype(jnp.bfloat16)
    before = jnp.dot(hot.astype(jnp.bfloat16), earlier, preferred_element_type=jnp.float32)
    rank = jnp.sum(before * hot, axis=0, keepdims=True).astype(jnp.int32)

    lane = jnp.where(is_big, cap_small + rank, rank)
    quota = jnp.where(is_big, quotient(cluster, shards), quotient(past, devices)) + 1
    info_ref[0:1, :] = jnp.where(is_big, owner * blocks + home_of(owner, blocks), target)
    info_ref[1:2, :] = lane
    info_ref[2:3, :] = jnp.where(is_big, -1, target * cap_small + rank)
    info_ref[3:8, :] = jnp.zeros((5, docs), jnp.int32)
    sends = [pltpu.make_async_copy(info_ref, info_hbm, sems.at[3])]
    sends[0].start()

    lanes = (iota((LANES, docs), 0) == lane).astype(jnp.float32).astype(jnp.bfloat16)
    high = ids_ref.shape[1]
    for shift, out in enumerate(ids_hbm):
        to = modulo(docs_at[0] + shift, shards)
        blk = iota((2 * high, docs), 0)
        mine = (blk < blocks) & ((blk + to * blocks == bucket) | (bucket == devices + to))
        values = jnp.where(mine, quota.astype(jnp.float32), 0.0).astype(jnp.bfloat16)
        ids_ref[shift] = dot_nt(values, lanes)[0:high, :]
        sends.append(pltpu.make_async_copy(ids_ref.at[shift], out, ids_sems.at[shift]))
        sends[-1].start()

    for fetch in fetches[1:]:
        fetch.wait()
    projected = jnp.dot(pooled_ref[...], weight_ref[...], preferred_element_type=jnp.float32)
    squares = jnp.sum(projected * projected, axis=1, keepdims=True)
    rows_ref[...] = (projected / jnp.sqrt(squares + 1e-06)).astype(jnp.bfloat16)
    sends.append(pltpu.make_async_copy(rows_ref, rows_hbm, sems.at[4]))
    sends[-1].start()

    kinds = 2 if blocks > 1 and shards > 1 else 1
    half = shards // kinds * cap_big
    place = modulo(owner, kinds) * half + owner // kinds * cap_big + rank
    big_ref[...] = picked_rows(rows_ref, jnp.where(is_big, place, -1), 0, shards * cap_big)
    for step, out in enumerate(big_hbm):
        kind = kind_of(blk_at[0] - step + blocks, blocks, kinds)
        sends.append(pltpu.make_async_copy(
            big_ref.at[pl.ds(pl.multiple_of(kind * half, half), half)], out, big_sems.at[step]))
        sends[-1].start()
    for send in sends:
        send.wait()


def kind_of(blk, blocks, kinds):
    return jnp.where(modulo(blk, blocks) == home_of(1, blocks), kinds - 1, 0)


def sort_small_kernel(rows_ref, info_ref, small_hbm, small_ref, sems):
    tile = small_ref.shape[0] // sems.shape[0]
    sends = []
    for part in range(sems.shape[0]):
        small_ref[part * tile:(part + 1) * tile, :] = picked_rows(rows_ref, info_ref[2:3, :], part * tile, tile)
        sends.append(pltpu.make_async_copy(
            small_ref.at[pl.ds(part * tile, tile)], small_hbm.at[pl.ds(part * tile, tile)], sems.at[part]))
        sends[-1].start()
    for send in sends:
        send.wait()


def group_kernel(shards, blocks, cap_big, docs_at, blk_at, small_in, *refs):
    held, tables = refs[:blocks], refs[blocks:blocks + shards]
    rows_refs, ids_refs = refs[blocks + shards + 1:-blocks], refs[-blocks:]
    kinds = 2 if blocks > 1 and shards > 1 else 1
    for shift, out in enumerate(rows_refs):
        at = pl.multiple_of(modulo(docs_at[0] + shards - shift, shards) // kinds * cap_big, cap_big)
        for step, block in enumerate(held):
            out[step * cap_big:(step + 1) * cap_big, :] = block[pl.ds(at, cap_big), :]
    for step, out in enumerate(ids_refs):
        to = modulo(blk_at[0] + step, blocks)
        out[...] = jnp.zeros(out.shape, jnp.float32)
        for shift, table in enumerate(tables):
            out[shift:shift + 1, :] = jnp.sum(
                jnp.where(iota(table.shape, 0) == to, table[...], 0.0), axis=0, keepdims=True)


def store_rows(values, ref):
    for device in range(ref.shape[0]):
        ref[device, 0:1, :] = values[device:device + 1, :]


def load_rows(ref):
    return jnp.concatenate([ref[device, 0:1, :] for device in range(ref.shape[0])], axis=0)


def small_sources(total, blocks, cap_small):
    at = iota((1, total), 1)
    source = at // cap_small
    return source // blocks, modulo(source, blocks), lax.rem(at, jnp.int32(cap_small))


def big_sources(total, docs_at, blk_at, shards, blocks, cap_big, cap_small):
    at = iota((1, total), 1)
    part, step = at // (blocks * cap_big), modulo(at // cap_big, blocks)
    return (modulo(docs_at[0] + part, shards), modulo(blk_at[0] + step, blocks),
            cap_small + lax.rem(at, jnp.int32(cap_big)))


def ids_kernel(shards, blocks, cap_big, cap_small, docs_at, blk_at, *refs):
    tables, small_ref, big_ref = refs[:blocks], refs[blocks], refs[blocks + 1]
    high = tables[0].shape[0]
    values = jnp.concatenate([table[...] for table in tables], axis=0)
    values = jnp.concatenate([values, jnp.zeros_like(values)], axis=0).astype(jnp.bfloat16)
    for ref, (docs, blk, lane) in (
        (small_ref, small_sources(small_ref.shape[1], blocks, cap_small)),
        (big_ref, big_sources(big_ref.shape[1], docs_at, blk_at, shards, blocks, cap_big, cap_small)),
    ):
        total = ref.shape[1]
        pick = (iota((LANES, total), 0) == lane).astype(jnp.float32).astype(jnp.bfloat16)
        found = jnp.dot(values, pick, preferred_element_type=jnp.float32)
        row = modulo(blk_at[0] + blocks - blk, blocks) * high + modulo(docs_at[0] + shards - docs, shards)
        ref[...] = jnp.sum(jnp.where(iota(found.shape, 0) == row, found, 0.0), axis=0, keepdims=True)


def as_column(row):
    return jnp.broadcast_to(row, (8, row.shape[1])).T[:, 0:1]


def block_best(queries, col_ids, first_row, others, row_ids, first_col):
    scores = dot_nt(queries, others)
    allowed = (col_ids == row_ids) & (row_ids > 0.0)
    if first_row is not None:
        allowed &= (iota(scores.shape, 0) + first_row) != (iota(scores.shape, 1) + first_col)
    return jnp.max(jnp.where(allowed, scores, -1.0), axis=0, keepdims=True)


def spread(best, docs, blk, lane, shards, blocks):
    total, devices = best.shape[1], shards * blocks
    mine = jnp.where(iota((devices, total), 0) == docs * blocks + blk, best, 0.0)
    place = (iota((LANES, total), 0) == lane).astype(jnp.float32).astype(jnp.bfloat16)
    found = dot_nt(thirds(mine), place)
    return found[:devices] + found[devices:2 * devices] + found[2 * devices:]


def thirds(values):
    high = values.astype(jnp.bfloat16)
    rest = values - high.astype(jnp.float32)
    middle = rest.astype(jnp.bfloat16)
    low = (rest - middle.astype(jnp.float32)).astype(jnp.bfloat16)
    return jnp.concatenate([high, middle, low], axis=0)


def big_kernel(shards, blocks, cap_big, cap_small, docs_at, blk_at, *refs):
    held, row_ref, back_ref = refs[:-2], refs[-2], refs[-1]
    size = held[0].shape[0]
    col_ids = as_column(row_ref[...])
    bests = [jnp.full((1, size), -1.0, jnp.float32) for _ in held]
    for row, queries in enumerate(held):
        for col, others in enumerate(held):
            same = 0 if row == col else None
            bests[col] = jnp.maximum(bests[col], block_best(
                queries[...], col_ids[row * size:(row + 1) * size], same,
                others[...], row_ref[:, col * size:(col + 1) * size], same))
    best = jnp.concatenate(bests, axis=1)
    back_ref[...] = spread(
        best, *big_sources(best.shape[1], docs_at, blk_at, shards, blocks, cap_big, cap_small), shards, blocks)


def small_kernel(shards, blocks, cap_small, rows_ref, row_ref, big_ref, back_hbm, lanes_ref, sem):
    total = rows_ref.shape[0]
    col_ids = as_column(row_ref[...])
    tile = tile_of(total)
    best = jnp.full((1, total), -1.0, jnp.float32)
    for at in range(0, total, tile):
        best = jnp.maximum(best, block_best(
            rows_ref[at:at + tile, :], col_ids[at:at + tile], at, rows_ref[...], row_ref[...], 0))
    back = spread(best, *small_sources(total, blocks, cap_small), shards, blocks)
    store_rows(big_ref[...] + back, lanes_ref)
    send = pltpu.make_async_copy(lanes_ref, back_hbm, sem)
    send.start()
    send.wait()


def masks_kernel(info_ref, device_ref, lane_ref):
    device = (iota((device_ref.shape[0] // 3, device_ref.shape[1]), 0) == info_ref[0:1, :]).astype(jnp.float32)
    device_ref[...] = jnp.concatenate([device] * 3, axis=0).astype(jnp.bfloat16)
    lane_ref[...] = (iota(lane_ref.shape, 0) == info_ref[1:2, :]).astype(jnp.float32)


def finish_kernel(back_ref, device_ref, lane_ref, out_ref):
    found = lax.dot_general(thirds(load_rows(back_ref)), device_ref[...], (((0,), (0,)), ((), ())),
                            preferred_element_type=jnp.float32)
    out_ref[...] = jnp.sum(jnp.where(lane_ref[...] > 0.0, found, 0.0), axis=0, keepdims=True)


def call(kernel, outs, ins, flops, moved, limit=16, scratch=(), aliases=None):
    specs = [pl.BlockSpec(memory_space=space) for _, _, space in outs]
    return pl.pallas_call(
        kernel,
        out_shape=[space(shape, dtype) if space is pltpu.HBM else jax.ShapeDtypeStruct(shape, dtype)
                   for shape, dtype, space in outs],
        in_specs=[pl.BlockSpec(memory_space=space) for space in ins],
        out_specs=specs,
        scratch_shapes=scratch,
        input_output_aliases=aliases or {},
        cost_estimate=pl.CostEstimate(flops=flops, bytes_accessed=moved, transcendentals=0),
        compiler_params=pltpu.CompilerParams(vmem_limit_bytes=limit << 20),
    )


def body(pooled, proj_weight, cluster):
    shards = lax.axis_size("docs")
    blocks = lax.axis_size("blk")
    devices = shards * blocks
    docs = pooled.shape[0]
    feature = proj_weight.shape[1]
    big_count = docs // 4
    small_count = docs - big_count
    cap_big = 2 * big_count // shards
    cap_small = 2 * small_count // devices
    small_slots = devices * cap_small
    big_slots = shards * cap_big
    big_total = blocks * big_slots
    sizes = (shards, blocks, cap_big, cap_small)
    f32, bf16, i32 = jnp.float32, jnp.bfloat16, jnp.int32
    vmem, hbm, smem, dma = pltpu.VMEM, pltpu.HBM, pltpu.SMEM, pltpu.SemaphoreType.DMA

    me = tuple(lax.axis_index(axis).astype(i32).reshape(1) for axis in ("docs", "blk"))
    kinds = 2 if blocks > 1 and shards > 1 else 1
    half = big_slots // kinds
    table = -(-blocks // 8) * 8
    rows, info, *sent = call(
        functools.partial(sort_kernel, *sizes),
        [((docs, feature), bf16, hbm), ((8, docs), i32, hbm)] + [((half, feature), bf16, hbm)] * blocks
        + [((table, LANES), f32, hbm)] * shards,
        [smem, smem, hbm, hbm, hbm],
        2 * docs * feature * (pooled.shape[1] + big_slots), 4 << 20, 60,
        [vmem(pooled.shape, bf16), vmem(proj_weight.shape, bf16), vmem((1, docs), i32),
         vmem((docs, feature), bf16), vmem((8, docs), i32), vmem((big_slots, feature), bf16),
         vmem((shards, table, LANES), f32), dma((5,)), dma((blocks,)), dma((shards,))],
    )(*me, pooled, proj_weight, cluster.reshape(1, docs))
    big_sent, tables = sent[:blocks], sent[blocks:]

    def along(x, axis, count, by):
        return lax.ppermute(x, axis, [(i, (i + by) % count) for i in range(count)])

    homes = [home_of(d, blocks) for d in range(kinds)]
    big_held = [big_sent[0]]
    for step in range(1, blocks):
        pairs = [(d * blocks + (home + step) % blocks, d * blocks + home) for d in range(shards) for home in homes]
        big_held.append(lax.ppermute(big_sent[step], ("docs", "blk"), pairs))
    tables = [tables[0]] + [along(tables[by], "docs", shards, by) for by in range(1, shards)]

    small_sent, = call(
        sort_small_kernel,
        [((small_slots, feature), bf16, hbm)],
        [vmem, vmem],
        2 * docs * feature * small_slots, 2 << 20, 16,
        [vmem((small_slots, feature), bf16), dma((3,))],
    )(rows, info)

    high = -(-shards // 8) * 8
    small_sent, *sent = call(
        functools.partial(group_kernel, shards, blocks, cap_big),
        [((small_slots, feature), bf16, hbm)] + [((blocks * cap_big, feature), bf16, vmem)] * shards
        + [((high, LANES), f32, vmem)] * blocks,
        [smem, smem, hbm] + [vmem] * (blocks + shards),
        shards * blocks * cap_big * feature, 4 << 20, aliases={2: 0},
    )(*me, small_sent, *big_held, *tables)
    grouped, tables = sent[:shards], sent[shards:]

    got_small = lax.all_to_all(
        small_sent.reshape(devices, cap_small, feature), ("docs", "blk"),
        split_axis=0, concat_axis=0, tiled=True).reshape(small_slots, feature)

    tables = [tables[0]] + [along(tables[by], "blk", blocks, by) for by in range(1, blocks)]
    parts = [grouped[0]]
    for shift in range(1, shards):
        pairs = [((d + shift) % shards * blocks + home_of(d, blocks), d * blocks + home_of(d, blocks))
                 for d in range(shards)]
        parts.append(lax.ppermute(grouped[shift], ("docs", "blk"), pairs))

    small_ids, big_ids = call(
        functools.partial(ids_kernel, *sizes),
        [((1, small_slots), f32, vmem), ((1, big_total), f32, vmem)],
        [smem, smem] + [vmem] * blocks,
        2 * high * blocks * LANES * (small_slots + big_total), 1 << 16,
    )(*me, *tables)

    back_big, = call(
        functools.partial(big_kernel, *sizes),
        [((devices, LANES), f32, vmem)], [smem, smem] + [vmem] * (shards + 1),
        2 * big_total * big_total * feature, 2 << 20,
    )(*me, *parts, big_ids)

    back, = call(
        functools.partial(small_kernel, shards, blocks, cap_small),
        [((devices, 1, LANES), f32, hbm)], [vmem, vmem, vmem],
        2 * small_slots * small_slots * feature, 2 << 20, 16,
        [vmem((devices, 1, LANES), f32), dma],
    )(got_small, small_ids, back_big)

    returned = lax.all_to_all(back, ("docs", "blk"), split_axis=0, concat_axis=0, tiled=True)
    masks = call(
        masks_kernel, [((3 * devices, docs), bf16, vmem), ((LANES, docs), f32, vmem)], [vmem],
        docs * LANES, 1 << 18,
    )(info)
    out, = call(
        finish_kernel, [((1, docs), f32, vmem)], [vmem, vmem, vmem],
        2 * docs * LANES * devices, 1 << 18,
    )(returned, *masks)
    return out.reshape(docs)


def solution(mesh):
    in_specs = (P(("slab", "docs", "blk"), None), P(), P(("slab", "docs", "blk")))
    out_specs = P(("slab", "docs", "blk"))
    return jax.shard_map(body, mesh=mesh, in_specs=in_specs, out_specs=out_specs, check_vma=False)
```

```python
import functools

import jax
import jax.numpy as jnp
from jax import lax
from jax.experimental import pallas as pl
from jax.experimental.pallas import tpu as pltpu
from jax.sharding import PartitionSpec as P

BIG_OWN = 4
LANES = 128


def modulo(x, n):
    return x & (n - 1) if n & (n - 1) == 0 else lax.rem(x, jnp.int32(n))


def quotient(x, n):
    if n & (n - 1) == 0:
        return lax.shift_right_logical(x, jnp.int32(n.bit_length() - 1))
    return lax.div(x, jnp.int32(n))


def iota(shape, axis):
    return lax.broadcasted_iota(jnp.int32, shape, axis)


def dot_nt(a, b):
    return lax.dot_general(a, b, (((1,), (1,)), ((), ())), preferred_element_type=jnp.float32)


def tile_of(rows, most=256):
    tile = most
    while rows % tile:
        tile //= 2
    return tile


def home_of(docs, blocks):
    return max(blocks // 2 - 1, 0) + (docs & min(blocks - 1, 1))


def picked_rows(rows_ref, slot, first, count):
    pick = (iota((count, rows_ref.shape[0]), 0) + first == slot).astype(jnp.float32).astype(jnp.bfloat16)
    return jnp.dot(pick, rows_ref[...], preferred_element_type=jnp.float32).astype(jnp.bfloat16)


def sort_kernel(shards, blocks, cap_big, cap_small, pooled_hbm, weight_hbm, cluster_hbm, small_hbm, rows_hbm, info_hbm,
                pooled_ref, weight_ref, cluster_ref, small_ref, rows_ref, info_ref, sems, small_sems):
    docs = rows_ref.shape[0]
    devices = shards * blocks
    limit = BIG_OWN * shards
    buckets = devices + shards

    fetches = [pltpu.make_async_copy(source, target, sems.at[n]) for n, (source, target) in enumerate(
        ((cluster_hbm, cluster_ref), (weight_hbm, weight_ref), (pooled_hbm, pooled_ref)))]
    for fetch in fetches:
        fetch.start()
    fetches[0].wait()

    cluster = cluster_ref[...]
    is_big = cluster < limit
    owner = modulo(cluster, shards)
    past = jnp.maximum(cluster - limit, 0)
    target = modulo(past, devices)
    bucket = jnp.where(is_big, devices + owner, target)

    padded = -(-buckets // 16) * 16
    hot = (iota((padded, docs), 0) == bucket).astype(jnp.float32)
    earlier = (iota((docs, docs), 0) < iota((docs, docs), 1)).astype(jnp.float32).astype(jnp.bfloat16)
    before = jnp.dot(hot.astype(jnp.bfloat16), earlier, preferred_element_type=jnp.float32)
    rank = jnp.sum(before * hot, axis=0, keepdims=True).astype(jnp.int32)

    info_ref[0:1, :] = jnp.where(is_big, owner * blocks + home_of(owner, blocks), target)
    info_ref[1:2, :] = jnp.where(is_big, cap_small + rank, rank)
    info_ref[2:3, :] = jnp.where(is_big, owner * cap_big + rank, -1)
    info_ref[3:4, :] = jnp.where(is_big, quotient(cluster, shards), quotient(past, devices)) + 1
    info_ref[4:5, :] = bucket
    info_ref[5:8, :] = jnp.zeros((3, docs), jnp.int32)
    sends = [pltpu.make_async_copy(info_ref, info_hbm, sems.at[3])]
    sends[0].start()
    small_slot = jnp.where(is_big, -1, target * cap_small + rank)

    for fetch in fetches[1:]:
        fetch.wait()
    projected = jnp.dot(pooled_ref[...], weight_ref[...], preferred_element_type=jnp.float32)
    squares = jnp.sum(projected * projected, axis=1, keepdims=True)
    rows_ref[...] = (projected / jnp.sqrt(squares + 1e-06)).astype(jnp.bfloat16)
    sends.append(pltpu.make_async_copy(rows_ref, rows_hbm, sems.at[4]))
    sends[-1].start()

    tile = small_ref.shape[0] // small_sems.shape[0]
    for part in range(small_sems.shape[0]):
        small_ref[part * tile:(part + 1) * tile, :] = picked_rows(rows_ref, small_slot, part * tile, tile)
        sends.append(pltpu.make_async_copy(
            small_ref.at[pl.ds(part * tile, tile)], small_hbm.at[pl.ds(part * tile, tile)], small_sems.at[part]))
        sends[-1].start()
    for send in sends:
        send.wait()


def sort_big_kernel(shards, blocks, cap_big, docs_at, rows_ref, info_ref, *out_refs):
    docs = rows_ref.shape[0]
    devices = shards * blocks
    quota, bucket = info_ref[3:4, :].astype(jnp.float32), info_ref[4:5, :]
    lanes = (iota((LANES, docs), 0) == info_ref[1:2, :]).astype(jnp.float32).astype(jnp.bfloat16)
    for shift, ref in enumerate(out_refs):
        to = modulo(docs_at[0] + shift, shards)
        ref[0:cap_big, :] = picked_rows(rows_ref, info_ref[2:3, :], to * cap_big, cap_big)
        table = ref.shape[0] - cap_big
        blk = iota((table, docs), 0)
        mine = (blk < blocks) & ((blk + to * blocks == bucket) | (bucket == devices + to))
        values = jnp.where(mine, quota, 0.0).astype(jnp.bfloat16)
        ref[cap_big:, 0:LANES] = dot_nt(values, lanes).astype(jnp.bfloat16)
        ref[cap_big:, LANES:] = jnp.zeros((table, ref.shape[1] - LANES), jnp.bfloat16)


def group_kernel(shards, blocks, cap_big, blk_at, *refs):
    held, group_ref, ids_refs = refs[:shards], refs[shards], refs[shards + 1:]
    tables = [ref[cap_big:, 0:LANES].astype(jnp.float32) for ref in held]
    total = shards * cap_big
    for shift, ref in enumerate(held):
        group_ref[shift * cap_big:(shift + 1) * cap_big, :] = ref[0:cap_big, :]
    spare = group_ref.shape[0] - total
    own = jnp.zeros((spare, LANES), jnp.float32)
    for shift, table in enumerate(tables):
        own = jnp.where(iota(own.shape, 0) == shift, table[0:1, :], own)
    group_ref[total:, 0:LANES] = own.astype(jnp.bfloat16)
    group_ref[total:, LANES:] = jnp.zeros((spare, group_ref.shape[1] - LANES), jnp.bfloat16)
    turn(tables, blk_at[0], blocks, ids_refs)


def turn(tables, at, count, outs):
    for step, out in enumerate(outs):
        to = modulo(at + step, count)
        out[...] = jnp.zeros(out.shape, jnp.float32)
        for place, table in enumerate(tables):
            out[place:place + 1, :] = jnp.sum(
                jnp.where(iota(table.shape, 0) == to, table, 0.0), axis=0, keepdims=True)


def turn_kernel(count, at_ref, *refs):
    held, outs = refs[:-count], refs[-count:]
    turn([ref[...] for ref in held], at_ref[0], count, outs)


def rows_up(count, to=8):
    return -(-count // to) * to


def small_sources(total, blocks, cap_small):
    at = iota((1, total), 1)
    source = at // cap_small
    return source // blocks, modulo(source, blocks), lax.rem(at, jnp.int32(cap_small))


def big_sources(total, shards, cap_big, cap_small):
    at = iota((1, total), 1)
    return (at // (shards * cap_big), modulo(at // cap_big, shards),
            cap_small + lax.rem(at, jnp.int32(cap_big)))


def ids_from(values, row, lane):
    pick = (iota((LANES, lane.shape[1]), 0) == lane).astype(jnp.float32).astype(jnp.bfloat16)
    found = jnp.dot(values, pick, preferred_element_type=jnp.float32)
    return jnp.sum(jnp.where(iota(found.shape, 0) == row, found, 0.0), axis=0, keepdims=True)


def ids_kernel(shards, blocks, cap_small, docs_at, blk_at, *refs):
    tables, ids_ref = refs[:-1], refs[-1]
    high = tables[0].shape[0]
    values = jnp.concatenate([table[...] for table in tables], axis=0)
    values = jnp.concatenate([values, jnp.zeros_like(values)], axis=0).astype(jnp.bfloat16)
    docs, blk, lane = small_sources(ids_ref.shape[1], blocks, cap_small)
    row = modulo(blk_at[0] + blocks - blk, blocks) * high + modulo(docs_at[0] + shards - docs, shards)
    ids_ref[...] = ids_from(values, row, lane)


def as_column(row):
    return jnp.broadcast_to(row, (8, row.shape[1])).T[:, 0:1]


def block_best(queries, col_ids, first_row, others, row_ids, first_col):
    scores = dot_nt(queries, others)
    allowed = (col_ids == row_ids) & (row_ids > 0.0)
    if first_row is not None:
        allowed &= (iota(scores.shape, 0) + first_row) != (iota(scores.shape, 1) + first_col)
    return jnp.max(jnp.where(allowed, scores, -1.0), axis=0, keepdims=True)


def spread(best, row, lane, rows):
    total = best.shape[1]
    mine = jnp.where(iota((rows, total), 0) == row, best, 0.0)
    place = (iota((LANES, total), 0) == lane).astype(jnp.float32).astype(jnp.bfloat16)
    found = dot_nt(thirds(mine), place)
    return found[:rows] + found[rows:2 * rows] + found[2 * rows:]


def thirds(values):
    high = values.astype(jnp.bfloat16)
    rest = values - high.astype(jnp.float32)
    middle = rest.astype(jnp.bfloat16)
    low = (rest - middle.astype(jnp.float32)).astype(jnp.bfloat16)
    return jnp.concatenate([high, middle, low], axis=0)


def big_kernel(shards, blocks, cap_big, cap_small, docs_at, *refs):
    held, back_ref = refs[:-1], refs[-1]
    size = shards * cap_big
    spare = held[0].shape[0] - size
    high = back_ref.shape[0] // blocks
    step, shift, lane = big_sources(blocks * size, shards, cap_big, cap_small)
    values = jnp.concatenate([ref[size:, 0:LANES] for ref in held], axis=0)
    row_ids = ids_from(values, step * spare + shift, lane)
    col_ids = as_column(row_ids)
    bests = [jnp.full((1, size), -1.0, jnp.float32) for _ in held]
    for row, queries in enumerate(held):
        for col, others in enumerate(held):
            same = 0 if row == col else None
            bests[col] = jnp.maximum(bests[col], block_best(
                queries[0:size, :], col_ids[row * size:(row + 1) * size], same,
                others[0:size, :], row_ids[:, col * size:(col + 1) * size], same))
    docs = modulo(docs_at[0] + shards - shift, shards)
    back_ref[...] = spread(jnp.concatenate(bests, axis=1), step * high + docs, lane, back_ref.shape[0])


def small_kernel(shards, blocks, cap_small, blk_at, rows_ref, row_ref, big_ref, *back_refs):
    total = rows_ref.shape[0]
    high = back_refs[0].shape[0]
    col_ids = as_column(row_ref[...])
    tile = tile_of(total)
    best = jnp.full((1, total), -1.0, jnp.float32)
    for at in range(0, total, tile):
        best = jnp.maximum(best, block_best(
            rows_ref[at:at + tile, :], col_ids[at:at + tile], at, rows_ref[...], row_ref[...], 0))
    docs, blk, lane = small_sources(total, blocks, cap_small)
    row = modulo(blk + blocks - blk_at[0], blocks) * high + docs
    back = big_ref[...] + spread(best, row, lane, big_ref.shape[0])
    for step, ref in enumerate(back_refs):
        ref[...] = back[step * high:(step + 1) * high, :]


def masks_kernel(shards, blocks, docs_at, blk_at, info_ref, row_ref, lane_ref):
    device = info_ref[0:1, :]
    high = row_ref.shape[0] // (3 * shards)
    row = (modulo(docs_at[0] + shards - device // blocks, shards) * high
           + modulo(blk_at[0] + blocks - modulo(device, blocks), blocks))
    mask = (iota((shards * high, row_ref.shape[1]), 0) == row).astype(jnp.float32)
    row_ref[...] = jnp.concatenate([mask] * 3, axis=0).astype(jnp.bfloat16)
    lane_ref[...] = (iota(lane_ref.shape, 0) == info_ref[1:2, :]).astype(jnp.float32)


def finish_kernel(*refs):
    held, (row_ref, lane_ref, out_ref) = refs[:-3], refs[-3:]
    values = thirds(jnp.concatenate([ref[...] for ref in held], axis=0))
    found = lax.dot_general(values, row_ref[...], (((0,), (0,)), ((), ())), preferred_element_type=jnp.float32)
    out_ref[...] = jnp.sum(jnp.where(lane_ref[...] > 0.0, found, 0.0), axis=0, keepdims=True)


def call(kernel, outs, ins, flops, moved, limit=16, scratch=()):
    specs = [pl.BlockSpec(memory_space=space) for _, _, space in outs]
    return pl.pallas_call(
        kernel,
        out_shape=[space(shape, dtype) if space is pltpu.HBM else jax.ShapeDtypeStruct(shape, dtype)
                   for shape, dtype, space in outs],
        in_specs=[pl.BlockSpec(memory_space=space) for space in ins],
        out_specs=specs,
        scratch_shapes=scratch,
        cost_estimate=pl.CostEstimate(flops=flops, bytes_accessed=moved, transcendentals=0),
        compiler_params=pltpu.CompilerParams(vmem_limit_bytes=limit << 20),
    )


def body(pooled, proj_weight, cluster):
    shards = lax.axis_size("docs")
    blocks = lax.axis_size("blk")
    devices = shards * blocks
    docs = pooled.shape[0]
    feature = proj_weight.shape[1]
    big_count = docs // 4
    small_count = docs - big_count
    cap_big = 2 * big_count // shards
    cap_small = 2 * small_count // devices
    small_slots = devices * cap_small
    big_slots = shards * cap_big
    big_total = blocks * big_slots
    sizes = (shards, blocks, cap_big, cap_small)
    f32, bf16, i32 = jnp.float32, jnp.bfloat16, jnp.int32
    vmem, hbm, smem, dma = pltpu.VMEM, pltpu.HBM, pltpu.SMEM, pltpu.SemaphoreType.DMA

    docs_at, blk_at = (lax.axis_index(axis).astype(i32).reshape(1) for axis in ("docs", "blk"))

    def along(x, axis, count, by):
        return lax.ppermute(x, axis, [(i, (i + by) % count) for i in range(count)])

    small_sent, rows, info = call(
        functools.partial(sort_kernel, *sizes),
        [((small_slots, feature), bf16, hbm), ((docs, feature), bf16, hbm), ((8, docs), i32, hbm)],
        [hbm, hbm, hbm],
        2 * docs * feature * (pooled.shape[1] + small_slots), 4 << 20, 60,
        [vmem(pooled.shape, bf16), vmem(proj_weight.shape, bf16), vmem((1, docs), i32),
         vmem((small_slots, feature), bf16), vmem((docs, feature), bf16), vmem((8, docs), i32),
         dma((5,)), dma((3,))],
    )(pooled, proj_weight, cluster.reshape(1, docs))

    got_small = lax.all_to_all(
        small_sent.reshape(devices, cap_small, feature), ("docs", "blk"),
        split_axis=0, concat_axis=0, tiled=True).reshape(small_slots, feature)

    big_sent = call(
        functools.partial(sort_big_kernel, shards, blocks, cap_big),
        [((cap_big + rows_up(blocks, 16), feature), bf16, vmem)] * shards,
        [smem, vmem, vmem],
        2 * docs * feature * big_slots, 2 << 20,
    )(docs_at, rows, info)
    held = [big_sent[0]] + [along(big_sent[by], "docs", shards, by) for by in range(1, shards)]

    group, *tables = call(
        functools.partial(group_kernel, shards, blocks, cap_big),
        [((big_slots + rows_up(shards, 16), feature), bf16, vmem)]
        + [((rows_up(shards), LANES), f32, vmem)] * blocks,
        [smem] + [vmem] * shards,
        big_slots * feature, 1 << 20,
    )(blk_at, *held)

    parts = [group]
    for step in range(1, blocks):
        pairs = [(d * blocks + (home_of(d, blocks) + step) % blocks, d * blocks + home_of(d, blocks))
                 for d in range(shards)]
        parts.append(lax.ppermute(group, ("docs", "blk"), pairs))
    tables = [tables[0]] + [along(tables[by], "blk", blocks, by) for by in range(1, blocks)]

    back_big, = call(
        functools.partial(big_kernel, *sizes),
        [((blocks * rows_up(shards), LANES), f32, vmem)], [smem] + [vmem] * blocks,
        2 * big_total * big_total * feature, 2 << 20,
    )(docs_at, *parts)

    small_ids, = call(
        functools.partial(ids_kernel, shards, blocks, cap_small),
        [((1, small_slots), f32, vmem)], [smem, smem] + [vmem] * blocks,
        2 * rows_up(shards) * blocks * LANES * small_slots, 1 << 16,
    )(docs_at, blk_at, *tables)

    back = call(
        functools.partial(small_kernel, shards, blocks, cap_small),
        [((rows_up(shards), LANES), f32, vmem)] * blocks, [smem, vmem, vmem, vmem],
        2 * small_slots * small_slots * feature, 2 << 20,
    )(blk_at, got_small, small_ids, back_big)
    back = [back[0]] + [along(back[by], "blk", blocks, by) for by in range(1, blocks)]
    back = call(
        functools.partial(turn_kernel, shards),
        [((rows_up(blocks), LANES), f32, vmem)] * shards, [smem] + [vmem] * blocks,
        shards * blocks * LANES, 1 << 16,
    )(docs_at, *back)
    back = [back[0]] + [along(back[by], "docs", shards, by) for by in range(1, shards)]

    masks = call(
        functools.partial(masks_kernel, shards, blocks),
        [((3 * shards * rows_up(blocks), docs), bf16, vmem), ((LANES, docs), f32, vmem)], [smem, smem, vmem],
        docs * LANES, 1 << 18,
    )(docs_at, blk_at, info)
    out, = call(
        finish_kernel, [((1, docs), f32, vmem)], [vmem] * (shards + 2),
        6 * docs * LANES * devices, 1 << 18,
    )(*back, *masks)
    return out.reshape(docs)


def solution(mesh):
    in_specs = (P(("slab", "docs", "blk"), None), P(), P(("slab", "docs", "blk")))
    out_specs = P(("slab", "docs", "blk"))
    return jax.shard_map(body, mesh=mesh, in_specs=in_specs, out_specs=out_specs, check_vma=False)
```

```python
import functools

import jax
import jax.numpy as jnp
from jax import lax
from jax.experimental import pallas as pl
from jax.experimental.pallas import tpu as pltpu
from jax.sharding import PartitionSpec as P

BIG_OWN = 4
LANES = 128


def modulo(x, n):
    return x & (n - 1) if n & (n - 1) == 0 else lax.rem(x, jnp.int32(n))


def quotient(x, n):
    if n & (n - 1) == 0:
        return lax.shift_right_logical(x, jnp.int32(n.bit_length() - 1))
    return lax.div(x, jnp.int32(n))


def iota(shape, axis):
    return lax.broadcasted_iota(jnp.int32, shape, axis)


def dot_nt(a, b):
    return lax.dot_general(a, b, (((1,), (1,)), ((), ())), preferred_element_type=jnp.float32)


def tile_of(rows, most=256):
    tile = most
    while rows % tile:
        tile //= 2
    return tile


def home_of(docs, blocks):
    return max(blocks // 2 - 1, 0) + (docs & min(blocks - 1, 1))


def picked_rows(rows_ref, slot, first, count):
    pick = (iota((count, rows_ref.shape[0]), 0) + first == slot).astype(jnp.float32).astype(jnp.bfloat16)
    return jnp.dot(pick, rows_ref[...], preferred_element_type=jnp.float32).astype(jnp.bfloat16)


def sort_kernel(shards, blocks, cap_big, cap_small, pooled_hbm, weight_hbm, cluster_hbm, small_hbm, rows_hbm, info_hbm,
                pooled_ref, weight_ref, cluster_ref, small_ref, rows_ref, info_ref, sems, small_sems):
    docs = rows_ref.shape[0]
    devices = shards * blocks
    limit = BIG_OWN * shards
    buckets = devices + shards

    fetches = [pltpu.make_async_copy(source, target, sems.at[n]) for n, (source, target) in enumerate(
        ((cluster_hbm, cluster_ref), (weight_hbm, weight_ref), (pooled_hbm, pooled_ref)))]
    for fetch in fetches:
        fetch.start()
    fetches[0].wait()

    cluster = cluster_ref[...]
    is_big = cluster < limit
    owner = modulo(cluster, shards)
    past = jnp.maximum(cluster - limit, 0)
    target = modulo(past, devices)
    bucket = jnp.where(is_big, devices + owner, target)

    padded = -(-buckets // 16) * 16
    hot = (iota((padded, docs), 0) == bucket).astype(jnp.float32)
    earlier = (iota((docs, docs), 0) < iota((docs, docs), 1)).astype(jnp.float32).astype(jnp.bfloat16)
    before = jnp.dot(hot.astype(jnp.bfloat16), earlier, preferred_element_type=jnp.float32)
    rank = jnp.sum(before * hot, axis=0, keepdims=True).astype(jnp.int32)

    info_ref[0:1, :] = jnp.where(is_big, owner * blocks + home_of(owner, blocks), target)
    info_ref[1:2, :] = jnp.where(is_big, cap_small + rank, rank)
    info_ref[2:3, :] = jnp.where(is_big, owner * cap_big + rank, -1)
    info_ref[3:4, :] = jnp.where(is_big, quotient(cluster, shards), quotient(past, devices)) + 1
    info_ref[4:5, :] = bucket
    info_ref[5:8, :] = jnp.zeros((3, docs), jnp.int32)
    sends = [pltpu.make_async_copy(info_ref, info_hbm, sems.at[3])]
    sends[0].start()
    small_slot = jnp.where(is_big, -1, target * cap_small + rank)

    for fetch in fetches[1:]:
        fetch.wait()
    projected = jnp.dot(pooled_ref[...], weight_ref[...], preferred_element_type=jnp.float32)
    squares = jnp.sum(projected * projected, axis=1, keepdims=True)
    rows_ref[...] = (projected / jnp.sqrt(squares + 1e-06)).astype(jnp.bfloat16)
    sends.append(pltpu.make_async_copy(rows_ref, rows_hbm, sems.at[4]))
    sends[-1].start()

    tile = small_ref.shape[0] // small_sems.shape[0]
    for part in range(small_sems.shape[0]):
        small_ref[part * tile:(part + 1) * tile, :] = picked_rows(rows_ref, small_slot, part * tile, tile)
        sends.append(pltpu.make_async_copy(
            small_ref.at[pl.ds(part * tile, tile)], small_hbm.at[pl.ds(part * tile, tile)], small_sems.at[part]))
        sends[-1].start()
    for send in sends:
        send.wait()


def sort_big_kernel(shards, blocks, cap_big, docs_at, blk_at, rows_ref, info_ref, *refs):
    big_refs, ids_refs = refs[:shards], refs[shards:]
    docs = rows_ref.shape[0]
    devices = shards * blocks
    quota, bucket = info_ref[3:4, :].astype(jnp.float32), info_ref[4:5, :]
    lanes = (iota((LANES, docs), 0) == info_ref[1:2, :]).astype(jnp.float32).astype(jnp.bfloat16)

    def table(mine):
        return dot_nt(jnp.where(mine, quota, 0.0).astype(jnp.bfloat16), lanes)

    for step, ref in enumerate(ids_refs):
        target = iota((2 * ref.shape[0], docs), 0) * blocks + modulo(blk_at[0] + step, blocks)
        ref[...] = table((target == bucket) & (target < devices))[0:ref.shape[0], :]
    for shift, ref in enumerate(big_refs):
        to = modulo(docs_at[0] + shift, shards)
        ref[0:cap_big, :] = picked_rows(rows_ref, info_ref[2:3, :], to * cap_big, cap_big)
        spare = ref.shape[0] - cap_big
        ref[cap_big:, 0:LANES] = table(
            (iota((spare, docs), 0) == 0) & (bucket == devices + to)).astype(jnp.bfloat16)
        ref[cap_big:, LANES:] = jnp.zeros((spare, ref.shape[1] - LANES), jnp.bfloat16)


def group_kernel(cap_big, *refs):
    held, group_ref = refs[:-1], refs[-1]
    total = len(held) * cap_big
    spare = group_ref.shape[0] - total
    own = jnp.zeros((spare, LANES), jnp.float32)
    for shift, ref in enumerate(held):
        group_ref[shift * cap_big:(shift + 1) * cap_big, :] = ref[0:cap_big, :]
        table = ref[cap_big:, 0:LANES].astype(jnp.float32)
        own = jnp.where(iota(own.shape, 0) == shift, table[0:1, :], own)
    group_ref[total:, 0:LANES] = own.astype(jnp.bfloat16)
    group_ref[total:, LANES:] = jnp.zeros((spare, group_ref.shape[1] - LANES), jnp.bfloat16)


def turn(tables, at, count, outs):
    for step, out in enumerate(outs):
        to = modulo(at + step, count)
        out[...] = jnp.zeros(out.shape, jnp.float32)
        for place, table in enumerate(tables):
            out[place:place + 1, :] = jnp.sum(
                jnp.where(iota(table.shape, 0) == to, table, 0.0), axis=0, keepdims=True)


def turn_kernel(count, at_ref, *refs):
    held, outs = refs[:-count], refs[-count:]
    turn([ref[...] for ref in held], at_ref[0], count, outs)


def rows_up(count, to=8):
    return -(-count // to) * to


def small_sources(total, blocks, cap_small):
    at = iota((1, total), 1)
    source = at // cap_small
    return source // blocks, modulo(source, blocks), lax.rem(at, jnp.int32(cap_small))


def big_sources(total, shards, cap_big, cap_small):
    at = iota((1, total), 1)
    return (at // (shards * cap_big), modulo(at // cap_big, shards),
            cap_small + lax.rem(at, jnp.int32(cap_big)))


def ids_from(values, row, lane):
    pick = (iota((LANES, lane.shape[1]), 0) == lane).astype(jnp.float32).astype(jnp.bfloat16)
    found = jnp.dot(values, pick, preferred_element_type=jnp.float32)
    return jnp.sum(jnp.where(iota(found.shape, 0) == row, found, 0.0), axis=0, keepdims=True)


def ids_kernel(shards, blocks, cap_small, docs_at, blk_at, *refs):
    tables, ids_ref = refs[:-1], refs[-1]
    high = tables[0].shape[0]
    values = jnp.concatenate([table[...] for table in tables], axis=0)
    values = jnp.concatenate([values, jnp.zeros_like(values)], axis=0).astype(jnp.bfloat16)
    docs, blk, lane = small_sources(ids_ref.shape[1], blocks, cap_small)
    row = modulo(docs_at[0] + shards - docs, shards) * high + modulo(blk_at[0] + blocks - blk, blocks)
    ids_ref[...] = ids_from(values, row, lane)


def as_column(row):
    return jnp.broadcast_to(row, (8, row.shape[1])).T[:, 0:1]


def block_best(queries, col_ids, first_row, others, row_ids, first_col):
    scores = dot_nt(queries, others)
    allowed = (col_ids == row_ids) & (row_ids > 0.0)
    if first_row is not None:
        allowed &= (iota(scores.shape, 0) + first_row) != (iota(scores.shape, 1) + first_col)
    return jnp.max(jnp.where(allowed, scores, -1.0), axis=0, keepdims=True)


def spread(best, row, lane, rows):
    total = best.shape[1]
    mine = jnp.where(iota((rows, total), 0) == row, best, 0.0)
    place = (iota((LANES, total), 0) == lane).astype(jnp.float32).astype(jnp.bfloat16)
    found = dot_nt(thirds(mine), place)
    return found[:rows] + found[rows:2 * rows] + found[2 * rows:]


def thirds(values):
    high = values.astype(jnp.bfloat16)
    rest = values - high.astype(jnp.float32)
    middle = rest.astype(jnp.bfloat16)
    low = (rest - middle.astype(jnp.float32)).astype(jnp.bfloat16)
    return jnp.concatenate([high, middle, low], axis=0)


def big_kernel(shards, blocks, cap_big, cap_small, docs_at, small_ref, *refs):
    held, back_refs = refs[:blocks], refs[blocks:]
    size = shards * cap_big
    spare = held[0].shape[0] - size
    high = back_refs[0].shape[0]
    step, shift, lane = big_sources(blocks * size, shards, cap_big, cap_small)
    values = jnp.concatenate([ref[size:, 0:LANES] for ref in held], axis=0)
    row_ids = ids_from(values, step * spare + shift, lane)
    col_ids = as_column(row_ids)
    bests = [jnp.full((1, size), -1.0, jnp.float32) for _ in held]
    for row, queries in enumerate(held):
        for col, others in enumerate(held):
            same = 0 if row == col else None
            bests[col] = jnp.maximum(bests[col], block_best(
                queries[0:size, :], col_ids[row * size:(row + 1) * size], same,
                others[0:size, :], row_ids[:, col * size:(col + 1) * size], same))
    docs = modulo(docs_at[0] + shards - shift, shards)
    back = small_ref[...] + spread(jnp.concatenate(bests, axis=1), step * high + docs, lane, small_ref.shape[0])
    for step, ref in enumerate(back_refs):
        ref[...] = back[step * high:(step + 1) * high, :]


def small_kernel(shards, blocks, cap_small, blk_at, rows_ref, row_ref, back_ref):
    total = rows_ref.shape[0]
    high = back_ref.shape[0] // blocks
    col_ids = as_column(row_ref[...])
    tile = tile_of(total)
    best = jnp.full((1, total), -1.0, jnp.float32)
    for at in range(0, total, tile):
        best = jnp.maximum(best, block_best(
            rows_ref[at:at + tile, :], col_ids[at:at + tile], at, rows_ref[...], row_ref[...], 0))
    docs, blk, lane = small_sources(total, blocks, cap_small)
    row = modulo(blk + blocks - blk_at[0], blocks) * high + docs
    back_ref[...] = spread(best, row, lane, back_ref.shape[0])


def masks_kernel(shards, blocks, docs_at, blk_at, info_ref, row_ref, lane_ref):
    device = info_ref[0:1, :]
    high = row_ref.shape[0] // (3 * shards)
    row = (modulo(docs_at[0] + shards - device // blocks, shards) * high
           + modulo(blk_at[0] + blocks - modulo(device, blocks), blocks))
    mask = (iota((shards * high, row_ref.shape[1]), 0) == row).astype(jnp.float32)
    row_ref[...] = jnp.concatenate([mask] * 3, axis=0).astype(jnp.bfloat16)
    lane_ref[...] = (iota(lane_ref.shape, 0) == info_ref[1:2, :]).astype(jnp.float32)


def finish_kernel(*refs):
    held, (row_ref, lane_ref, out_ref) = refs[:-3], refs[-3:]
    values = thirds(jnp.concatenate([ref[...] for ref in held], axis=0))
    found = lax.dot_general(values, row_ref[...], (((0,), (0,)), ((), ())), preferred_element_type=jnp.float32)
    out_ref[...] = jnp.sum(jnp.where(lane_ref[...] > 0.0, found, 0.0), axis=0, keepdims=True)


def call(kernel, outs, ins, flops, moved, limit=16, scratch=()):
    specs = [pl.BlockSpec(memory_space=space) for _, _, space in outs]
    return pl.pallas_call(
        kernel,
        out_shape=[space(shape, dtype) if space is pltpu.HBM else jax.ShapeDtypeStruct(shape, dtype)
                   for shape, dtype, space in outs],
        in_specs=[pl.BlockSpec(memory_space=space) for space in ins],
        out_specs=specs,
        scratch_shapes=scratch,
        cost_estimate=pl.CostEstimate(flops=flops, bytes_accessed=moved, transcendentals=0),
        compiler_params=pltpu.CompilerParams(vmem_limit_bytes=limit << 20),
    )


def body(pooled, proj_weight, cluster):
    shards = lax.axis_size("docs")
    blocks = lax.axis_size("blk")
    devices = shards * blocks
    docs = pooled.shape[0]
    feature = proj_weight.shape[1]
    big_count = docs // 4
    small_count = docs - big_count
    cap_big = 2 * big_count // shards
    cap_small = 2 * small_count // devices
    small_slots = devices * cap_small
    big_slots = shards * cap_big
    big_total = blocks * big_slots
    sizes = (shards, blocks, cap_big, cap_small)
    f32, bf16, i32 = jnp.float32, jnp.bfloat16, jnp.int32
    vmem, hbm, smem, dma = pltpu.VMEM, pltpu.HBM, pltpu.SMEM, pltpu.SemaphoreType.DMA

    docs_at, blk_at = (lax.axis_index(axis).astype(i32).reshape(1) for axis in ("docs", "blk"))

    def along(x, axis, count, by):
        return lax.ppermute(x, axis, [(i, (i + by) % count) for i in range(count)])

    small_sent, rows, info = call(
        functools.partial(sort_kernel, *sizes),
        [((small_slots, feature), bf16, hbm), ((docs, feature), bf16, hbm), ((8, docs), i32, hbm)],
        [hbm, hbm, hbm],
        2 * docs * feature * (pooled.shape[1] + small_slots), 4 << 20, 60,
        [vmem(pooled.shape, bf16), vmem(proj_weight.shape, bf16), vmem((1, docs), i32),
         vmem((small_slots, feature), bf16), vmem((docs, feature), bf16), vmem((8, docs), i32),
         dma((5,)), dma((3,))],
    )(pooled, proj_weight, cluster.reshape(1, docs))

    got_small = lax.all_to_all(
        small_sent.reshape(devices, cap_small, feature), ("docs", "blk"),
        split_axis=0, concat_axis=0, tiled=True).reshape(small_slots, feature)

    big_sent = call(
        functools.partial(sort_big_kernel, shards, blocks, cap_big),
        [((cap_big + 16, feature), bf16, vmem)] * shards + [((rows_up(shards), LANES), f32, vmem)] * blocks,
        [smem, smem, vmem, vmem],
        2 * docs * feature * big_slots, 2 << 20,
    )(docs_at, blk_at, rows, info)
    big_sent, tables = big_sent[:shards], big_sent[shards:]
    tables = [tables[0]] + [along(tables[by], "blk", blocks, by) for by in range(1, blocks)]
    held = [big_sent[0]] + [along(big_sent[by], "docs", shards, by) for by in range(1, shards)]

    group, = call(
        functools.partial(group_kernel, cap_big),
        [((big_slots + rows_up(shards, 16), feature), bf16, vmem)], [vmem] * shards,
        big_slots * feature, 1 << 20,
    )(*held)
    parts = [group]
    for step in range(1, blocks):
        pairs = [(d * blocks + (home_of(d, blocks) + step) % blocks, d * blocks + home_of(d, blocks))
                 for d in range(shards)]
        parts.append(lax.ppermute(group, ("docs", "blk"), pairs))

    def turned(tables):
        tables = call(
            functools.partial(turn_kernel, shards),
            [((rows_up(blocks), LANES), f32, vmem)] * shards, [smem] + [vmem] * blocks,
            shards * blocks * LANES, 1 << 16,
        )(docs_at, *tables)
        return [tables[0]] + [along(tables[by], "docs", shards, by) for by in range(1, shards)]

    tables = turned(tables)
    small_ids, = call(
        functools.partial(ids_kernel, shards, blocks, cap_small),
        [((1, small_slots), f32, vmem)], [smem, smem] + [vmem] * shards,
        2 * rows_up(blocks) * shards * LANES * small_slots, 1 << 16,
    )(docs_at, blk_at, *tables)

    back_small, = call(
        functools.partial(small_kernel, shards, blocks, cap_small),
        [((blocks * rows_up(shards), LANES), f32, vmem)], [smem, vmem, vmem],
        2 * small_slots * small_slots * feature, 2 << 20,
    )(blk_at, got_small, small_ids)
    back = call(
        functools.partial(big_kernel, *sizes),
        [((rows_up(shards), LANES), f32, vmem)] * blocks, [smem, vmem] + [vmem] * blocks,
        2 * big_total * big_total * feature, 2 << 20,
    )(docs_at, back_small, *parts)
    back = [back[0]] + [along(back[by], "blk", blocks, by) for by in range(1, blocks)]
    back = turned(back)

    masks = call(
        functools.partial(masks_kernel, shards, blocks),
        [((3 * shards * rows_up(blocks), docs), bf16, vmem), ((LANES, docs), f32, vmem)], [smem, smem, vmem],
        docs * LANES, 1 << 18,
    )(docs_at, blk_at, info)
    out, = call(
        finish_kernel, [((1, docs), f32, vmem)], [vmem] * (shards + 2),
        6 * docs * LANES * devices, 1 << 18,
    )(*back, *masks)
    return out.reshape(docs)


def solution(mesh):
    in_specs = (P(("slab", "docs", "blk"), None), P(), P(("slab", "docs", "blk")))
    out_specs = P(("slab", "docs", "blk"))
    return jax.shard_map(body, mesh=mesh, in_specs=in_specs, out_specs=out_specs, check_vma=False)
```

```python
import functools

import jax
import jax.numpy as jnp
from jax import lax
from jax.experimental import pallas as pl
from jax.experimental.pallas import tpu as pltpu
from jax.sharding import PartitionSpec as P

BIG_OWN = 4
LANES = 128


def modulo(x, n):
    return x & (n - 1) if n & (n - 1) == 0 else lax.rem(x, jnp.int32(n))


def quotient(x, n):
    if n & (n - 1) == 0:
        return lax.shift_right_logical(x, jnp.int32(n.bit_length() - 1))
    return lax.div(x, jnp.int32(n))


def iota(shape, axis):
    return lax.broadcasted_iota(jnp.int32, shape, axis)


def dot_nt(a, b):
    return lax.dot_general(a, b, (((1,), (1,)), ((), ())), preferred_element_type=jnp.float32)


def tile_of(rows, most=256):
    tile = most
    while rows % tile:
        tile //= 2
    return tile


def home_of(docs, blocks):
    return max(blocks // 2 - 1, 0) + (docs & min(blocks - 1, 1))


def picked_rows(rows_ref, slot, first, count):
    pick = (iota((count, rows_ref.shape[0]), 0) + first == slot).astype(jnp.float32).astype(jnp.bfloat16)
    return jnp.dot(pick, rows_ref[...], preferred_element_type=jnp.float32).astype(jnp.bfloat16)


def sort_kernel(shards, blocks, cap_big, cap_small, pooled_hbm, weight_hbm, cluster_hbm, small_hbm, rows_hbm, info_hbm,
                pooled_ref, weight_ref, cluster_ref, small_ref, rows_ref, info_ref, sems, small_sems):
    docs = rows_ref.shape[0]
    devices = shards * blocks
    limit = BIG_OWN * shards
    buckets = devices + shards

    fetches = [pltpu.make_async_copy(source, target, sems.at[n]) for n, (source, target) in enumerate(
        ((cluster_hbm, cluster_ref), (weight_hbm, weight_ref), (pooled_hbm, pooled_ref)))]
    for fetch in fetches:
        fetch.start()
    fetches[0].wait()

    cluster = cluster_ref[...]
    is_big = cluster < limit
    owner = modulo(cluster, shards)
    past = jnp.maximum(cluster - limit, 0)
    target = modulo(past, devices)
    bucket = jnp.where(is_big, devices + owner, target)

    padded = -(-buckets // 16) * 16
    hot = (iota((padded, docs), 0) == bucket).astype(jnp.float32)
    earlier = (iota((docs, docs), 0) < iota((docs, docs), 1)).astype(jnp.float32).astype(jnp.bfloat16)
    before = jnp.dot(hot.astype(jnp.bfloat16), earlier, preferred_element_type=jnp.float32)
    rank = jnp.sum(before * hot, axis=0, keepdims=True).astype(jnp.int32)

    info_ref[0:1, :] = jnp.where(is_big, owner * blocks + home_of(owner, blocks), target)
    info_ref[1:2, :] = jnp.where(is_big, cap_small + rank, rank)
    info_ref[2:3, :] = jnp.where(is_big, owner * cap_big + rank, -1)
    info_ref[3:4, :] = jnp.where(is_big, quotient(cluster, shards), quotient(past, devices)) + 1
    info_ref[4:5, :] = bucket
    info_ref[5:8, :] = jnp.zeros((3, docs), jnp.int32)
    sends = [pltpu.make_async_copy(info_ref, info_hbm, sems.at[3])]
    sends[0].start()
    small_slot = jnp.where(is_big, -1, target * cap_small + rank)

    for fetch in fetches[1:]:
        fetch.wait()
    projected = jnp.dot(pooled_ref[...], weight_ref[...], preferred_element_type=jnp.float32)
    squares = jnp.sum(projected * projected, axis=1, keepdims=True)
    rows_ref[...] = (projected / jnp.sqrt(squares + 1e-06)).astype(jnp.bfloat16)
    sends.append(pltpu.make_async_copy(rows_ref, rows_hbm, sems.at[4]))
    sends[-1].start()

    tile = small_ref.shape[0] // small_sems.shape[0]
    for part in range(small_sems.shape[0]):
        small_ref[part * tile:(part + 1) * tile, :] = picked_rows(rows_ref, small_slot, part * tile, tile)
        sends.append(pltpu.make_async_copy(
            small_ref.at[pl.ds(part * tile, tile)], small_hbm.at[pl.ds(part * tile, tile)], small_sems.at[part]))
        sends[-1].start()
    for send in sends:
        send.wait()


def sort_big_kernel(shards, blocks, cap_big, docs_at, blk_at, rows_ref, info_ref, *refs):
    big_refs, ids_refs = refs[:shards], refs[shards:]
    docs = rows_ref.shape[0]
    devices = shards * blocks
    quota, bucket = info_ref[3:4, :].astype(jnp.float32), info_ref[4:5, :]
    lanes = (iota((LANES, docs), 0) == info_ref[1:2, :]).astype(jnp.float32).astype(jnp.bfloat16)

    def table(mine):
        return dot_nt(jnp.where(mine, quota, 0.0).astype(jnp.bfloat16), lanes)

    for step, ref in enumerate(ids_refs):
        target = iota((2 * ref.shape[0], docs), 0) * blocks + modulo(blk_at[0] + step, blocks)
        ref[...] = table((target == bucket) & (target < devices))[0:ref.shape[0], :]
    for shift, ref in enumerate(big_refs):
        to = modulo(docs_at[0] + shift, shards)
        ref[0:cap_big, :] = picked_rows(rows_ref, info_ref[2:3, :], to * cap_big, cap_big)
        spare = ref.shape[0] - cap_big
        ref[cap_big:, 0:LANES] = table(
            (iota((spare, docs), 0) == 0) & (bucket == devices + to)).astype(jnp.bfloat16)
        ref[cap_big:, LANES:] = jnp.zeros((spare, ref.shape[1] - LANES), jnp.bfloat16)


def group_kernel(shards, blocks, cap_big, docs_at, *refs):
    held, tables = refs[:shards], refs[shards:shards + blocks]
    group_ref, ids_refs = refs[shards + blocks], refs[shards + blocks + 1:]
    total = shards * cap_big
    spare = group_ref.shape[0] - total
    own = jnp.zeros((spare, LANES), jnp.float32)
    for shift, ref in enumerate(held):
        group_ref[shift * cap_big:(shift + 1) * cap_big, :] = ref[0:cap_big, :]
        table = ref[cap_big:, 0:LANES].astype(jnp.float32)
        own = jnp.where(iota(own.shape, 0) == shift, table[0:1, :], own)
    group_ref[total:, 0:LANES] = own.astype(jnp.bfloat16)
    group_ref[total:, LANES:] = jnp.zeros((spare, group_ref.shape[1] - LANES), jnp.bfloat16)
    turn([table[...] for table in tables], docs_at[0], shards, ids_refs)


def turn(tables, at, count, outs):
    for step, out in enumerate(outs):
        to = modulo(at + step, count)
        out[...] = jnp.zeros(out.shape, jnp.float32)
        for place, table in enumerate(tables):
            out[place:place + 1, :] = jnp.sum(
                jnp.where(iota(table.shape, 0) == to, table, 0.0), axis=0, keepdims=True)


def turn_kernel(count, at_ref, *refs):
    held, outs = refs[:-count], refs[-count:]
    turn([ref[...] for ref in held], at_ref[0], count, outs)


def rows_up(count, to=8):
    return -(-count // to) * to


def small_sources(total, blocks, cap_small):
    at = iota((1, total), 1)
    source = at // cap_small
    return source // blocks, modulo(source, blocks), lax.rem(at, jnp.int32(cap_small))


def big_sources(total, shards, cap_big, cap_small):
    at = iota((1, total), 1)
    return (at // (shards * cap_big), modulo(at // cap_big, shards),
            cap_small + lax.rem(at, jnp.int32(cap_big)))


def ids_from(values, row, lane):
    pick = (iota((LANES, lane.shape[1]), 0) == lane).astype(jnp.float32).astype(jnp.bfloat16)
    found = jnp.dot(values, pick, preferred_element_type=jnp.float32)
    return jnp.sum(jnp.where(iota(found.shape, 0) == row, found, 0.0), axis=0, keepdims=True)


def ids_kernel(shards, blocks, cap_small, docs_at, blk_at, *refs):
    tables, ids_ref = refs[:-1], refs[-1]
    high = tables[0].shape[0]
    values = jnp.concatenate([table[...] for table in tables], axis=0)
    values = jnp.concatenate([values, jnp.zeros_like(values)], axis=0).astype(jnp.bfloat16)
    docs, blk, lane = small_sources(ids_ref.shape[1], blocks, cap_small)
    row = modulo(docs_at[0] + shards - docs, shards) * high + modulo(blk_at[0] + blocks - blk, blocks)
    ids_ref[...] = ids_from(values, row, lane)


def as_column(row):
    return jnp.broadcast_to(row, (8, row.shape[1])).T[:, 0:1]


def block_best(queries, col_ids, first_row, others, row_ids, first_col):
    scores = dot_nt(queries, others)
    allowed = (col_ids == row_ids) & (row_ids > 0.0)
    if first_row is not None:
        allowed &= (iota(scores.shape, 0) + first_row) != (iota(scores.shape, 1) + first_col)
    return jnp.max(jnp.where(allowed, scores, -1.0), axis=0, keepdims=True)


def spread(best, row, lane, rows):
    total = best.shape[1]
    mine = jnp.where(iota((rows, total), 0) == row, best, 0.0)
    place = (iota((LANES, total), 0) == lane).astype(jnp.float32).astype(jnp.bfloat16)
    found = dot_nt(thirds(mine), place)
    return found[:rows] + found[rows:2 * rows] + found[2 * rows:]


def thirds(values):
    high = values.astype(jnp.bfloat16)
    rest = values - high.astype(jnp.float32)
    middle = rest.astype(jnp.bfloat16)
    low = (rest - middle.astype(jnp.float32)).astype(jnp.bfloat16)
    return jnp.concatenate([high, middle, low], axis=0)


def big_kernel(shards, blocks, cap_big, cap_small, docs_at, small_ref, *refs):
    held, back_refs = refs[:blocks], refs[blocks:]
    size = shards * cap_big
    spare = held[0].shape[0] - size
    high = back_refs[0].shape[0]
    step, shift, lane = big_sources(blocks * size, shards, cap_big, cap_small)
    values = jnp.concatenate([ref[size:, 0:LANES] for ref in held], axis=0)
    row_ids = ids_from(values, step * spare + shift, lane)
    col_ids = as_column(row_ids)
    bests = [jnp.full((1, size), -1.0, jnp.float32) for _ in held]
    for row, queries in enumerate(held):
        for col, others in enumerate(held):
            same = 0 if row == col else None
            bests[col] = jnp.maximum(bests[col], block_best(
                queries[0:size, :], col_ids[row * size:(row + 1) * size], same,
                others[0:size, :], row_ids[:, col * size:(col + 1) * size], same))
    docs = modulo(docs_at[0] + shards - shift, shards)
    back = small_ref[...] + spread(jnp.concatenate(bests, axis=1), step * high + docs, lane, small_ref.shape[0])
    for step, ref in enumerate(back_refs):
        ref[...] = back[step * high:(step + 1) * high, :]


def small_kernel(shards, blocks, cap_small, blk_at, rows_ref, row_ref, back_ref):
    total = rows_ref.shape[0]
    high = back_ref.shape[0] // blocks
    col_ids = as_column(row_ref[...])
    tile = tile_of(total)
    best = jnp.full((1, total), -1.0, jnp.float32)
    for at in range(0, total, tile):
        best = jnp.maximum(best, block_best(
            rows_ref[at:at + tile, :], col_ids[at:at + tile], at, rows_ref[...], row_ref[...], 0))
    docs, blk, lane = small_sources(total, blocks, cap_small)
    row = modulo(blk + blocks - blk_at[0], blocks) * high + docs
    back_ref[...] = spread(best, row, lane, back_ref.shape[0])


def masks_kernel(shards, blocks, docs_at, blk_at, info_ref, row_ref, lane_ref):
    device = info_ref[0:1, :]
    high = row_ref.shape[0] // (3 * shards)
    row = (modulo(docs_at[0] + shards - device // blocks, shards) * high
           + modulo(blk_at[0] + blocks - modulo(device, blocks), blocks))
    mask = (iota((shards * high, row_ref.shape[1]), 0) == row).astype(jnp.float32)
    row_ref[...] = jnp.concatenate([mask] * 3, axis=0).astype(jnp.bfloat16)
    lane_ref[...] = (iota(lane_ref.shape, 0) == info_ref[1:2, :]).astype(jnp.float32)


def finish_kernel(*refs):
    held, (row_ref, lane_ref, out_ref) = refs[:-3], refs[-3:]
    values = thirds(jnp.concatenate([ref[...] for ref in held], axis=0))
    found = lax.dot_general(values, row_ref[...], (((0,), (0,)), ((), ())), preferred_element_type=jnp.float32)
    out_ref[...] = jnp.sum(jnp.where(lane_ref[...] > 0.0, found, 0.0), axis=0, keepdims=True)


def call(kernel, outs, ins, flops, moved, limit=16, scratch=()):
    specs = [pl.BlockSpec(memory_space=space) for _, _, space in outs]
    return pl.pallas_call(
        kernel,
        out_shape=[space(shape, dtype) if space is pltpu.HBM else jax.ShapeDtypeStruct(shape, dtype)
                   for shape, dtype, space in outs],
        in_specs=[pl.BlockSpec(memory_space=space) for space in ins],
        out_specs=specs,
        scratch_shapes=scratch,
        cost_estimate=pl.CostEstimate(flops=flops, bytes_accessed=moved, transcendentals=0),
        compiler_params=pltpu.CompilerParams(vmem_limit_bytes=limit << 20),
    )


def body(pooled, proj_weight, cluster):
    shards = lax.axis_size("docs")
    blocks = lax.axis_size("blk")
    devices = shards * blocks
    docs = pooled.shape[0]
    feature = proj_weight.shape[1]
    big_count = docs // 4
    small_count = docs - big_count
    cap_big = 2 * big_count // shards
    cap_small = 2 * small_count // devices
    small_slots = devices * cap_small
    big_slots = shards * cap_big
    big_total = blocks * big_slots
    sizes = (shards, blocks, cap_big, cap_small)
    f32, bf16, i32 = jnp.float32, jnp.bfloat16, jnp.int32
    vmem, hbm, smem, dma = pltpu.VMEM, pltpu.HBM, pltpu.SMEM, pltpu.SemaphoreType.DMA

    docs_at, blk_at = (lax.axis_index(axis).astype(i32).reshape(1) for axis in ("docs", "blk"))

    def along(x, axis, count, by):
        return lax.ppermute(x, axis, [(i, (i + by) % count) for i in range(count)])

    small_sent, rows, info = call(
        functools.partial(sort_kernel, *sizes),
        [((small_slots, feature), bf16, hbm), ((docs, feature), bf16, hbm), ((8, docs), i32, hbm)],
        [hbm, hbm, hbm],
        2 * docs * feature * (pooled.shape[1] + small_slots), 4 << 20, 60,
        [vmem(pooled.shape, bf16), vmem(proj_weight.shape, bf16), vmem((1, docs), i32),
         vmem((small_slots, feature), bf16), vmem((docs, feature), bf16), vmem((8, docs), i32),
         dma((5,)), dma((3,))],
    )(pooled, proj_weight, cluster.reshape(1, docs))

    got_small = lax.all_to_all(
        small_sent.reshape(devices, cap_small, feature), ("docs", "blk"),
        split_axis=0, concat_axis=0, tiled=True).reshape(small_slots, feature)

    big_sent = call(
        functools.partial(sort_big_kernel, shards, blocks, cap_big),
        [((cap_big + 16, feature), bf16, vmem)] * shards + [((rows_up(shards), LANES), f32, vmem)] * blocks,
        [smem, smem, vmem, vmem],
        2 * docs * feature * big_slots, 2 << 20,
    )(docs_at, blk_at, rows, info)
    big_sent, tables = big_sent[:shards], big_sent[shards:]
    tables = [tables[0]] + [along(tables[by], "blk", blocks, by) for by in range(1, blocks)]
    held = [big_sent[0]] + [along(big_sent[by], "docs", shards, by) for by in range(1, shards)]

    group, *tables = call(
        functools.partial(group_kernel, shards, blocks, cap_big),
        [((big_slots + rows_up(shards, 16), feature), bf16, vmem)] + [((rows_up(blocks), LANES), f32, vmem)] * shards,
        [smem] + [vmem] * (shards + blocks),
        big_slots * feature, 1 << 20,
    )(docs_at, *held, *tables)
    tables = [tables[0]] + [along(tables[by], "docs", shards, by) for by in range(1, shards)]
    parts = [group]
    for step in range(1, blocks):
        pairs = [(d * blocks + (home_of(d, blocks) + step) % blocks, d * blocks + home_of(d, blocks))
                 for d in range(shards)]
        parts.append(lax.ppermute(group, ("docs", "blk"), pairs))

    small_ids, = call(
        functools.partial(ids_kernel, shards, blocks, cap_small),
        [((1, small_slots), f32, vmem)], [smem, smem] + [vmem] * shards,
        2 * rows_up(blocks) * shards * LANES * small_slots, 1 << 16,
    )(docs_at, blk_at, *tables)

    back_small, = call(
        functools.partial(small_kernel, shards, blocks, cap_small),
        [((blocks * rows_up(shards), LANES), f32, vmem)], [smem, vmem, vmem],
        2 * small_slots * small_slots * feature, 2 << 20,
    )(blk_at, got_small, small_ids)
    back = call(
        functools.partial(big_kernel, *sizes),
        [((rows_up(shards), LANES), f32, vmem)] * blocks, [smem, vmem] + [vmem] * blocks,
        2 * big_total * big_total * feature, 2 << 20,
    )(docs_at, back_small, *parts)
    back = [back[0]] + [along(back[by], "blk", blocks, by) for by in range(1, blocks)]
    back = call(
        functools.partial(turn_kernel, shards),
        [((rows_up(blocks), LANES), f32, vmem)] * shards, [smem] + [vmem] * blocks,
        shards * blocks * LANES, 1 << 16,
    )(docs_at, *back)
    back = [back[0]] + [along(back[by], "docs", shards, by) for by in range(1, shards)]

    masks = call(
        functools.partial(masks_kernel, shards, blocks),
        [((3 * shards * rows_up(blocks), docs), bf16, vmem), ((LANES, docs), f32, vmem)], [smem, smem, vmem],
        docs * LANES, 1 << 18,
    )(docs_at, blk_at, info)
    out, = call(
        finish_kernel, [((1, docs), f32, vmem)], [vmem] * (shards + 2),
        6 * docs * LANES * devices, 1 << 18,
    )(*back, *masks)
    return out.reshape(docs)


def solution(mesh):
    in_specs = (P(("slab", "docs", "blk"), None), P(), P(("slab", "docs", "blk")))
    out_specs = P(("slab", "docs", "blk"))
    return jax.shard_map(body, mesh=mesh, in_specs=in_specs, out_specs=out_specs, check_vma=False)
```

```python
import functools

import jax
import jax.numpy as jnp
from jax import lax
from jax.experimental import pallas as pl
from jax.experimental.pallas import tpu as pltpu
from jax.sharding import PartitionSpec as P

BIG_OWN = 4
LANES = 128


def modulo(x, n):
    return x & (n - 1) if n & (n - 1) == 0 else lax.rem(x, jnp.int32(n))


def quotient(x, n):
    if n & (n - 1) == 0:
        return lax.shift_right_logical(x, jnp.int32(n.bit_length() - 1))
    return lax.div(x, jnp.int32(n))


def iota(shape, axis):
    return lax.broadcasted_iota(jnp.int32, shape, axis)


def dot_nt(a, b):
    return lax.dot_general(a, b, (((1,), (1,)), ((), ())), preferred_element_type=jnp.float32)


def tile_of(rows, most=256):
    tile = most
    while rows % tile:
        tile //= 2
    return tile


def home_of(docs, blocks):
    return max(blocks // 2 - 1, 0) + (docs & min(blocks - 1, 1))


def picked_rows(rows_ref, slot, first, count):
    pick = (iota((count, rows_ref.shape[0]), 0) + first == slot).astype(jnp.float32).astype(jnp.bfloat16)
    return jnp.dot(pick, rows_ref[...], preferred_element_type=jnp.float32).astype(jnp.bfloat16)


def sort_kernel(shards, blocks, cap_big, cap_small, pooled_hbm, weight_hbm, cluster_hbm, small_hbm, rows_hbm, info_hbm,
                pooled_ref, weight_ref, cluster_ref, small_ref, rows_ref, info_ref, sems, small_sems):
    docs, feature = rows_ref.shape
    devices = shards * blocks
    limit = BIG_OWN * shards
    buckets = devices + shards

    fetches = [pltpu.make_async_copy(source, target, sems.at[n]) for n, (source, target) in enumerate(
        ((cluster_hbm, cluster_ref), (weight_hbm, weight_ref), (pooled_hbm, pooled_ref)))]
    for fetch in fetches:
        fetch.start()
    fetches[0].wait()

    cluster = cluster_ref[...]
    is_big = cluster < limit
    owner = modulo(cluster, shards)
    past = jnp.maximum(cluster - limit, 0)
    target = modulo(past, devices)
    bucket = jnp.where(is_big, devices + owner, target)

    padded = -(-buckets // 16) * 16
    hot = (iota((padded, docs), 0) == bucket).astype(jnp.float32)
    earlier = (iota((docs, docs), 0) < iota((docs, docs), 1)).astype(jnp.float32).astype(jnp.bfloat16)
    before = jnp.dot(hot.astype(jnp.bfloat16), earlier, preferred_element_type=jnp.float32)
    rank = jnp.sum(before * hot, axis=0, keepdims=True).astype(jnp.int32)

    info_ref[0:1, :] = jnp.where(is_big, owner * blocks + home_of(owner, blocks), target)
    info_ref[1:2, :] = jnp.where(is_big, cap_small + rank, rank)
    info_ref[2:3, :] = jnp.where(is_big, owner * cap_big + rank, -1)
    info_ref[3:4, :] = jnp.where(is_big, quotient(cluster, shards), quotient(past, devices)) + 1
    info_ref[4:5, :] = bucket
    info_ref[5:8, :] = jnp.zeros((3, docs), jnp.int32)
    sends = [pltpu.make_async_copy(info_ref, info_hbm, sems.at[3])]
    sends[0].start()
    small_slot = jnp.where(is_big, -1, target * cap_small + rank)
    ids = ids_table(iota((devices, docs), 0) == bucket, info_ref)

    for fetch in fetches[1:]:
        fetch.wait()
    projected = jnp.dot(pooled_ref[...], weight_ref[...], preferred_element_type=jnp.float32)
    squares = jnp.sum(projected * projected, axis=1, keepdims=True)
    rows_ref[...] = (projected / jnp.sqrt(squares + 1e-06)).astype(jnp.bfloat16)
    sends.append(pltpu.make_async_copy(rows_ref, rows_hbm, sems.at[4]))
    sends[-1].start()

    slabs = feature // LANES
    group = devices // small_sems.shape[0]
    for part in range(small_sems.shape[0]):
        first = part * group
        picked = picked_rows(rows_ref, small_slot, first * cap_small, group * cap_small)
        for device in range(group):
            for slab in range(slabs):
                small_ref[first + device, slab * cap_small:(slab + 1) * cap_small, :] = picked[
                    device * cap_small:(device + 1) * cap_small, slab * LANES:(slab + 1) * LANES]
            small_ref[first + device, slabs * cap_small:, :] = jnp.broadcast_to(
                ids[first + device:first + device + 1, :], (16, LANES)).astype(jnp.bfloat16)
        sends.append(pltpu.make_async_copy(
            small_ref.at[pl.ds(first, group)], small_hbm.at[pl.ds(first, group)], small_sems.at[part]))
        sends[-1].start()
    for send in sends:
        send.wait()


def ids_table(mine, info_ref):
    docs = info_ref.shape[1]
    quota = info_ref[3:4, :].astype(jnp.float32)
    lanes = (iota((LANES, docs), 0) == info_ref[1:2, :]).astype(jnp.float32).astype(jnp.bfloat16)
    return dot_nt(jnp.where(mine, quota, 0.0).astype(jnp.bfloat16), lanes)


def sort_big_kernel(shards, blocks, cap_big, docs_at, rows_ref, info_ref, *big_refs):
    devices = shards * blocks
    for shift, ref in enumerate(big_refs):
        to = modulo(docs_at[0] + shift, shards)
        ref[0:cap_big, :] = picked_rows(rows_ref, info_ref[2:3, :], to * cap_big, cap_big)
        spare = ref.shape[0] - cap_big
        mine = (iota((spare, info_ref.shape[1]), 0) == 0) & (info_ref[4:5, :] == devices + to)
        ref[cap_big:, 0:LANES] = ids_table(mine, info_ref).astype(jnp.bfloat16)
        ref[cap_big:, LANES:] = jnp.zeros((spare, ref.shape[1] - LANES), jnp.bfloat16)


def group_kernel(cap_big, *refs):
    held, group_ref = refs[:-1], refs[-1]
    total = len(held) * cap_big
    spare = group_ref.shape[0] - total
    own = jnp.zeros((spare, LANES), jnp.float32)
    for shift, ref in enumerate(held):
        group_ref[shift * cap_big:(shift + 1) * cap_big, :] = ref[0:cap_big, :]
        table = ref[cap_big:, 0:LANES].astype(jnp.float32)
        own = jnp.where(iota(own.shape, 0) == shift, table[0:1, :], own)
    group_ref[total:, 0:LANES] = own.astype(jnp.bfloat16)
    group_ref[total:, LANES:] = jnp.zeros((spare, group_ref.shape[1] - LANES), jnp.bfloat16)


def turn(tables, at, count, outs):
    for step, out in enumerate(outs):
        to = modulo(at + step, count)
        out[...] = jnp.zeros(out.shape, jnp.float32)
        for place, table in enumerate(tables):
            out[place:place + 1, :] = jnp.sum(
                jnp.where(iota(table.shape, 0) == to, table, 0.0), axis=0, keepdims=True)


def turn_kernel(count, at_ref, *refs):
    held, outs = refs[:-count], refs[-count:]
    turn([ref[...] for ref in held], at_ref[0], count, outs)


def rows_up(count, to=8):
    return -(-count // to) * to


def small_sources(total, blocks, cap_small):
    at = iota((1, total), 1)
    source = at // cap_small
    return source // blocks, modulo(source, blocks), lax.rem(at, jnp.int32(cap_small))


def big_sources(total, shards, cap_big, cap_small):
    at = iota((1, total), 1)
    return (at // (shards * cap_big), modulo(at // cap_big, shards),
            cap_small + lax.rem(at, jnp.int32(cap_big)))


def ids_from(values, row, lane):
    pick = (iota((LANES, lane.shape[1]), 0) == lane).astype(jnp.float32).astype(jnp.bfloat16)
    found = jnp.dot(values, pick, preferred_element_type=jnp.float32)
    return jnp.sum(jnp.where(iota(found.shape, 0) == row, found, 0.0), axis=0, keepdims=True)


def as_column(row):
    return jnp.broadcast_to(row, (8, row.shape[1])).T[:, 0:1]


def block_best(queries, col_ids, first_row, others, row_ids, first_col):
    scores = dot_nt(queries, others)
    allowed = (col_ids == row_ids) & (row_ids > 0.0)
    if first_row is not None:
        allowed &= (iota(scores.shape, 0) + first_row) != (iota(scores.shape, 1) + first_col)
    return jnp.max(jnp.where(allowed, scores, -1.0), axis=0, keepdims=True)


def spread(best, row, lane, rows):
    total = best.shape[1]
    mine = jnp.where(iota((rows, total), 0) == row, best, 0.0)
    place = (iota((LANES, total), 0) == lane).astype(jnp.float32).astype(jnp.bfloat16)
    found = dot_nt(thirds(mine), place)
    return found[:rows] + found[rows:2 * rows] + found[2 * rows:]


def thirds(values):
    high = values.astype(jnp.bfloat16)
    rest = values - high.astype(jnp.float32)
    middle = rest.astype(jnp.bfloat16)
    low = (rest - middle.astype(jnp.float32)).astype(jnp.bfloat16)
    return jnp.concatenate([high, middle, low], axis=0)


def big_kernel(shards, blocks, cap_big, cap_small, docs_at, small_ref, *refs):
    held, back_refs = refs[:blocks], refs[blocks:]
    size = shards * cap_big
    spare = held[0].shape[0] - size
    high = back_refs[0].shape[0]
    step, shift, lane = big_sources(blocks * size, shards, cap_big, cap_small)
    values = jnp.concatenate([ref[size:, 0:LANES] for ref in held], axis=0)
    row_ids = ids_from(values, step * spare + shift, lane)
    col_ids = as_column(row_ids)
    bests = [jnp.full((1, size), -1.0, jnp.float32) for _ in held]
    for row, queries in enumerate(held):
        for col, others in enumerate(held):
            same = 0 if row == col else None
            bests[col] = jnp.maximum(bests[col], block_best(
                queries[0:size, :], col_ids[row * size:(row + 1) * size], same,
                others[0:size, :], row_ids[:, col * size:(col + 1) * size], same))
    docs = modulo(docs_at[0] + shards - shift, shards)
    back = small_ref[...] + spread(jnp.concatenate(bests, axis=1), step * high + docs, lane, small_ref.shape[0])
    for step, ref in enumerate(back_refs):
        ref[...] = back[step * high:(step + 1) * high, :]


def small_kernel(shards, blocks, cap_small, blk_at, got_ref, back_ref, rows_ref):
    total, feature = rows_ref.shape
    high = back_ref.shape[0] // blocks
    slabs = feature // LANES
    values = []
    for device in range(got_ref.shape[0]):
        for slab in range(slabs):
            rows_ref[device * cap_small:(device + 1) * cap_small, slab * LANES:(slab + 1) * LANES] = got_ref[
                device, slab * cap_small:(slab + 1) * cap_small, :]
        values.append(got_ref[device, slabs * cap_small:, :].astype(jnp.float32)[0:1, :])
    docs, blk, lane = small_sources(total, blocks, cap_small)
    row_ids = ids_from(jnp.concatenate(values, axis=0).astype(jnp.bfloat16), docs * blocks + blk, lane)
    col_ids = as_column(row_ids)
    tile = tile_of(total)
    best = jnp.full((1, total), -1.0, jnp.float32)
    for at in range(0, total, tile):
        best = jnp.maximum(best, block_best(
            rows_ref[at:at + tile, :], col_ids[at:at + tile], at, rows_ref[...], row_ids, 0))
    row = modulo(blk + blocks - blk_at[0], blocks) * high + docs
    back_ref[...] = spread(best, row, lane, back_ref.shape[0])


def masks_kernel(shards, blocks, docs_at, blk_at, info_ref, row_ref, lane_ref):
    device = info_ref[0:1, :]
    high = row_ref.shape[0] // (3 * shards)
    row = (modulo(docs_at[0] + shards - device // blocks, shards) * high
           + modulo(blk_at[0] + blocks - modulo(device, blocks), blocks))
    mask = (iota((shards * high, row_ref.shape[1]), 0) == row).astype(jnp.float32)
    row_ref[...] = jnp.concatenate([mask] * 3, axis=0).astype(jnp.bfloat16)
    lane_ref[...] = (iota(lane_ref.shape, 0) == info_ref[1:2, :]).astype(jnp.float32)


def finish_kernel(*refs):
    held, (row_ref, lane_ref, out_ref) = refs[:-3], refs[-3:]
    values = thirds(jnp.concatenate([ref[...] for ref in held], axis=0))
    found = lax.dot_general(values, row_ref[...], (((0,), (0,)), ((), ())), preferred_element_type=jnp.float32)
    out_ref[...] = jnp.sum(jnp.where(lane_ref[...] > 0.0, found, 0.0), axis=0, keepdims=True)


def call(kernel, outs, ins, flops, moved, limit=16, scratch=()):
    specs = [pl.BlockSpec(memory_space=space) for _, _, space in outs]
    return pl.pallas_call(
        kernel,
        out_shape=[space(shape, dtype) if space is pltpu.HBM else jax.ShapeDtypeStruct(shape, dtype)
                   for shape, dtype, space in outs],
        in_specs=[pl.BlockSpec(memory_space=space) for space in ins],
        out_specs=specs,
        scratch_shapes=scratch,
        cost_estimate=pl.CostEstimate(flops=flops, bytes_accessed=moved, transcendentals=0),
        compiler_params=pltpu.CompilerParams(vmem_limit_bytes=limit << 20),
    )


def body(pooled, proj_weight, cluster):
    shards = lax.axis_size("docs")
    blocks = lax.axis_size("blk")
    devices = shards * blocks
    docs = pooled.shape[0]
    feature = proj_weight.shape[1]
    big_count = docs // 4
    small_count = docs - big_count
    cap_big = 2 * big_count // shards
    cap_small = rows_up(2 * small_count // devices, 16)
    small_slots = devices * cap_small
    big_slots = shards * cap_big
    big_total = blocks * big_slots
    sizes = (shards, blocks, cap_big, cap_small)
    f32, bf16, i32 = jnp.float32, jnp.bfloat16, jnp.int32
    vmem, hbm, smem, dma = pltpu.VMEM, pltpu.HBM, pltpu.SMEM, pltpu.SemaphoreType.DMA

    docs_at, blk_at = (lax.axis_index(axis).astype(i32).reshape(1) for axis in ("docs", "blk"))

    def along(x, axis, count, by):
        return lax.ppermute(x, axis, [(i, (i + by) % count) for i in range(count)])

    small_rows = feature // LANES * cap_small + 16
    small_sent, rows, info = call(
        functools.partial(sort_kernel, *sizes),
        [((devices, small_rows, LANES), bf16, hbm), ((docs, feature), bf16, hbm), ((8, docs), i32, hbm)],
        [hbm, hbm, hbm],
        2 * docs * feature * (pooled.shape[1] + small_slots), 4 << 20, 60,
        [vmem(pooled.shape, bf16), vmem(proj_weight.shape, bf16), vmem((1, docs), i32),
         vmem((devices, small_rows, LANES), bf16), vmem((docs, feature), bf16), vmem((8, docs), i32),
         dma((5,)), dma((4,))],
    )(pooled, proj_weight, cluster.reshape(1, docs))

    got_small = lax.all_to_all(small_sent, ("docs", "blk"), split_axis=0, concat_axis=0, tiled=True)

    big_sent = call(
        functools.partial(sort_big_kernel, shards, blocks, cap_big),
        [((cap_big + 16, feature), bf16, vmem)] * shards,
        [smem, vmem, vmem],
        2 * docs * feature * big_slots, 2 << 20,
    )(docs_at, rows, info)
    held = [big_sent[0]] + [along(big_sent[by], "docs", shards, by) for by in range(1, shards)]
    group, = call(
        functools.partial(group_kernel, cap_big),
        [((big_slots + rows_up(shards, 16), feature), bf16, vmem)], [vmem] * shards,
        big_slots * feature, 1 << 20,
    )(*held)
    parts = [group]
    for step in range(1, blocks):
        pairs = [(d * blocks + (home_of(d, blocks) + step) % blocks, d * blocks + home_of(d, blocks))
                 for d in range(shards)]
        parts.append(lax.ppermute(group, ("docs", "blk"), pairs))

    back_small, = call(
        functools.partial(small_kernel, shards, blocks, cap_small),
        [((blocks * rows_up(shards), LANES), f32, vmem)], [smem, vmem],
        2 * small_slots * small_slots * feature, 2 << 20, 16,
        [vmem((small_slots, feature), bf16)],
    )(blk_at, got_small)
    back = call(
        functools.partial(big_kernel, *sizes),
        [((rows_up(shards), LANES), f32, vmem)] * blocks, [smem, vmem] + [vmem] * blocks,
        2 * big_total * big_total * feature, 2 << 20,
    )(docs_at, back_small, *parts)
    back = [back[0]] + [along(back[by], "blk", blocks, by) for by in range(1, blocks)]
    back = call(
        functools.partial(turn_kernel, shards),
        [((rows_up(blocks), LANES), f32, vmem)] * shards, [smem] + [vmem] * blocks,
        shards * blocks * LANES, 1 << 16,
    )(docs_at, *back)
    back = [back[0]] + [along(back[by], "docs", shards, by) for by in range(1, shards)]

    masks = call(
        functools.partial(masks_kernel, shards, blocks),
        [((3 * shards * rows_up(blocks), docs), bf16, vmem), ((LANES, docs), f32, vmem)], [smem, smem, vmem],
        docs * LANES, 1 << 18,
    )(docs_at, blk_at, info)
    out, = call(
        finish_kernel, [((1, docs), f32, vmem)], [vmem] * (shards + 2),
        6 * docs * LANES * devices, 1 << 18,
    )(*back, *masks)
    return out.reshape(docs)


def solution(mesh):
    in_specs = (P(("slab", "docs", "blk"), None), P(), P(("slab", "docs", "blk")))
    out_specs = P(("slab", "docs", "blk"))
    return jax.shard_map(body, mesh=mesh, in_specs=in_specs, out_specs=out_specs, check_vma=False)
```

```python
import functools

import jax
import jax.numpy as jnp
from jax import lax
from jax.experimental import pallas as pl
from jax.experimental.pallas import tpu as pltpu
from jax.sharding import PartitionSpec as P

BIG_OWN = 4
LANES = 128


def modulo(x, n):
    return x & (n - 1) if n & (n - 1) == 0 else lax.rem(x, jnp.int32(n))


def quotient(x, n):
    if n & (n - 1) == 0:
        return lax.shift_right_logical(x, jnp.int32(n.bit_length() - 1))
    return lax.div(x, jnp.int32(n))


def iota(shape, axis):
    return lax.broadcasted_iota(jnp.int32, shape, axis)


def dot_nt(a, b):
    return lax.dot_general(a, b, (((1,), (1,)), ((), ())), preferred_element_type=jnp.float32)


def tile_of(rows, most=256):
    tile = most
    while rows % tile:
        tile //= 2
    return tile


def home_of(docs, blocks):
    return max(blocks // 2 - 1, 0) + (docs & min(blocks - 1, 1))


def picked_rows(rows_ref, slot, first, count):
    pick = (iota((count, rows_ref.shape[0]), 0) + first == slot).astype(jnp.float32).astype(jnp.bfloat16)
    return jnp.dot(pick, rows_ref[...], preferred_element_type=jnp.float32).astype(jnp.bfloat16)


def kinds_of(shards, blocks):
    return 2 if blocks > 1 and shards > 1 else 1


def sort_kernel(shards, blocks, cap_big, cap_small, blk_at, pooled_hbm, weight_hbm, cluster_hbm, small_hbm, info_hbm,
                *refs):
    big_hbm = refs[:blocks]
    pooled_ref, weight_ref, cluster_ref, small_ref, big_ref, rows_ref, info_ref, sems, small_sems, big_sems = refs[blocks:]
    docs, feature = rows_ref.shape
    devices = shards * blocks
    limit = BIG_OWN * shards
    buckets = devices + shards

    fetches = [pltpu.make_async_copy(source, target, sems.at[n]) for n, (source, target) in enumerate(
        ((cluster_hbm, cluster_ref), (weight_hbm, weight_ref), (pooled_hbm, pooled_ref)))]
    for fetch in fetches:
        fetch.start()
    fetches[0].wait()

    cluster = cluster_ref[...]
    is_big = cluster < limit
    owner = modulo(cluster, shards)
    past = jnp.maximum(cluster - limit, 0)
    target = modulo(past, devices)
    bucket = jnp.where(is_big, devices + owner, target)

    padded = -(-buckets // 16) * 16
    hot = (iota((padded, docs), 0) == bucket).astype(jnp.float32)
    earlier = (iota((docs, docs), 0) < iota((docs, docs), 1)).astype(jnp.float32).astype(jnp.bfloat16)
    before = jnp.dot(hot.astype(jnp.bfloat16), earlier, preferred_element_type=jnp.float32)
    rank = jnp.sum(before * hot, axis=0, keepdims=True).astype(jnp.int32)

    info_ref[0:1, :] = jnp.where(is_big, owner * blocks + home_of(owner, blocks), target)
    info_ref[1:2, :] = jnp.where(is_big, cap_small + rank, rank)
    info_ref[2:3, :] = jnp.where(is_big, quotient(cluster, shards), quotient(past, devices)) + 1
    info_ref[3:8, :] = jnp.zeros((5, docs), jnp.int32)
    sends = [pltpu.make_async_copy(info_ref, info_hbm, sems.at[3])]
    sends[0].start()
    small_slot = jnp.where(is_big, -1, target * cap_small + rank)
    ids = ids_table(iota((devices, docs), 0) == bucket, info_ref)
    kinds = kinds_of(shards, blocks)
    half = shards // kinds * cap_big
    big_slot = jnp.where(is_big, modulo(owner, kinds) * half + quotient(owner, kinds) * cap_big + rank, -1)
    for kind in range(kinds):
        index = iota((big_ref.shape[1] - half, docs), 0)
        mine = (index < shards // kinds) & (index * kinds + (devices + kind) == bucket)
        big_ref[kind, half:, 0:LANES] = ids_table(mine, info_ref).astype(jnp.bfloat16)
        big_ref[kind, half:, LANES:] = jnp.zeros((index.shape[0], feature - LANES), jnp.bfloat16)

    for fetch in fetches[1:]:
        fetch.wait()
    projected = jnp.dot(pooled_ref[...], weight_ref[...], preferred_element_type=jnp.float32)
    squares = jnp.sum(projected * projected, axis=1, keepdims=True)
    rows_ref[...] = (projected / jnp.sqrt(squares + 1e-06)).astype(jnp.bfloat16)
    for kind in range(kinds):
        big_ref[kind, 0:half, :] = picked_rows(rows_ref, big_slot, kind * half, half)
    for step, out in enumerate(big_hbm):
        kind = kind_of(blk_at[0] + blocks - step, blocks, kinds)
        sends.append(pltpu.make_async_copy(big_ref.at[kind], out, big_sems.at[step]))
        sends[-1].start()

    slabs = feature // LANES
    group = devices // small_sems.shape[0]
    for part in range(small_sems.shape[0]):
        first = part * group
        picked = picked_rows(rows_ref, small_slot, first * cap_small, group * cap_small)
        for device in range(group):
            for slab in range(slabs):
                small_ref[first + device, slab * cap_small:(slab + 1) * cap_small, :] = picked[
                    device * cap_small:(device + 1) * cap_small, slab * LANES:(slab + 1) * LANES]
            small_ref[first + device, slabs * cap_small:, :] = jnp.broadcast_to(
                ids[first + device:first + device + 1, :], (16, LANES)).astype(jnp.bfloat16)
        sends.append(pltpu.make_async_copy(
            small_ref.at[pl.ds(first, group)], small_hbm.at[pl.ds(first, group)], small_sems.at[part]))
        sends[-1].start()
    for send in sends:
        send.wait()


def ids_table(mine, info_ref):
    docs = info_ref.shape[1]
    quota = info_ref[2:3, :].astype(jnp.float32)
    lanes = (iota((LANES, docs), 0) == info_ref[1:2, :]).astype(jnp.float32).astype(jnp.bfloat16)
    return dot_nt(jnp.where(mine, quota, 0.0).astype(jnp.bfloat16), lanes)


def kind_of(blk, blocks, kinds):
    return jnp.where(modulo(blk, blocks) == home_of(1, blocks), kinds - 1, 0)


def group_kernel(shards, blocks, cap_big, docs_at, small_in, *refs):
    held, outs = refs[:blocks], refs[blocks + 1:]
    kinds = kinds_of(shards, blocks)
    half = shards // kinds * cap_big
    total = blocks * cap_big
    tables = [block[half:, 0:LANES].astype(jnp.float32) for block in held]
    for shift, out in enumerate(outs):
        place = quotient(modulo(docs_at[0] + shards - shift, shards), kinds)
        at = pl.multiple_of(place * cap_big, cap_big)
        spare = out.shape[0] - total
        own = jnp.zeros((spare, LANES), jnp.float32)
        for step, block in enumerate(held):
            out[step * cap_big:(step + 1) * cap_big, :] = block[pl.ds(at, cap_big), :]
            ids = jnp.sum(jnp.where(iota(tables[step].shape, 0) == place, tables[step], 0.0), axis=0, keepdims=True)
            own = jnp.where(iota(own.shape, 0) == step, ids, own)
        out[total:, 0:LANES] = own.astype(jnp.bfloat16)
        out[total:, LANES:] = jnp.zeros((spare, out.shape[1] - LANES), jnp.bfloat16)


def turn(tables, at, count, outs):
    for step, out in enumerate(outs):
        to = modulo(at + step, count)
        out[...] = jnp.zeros(out.shape, jnp.float32)
        for place, table in enumerate(tables):
            out[place:place + 1, :] = jnp.sum(
                jnp.where(iota(table.shape, 0) == to, table, 0.0), axis=0, keepdims=True)


def turn_kernel(count, at_ref, *refs):
    held, outs = refs[:-count], refs[-count:]
    turn([ref[...] for ref in held], at_ref[0], count, outs)


def rows_up(count, to=8):
    return -(-count // to) * to


def small_sources(total, blocks, cap_small):
    at = iota((1, total), 1)
    source = at // cap_small
    return source // blocks, modulo(source, blocks), lax.rem(at, jnp.int32(cap_small))


def big_sources(total, blocks, cap_big, cap_small):
    at = iota((1, total), 1)
    return (at // (blocks * cap_big), modulo(at // cap_big, blocks),
            cap_small + lax.rem(at, jnp.int32(cap_big)))


def ids_from(values, row, lane):
    pick = (iota((LANES, lane.shape[1]), 0) == lane).astype(jnp.float32).astype(jnp.bfloat16)
    found = jnp.dot(values, pick, preferred_element_type=jnp.float32)
    return jnp.sum(jnp.where(iota(found.shape, 0) == row, found, 0.0), axis=0, keepdims=True)


def as_column(row):
    return jnp.broadcast_to(row, (8, row.shape[1])).T[:, 0:1]


def block_best(queries, col_ids, first_row, others, row_ids, first_col):
    scores = dot_nt(queries, others)
    allowed = (col_ids == row_ids) & (row_ids > 0.0)
    if first_row is not None:
        allowed &= (iota(scores.shape, 0) + first_row) != (iota(scores.shape, 1) + first_col)
    return jnp.max(jnp.where(allowed, scores, -1.0), axis=0, keepdims=True)


def spread(best, row, lane, rows):
    total = best.shape[1]
    mine = jnp.where(iota((rows, total), 0) == row, best, 0.0)
    place = (iota((LANES, total), 0) == lane).astype(jnp.float32).astype(jnp.bfloat16)
    found = dot_nt(thirds(mine), place)
    return found[:rows] + found[rows:2 * rows] + found[2 * rows:]


def thirds(values):
    high = values.astype(jnp.bfloat16)
    rest = values - high.astype(jnp.float32)
    middle = rest.astype(jnp.bfloat16)
    low = (rest - middle.astype(jnp.float32)).astype(jnp.bfloat16)
    return jnp.concatenate([high, middle, low], axis=0)


def big_kernel(shards, blocks, cap_big, cap_small, docs_at, *refs):
    held, back_ref = refs[:-1], refs[-1]
    size = blocks * cap_big
    spare = held[0].shape[0] - size
    high = back_ref.shape[0] // blocks
    shift, step, lane = big_sources(shards * size, blocks, cap_big, cap_small)
    values = jnp.concatenate([ref[size:, 0:LANES] for ref in held], axis=0)
    row_ids = ids_from(values, shift * spare + step, lane)
    col_ids = as_column(row_ids)
    bests = [jnp.full((1, size), -1.0, jnp.float32) for _ in held]
    for row, queries in enumerate(held):
        for col, others in enumerate(held):
            same = 0 if row == col else None
            bests[col] = jnp.maximum(bests[col], block_best(
                queries[0:size, :], col_ids[row * size:(row + 1) * size], same,
                others[0:size, :], row_ids[:, col * size:(col + 1) * size], same))
    row = step * high + modulo(docs_at[0] + shift, shards)
    back_ref[...] = spread(jnp.concatenate(bests, axis=1), row, lane, back_ref.shape[0])


def small_kernel(shards, blocks, cap_small, blk_at, got_ref, big_ref, *refs):
    back_refs, rows_ref = refs[:-1], refs[-1]
    total, feature = rows_ref.shape
    high = back_refs[0].shape[0]
    slabs = feature // LANES
    values = []
    for device in range(got_ref.shape[0]):
        for slab in range(slabs):
            rows_ref[device * cap_small:(device + 1) * cap_small, slab * LANES:(slab + 1) * LANES] = got_ref[
                device, slab * cap_small:(slab + 1) * cap_small, :]
        values.append(got_ref[device, slabs * cap_small:, :].astype(jnp.float32)[0:1, :])
    docs, blk, lane = small_sources(total, blocks, cap_small)
    row_ids = ids_from(jnp.concatenate(values, axis=0).astype(jnp.bfloat16), docs * blocks + blk, lane)
    col_ids = as_column(row_ids)
    tile = tile_of(total)
    best = jnp.full((1, total), -1.0, jnp.float32)
    for at in range(0, total, tile):
        best = jnp.maximum(best, block_best(
            rows_ref[at:at + tile, :], col_ids[at:at + tile], at, rows_ref[...], row_ids, 0))
    row = modulo(blk + blocks - blk_at[0], blocks) * high + docs
    back = big_ref[...] + spread(best, row, lane, big_ref.shape[0])
    for step, ref in enumerate(back_refs):
        ref[...] = back[step * high:(step + 1) * high, :]


def masks_kernel(shards, blocks, docs_at, blk_at, info_ref, row_ref, lane_ref):
    device = info_ref[0:1, :]
    high = row_ref.shape[0] // (3 * shards)
    row = (modulo(docs_at[0] + shards - device // blocks, shards) * high
           + modulo(blk_at[0] + blocks - modulo(device, blocks), blocks))
    mask = (iota((shards * high, row_ref.shape[1]), 0) == row).astype(jnp.float32)
    row_ref[...] = jnp.concatenate([mask] * 3, axis=0).astype(jnp.bfloat16)
    lane_ref[...] = (iota(lane_ref.shape, 0) == info_ref[1:2, :]).astype(jnp.float32)


def finish_kernel(*refs):
    held, (row_ref, lane_ref, out_ref) = refs[:-3], refs[-3:]
    values = thirds(jnp.concatenate([ref[...] for ref in held], axis=0))
    found = lax.dot_general(values, row_ref[...], (((0,), (0,)), ((), ())), preferred_element_type=jnp.float32)
    out_ref[...] = jnp.sum(jnp.where(lane_ref[...] > 0.0, found, 0.0), axis=0, keepdims=True)


def call(kernel, outs, ins, flops, moved, limit=16, scratch=(), aliases=None):
    specs = [pl.BlockSpec(memory_space=space) for _, _, space in outs]
    return pl.pallas_call(
        kernel,
        out_shape=[space(shape, dtype) if space is pltpu.HBM else jax.ShapeDtypeStruct(shape, dtype)
                   for shape, dtype, space in outs],
        in_specs=[pl.BlockSpec(memory_space=space) for space in ins],
        out_specs=specs,
        scratch_shapes=scratch,
        input_output_aliases=aliases or {},
        cost_estimate=pl.CostEstimate(flops=flops, bytes_accessed=moved, transcendentals=0),
        compiler_params=pltpu.CompilerParams(vmem_limit_bytes=limit << 20),
    )


def body(pooled, proj_weight, cluster):
    shards = lax.axis_size("docs")
    blocks = lax.axis_size("blk")
    devices = shards * blocks
    docs = pooled.shape[0]
    feature = proj_weight.shape[1]
    big_count = docs // 4
    small_count = docs - big_count
    cap_big = 2 * big_count // shards
    cap_small = rows_up(2 * small_count // devices, 16)
    small_slots = devices * cap_small
    big_slots = shards * cap_big
    big_total = blocks * big_slots
    sizes = (shards, blocks, cap_big, cap_small)
    f32, bf16, i32 = jnp.float32, jnp.bfloat16, jnp.int32
    vmem, hbm, smem, dma = pltpu.VMEM, pltpu.HBM, pltpu.SMEM, pltpu.SemaphoreType.DMA

    docs_at, blk_at = (lax.axis_index(axis).astype(i32).reshape(1) for axis in ("docs", "blk"))

    def along(x, axis, count, by):
        return lax.ppermute(x, axis, [(i, (i + by) % count) for i in range(count)])

    small_rows = feature // LANES * cap_small + 16
    small_rows = feature // LANES * cap_small + 16
    kinds = kinds_of(shards, blocks)
    big_rows = big_slots // kinds + rows_up(shards // kinds, 16)
    small_sent, info, *big_sent = call(
        functools.partial(sort_kernel, *sizes),
        [((devices, small_rows, LANES), bf16, hbm), ((8, docs), i32, hbm)] + [((big_rows, feature), bf16, hbm)] * blocks,
        [smem, hbm, hbm, hbm],
        2 * docs * feature * (pooled.shape[1] + small_slots), 4 << 20, 60,
        [vmem(pooled.shape, bf16), vmem(proj_weight.shape, bf16), vmem((1, docs), i32),
         vmem((devices, small_rows, LANES), bf16), vmem((kinds, big_rows, feature), bf16),
         vmem((docs, feature), bf16), vmem((8, docs), i32), dma((4,)), dma((4,)), dma((blocks,))],
    )(blk_at, pooled, proj_weight, cluster.reshape(1, docs))

    homes = [home_of(d, blocks) for d in range(kinds)]
    big_held = [big_sent[0]]
    for step in range(1, blocks):
        pairs = [(d * blocks + (home + step) % blocks, d * blocks + home) for d in range(shards) for home in homes]
        big_held.append(lax.ppermute(big_sent[step], ("docs", "blk"), pairs))

    small_sent, *grouped = call(
        functools.partial(group_kernel, shards, blocks, cap_big),
        [((devices, small_rows, LANES), bf16, hbm)]
        + [((blocks * cap_big + rows_up(blocks, 16), feature), bf16, vmem)] * shards,
        [smem, hbm] + [vmem] * blocks,
        shards * blocks * cap_big * feature, 4 << 20, aliases={1: 0},
    )(docs_at, small_sent, *big_held)

    got_small = lax.all_to_all(small_sent, ("docs", "blk"), split_axis=0, concat_axis=0, tiled=True)

    parts = [grouped[0]]
    for shift in range(1, shards):
        pairs = [((d + shift) % shards * blocks + home_of(d, blocks), d * blocks + home_of(d, blocks))
                 for d in range(shards)]
        parts.append(lax.ppermute(grouped[shift], ("docs", "blk"), pairs))

    back_big, = call(
        functools.partial(big_kernel, *sizes),
        [((blocks * rows_up(shards), LANES), f32, vmem)], [smem] + [vmem] * shards,
        2 * big_total * big_total * feature, 2 << 20,
    )(docs_at, *parts)
    back = call(
        functools.partial(small_kernel, shards, blocks, cap_small),
        [((rows_up(shards), LANES), f32, vmem)] * blocks, [smem, vmem, vmem],
        2 * small_slots * small_slots * feature, 2 << 20, 16,
        [vmem((small_slots, feature), bf16)],
    )(blk_at, got_small, back_big)
    back = [back[0]] + [along(back[by], "blk", blocks, by) for by in range(1, blocks)]
    back = call(
        functools.partial(turn_kernel, shards),
        [((rows_up(blocks), LANES), f32, vmem)] * shards, [smem] + [vmem] * blocks,
        shards * blocks * LANES, 1 << 16,
    )(docs_at, *back)
    back = [back[0]] + [along(back[by], "docs", shards, by) for by in range(1, shards)]

    masks = call(
        functools.partial(masks_kernel, shards, blocks),
        [((3 * shards * rows_up(blocks), docs), bf16, vmem), ((LANES, docs), f32, vmem)], [smem, smem, vmem],
        docs * LANES, 1 << 18,
    )(docs_at, blk_at, info)
    out, = call(
        finish_kernel, [((1, docs), f32, vmem)], [vmem] * (shards + 2),
        6 * docs * LANES * devices, 1 << 18,
    )(*back, *masks)
    return out.reshape(docs)


def solution(mesh):
    in_specs = (P(("slab", "docs", "blk"), None), P(), P(("slab", "docs", "blk")))
    out_specs = P(("slab", "docs", "blk"))
    return jax.shard_map(body, mesh=mesh, in_specs=in_specs, out_specs=out_specs, check_vma=False)
```

```python
import functools

import jax
import jax.numpy as jnp
from jax import lax
from jax.experimental import pallas as pl
from jax.experimental.pallas import tpu as pltpu
from jax.sharding import PartitionSpec as P

BIG_OWN = 4
LANES = 128


def modulo(x, n):
    return x & (n - 1) if n & (n - 1) == 0 else lax.rem(x, jnp.int32(n))


def quotient(x, n):
    if n & (n - 1) == 0:
        return lax.shift_right_logical(x, jnp.int32(n.bit_length() - 1))
    return lax.div(x, jnp.int32(n))


def iota(shape, axis):
    return lax.broadcasted_iota(jnp.int32, shape, axis)


def dot_nt(a, b):
    return lax.dot_general(a, b, (((1,), (1,)), ((), ())), preferred_element_type=jnp.float32)


def tile_of(rows, most=256):
    tile = most
    while rows % tile:
        tile //= 2
    return tile


def home_of(docs, blocks):
    return max(blocks // 2 - 1, 0) + (docs & min(blocks - 1, 1))


def picked_rows(rows_ref, slot, first, count):
    pick = (iota((count, rows_ref.shape[0]), 0) + first == slot).astype(jnp.float32).astype(jnp.bfloat16)
    return jnp.dot(pick, rows_ref[...], preferred_element_type=jnp.float32).astype(jnp.bfloat16)


def sort_kernel(shards, blocks, cap_big, cap_small, pooled_hbm, weight_hbm, cluster_hbm, small_hbm, rows_hbm, info_hbm,
                pooled_ref, weight_ref, cluster_ref, small_ref, rows_ref, info_ref, sems, small_sems):
    docs, feature = rows_ref.shape
    devices = shards * blocks
    limit = BIG_OWN * shards
    buckets = devices + shards

    fetches = [pltpu.make_async_copy(source, target, sems.at[n]) for n, (source, target) in enumerate(
        ((cluster_hbm, cluster_ref), (weight_hbm, weight_ref), (pooled_hbm, pooled_ref)))]
    for fetch in fetches:
        fetch.start()
    fetches[0].wait()

    cluster = cluster_ref[...]
    is_big = cluster < limit
    owner = modulo(cluster, shards)
    past = jnp.maximum(cluster - limit, 0)
    target = modulo(past, devices)
    bucket = jnp.where(is_big, devices + owner, target)

    padded = -(-buckets // 16) * 16
    hot = (iota((padded, docs), 0) == bucket).astype(jnp.float32)
    earlier = (iota((docs, docs), 0) < iota((docs, docs), 1)).astype(jnp.float32).astype(jnp.bfloat16)
    before = jnp.dot(hot.astype(jnp.bfloat16), earlier, preferred_element_type=jnp.float32)
    rank = jnp.sum(before * hot, axis=0, keepdims=True).astype(jnp.int32)

    info_ref[0:1, :] = jnp.where(is_big, owner * blocks + home_of(owner, blocks), target)
    info_ref[1:2, :] = jnp.where(is_big, cap_small + rank, rank)
    info_ref[2:3, :] = jnp.where(is_big, owner * cap_big + rank, -1)
    info_ref[3:4, :] = jnp.where(is_big, quotient(cluster, shards), quotient(past, devices)) + 1
    info_ref[4:5, :] = bucket
    info_ref[5:8, :] = jnp.zeros((3, docs), jnp.int32)
    sends = [pltpu.make_async_copy(info_ref, info_hbm, sems.at[3])]
    sends[0].start()
    small_slot = jnp.where(is_big, -1, target * cap_small + rank)
    ids = ids_table(iota((devices, docs), 0) == bucket, info_ref)

    for fetch in fetches[1:]:
        fetch.wait()
    projected = jnp.dot(pooled_ref[...], weight_ref[...], preferred_element_type=jnp.float32)
    squares = jnp.sum(projected * projected, axis=1, keepdims=True)
    rows_ref[...] = (projected * lax.rsqrt(squares + 1e-06)).astype(jnp.bfloat16)
    sends.append(pltpu.make_async_copy(rows_ref, rows_hbm, sems.at[4]))
    sends[-1].start()

    slabs = feature // LANES
    group = devices // small_sems.shape[0]
    for part in range(small_sems.shape[0]):
        first = part * group
        picked = picked_rows(rows_ref, small_slot, first * cap_small, group * cap_small)
        for device in range(group):
            for slab in range(slabs):
                small_ref[first + device, slab * cap_small:(slab + 1) * cap_small, :] = picked[
                    device * cap_small:(device + 1) * cap_small, slab * LANES:(slab + 1) * LANES]
            small_ref[first + device, slabs * cap_small:, :] = jnp.broadcast_to(
                ids[first + device:first + device + 1, :], (16, LANES)).astype(jnp.bfloat16)
        sends.append(pltpu.make_async_copy(
            small_ref.at[pl.ds(first, group)], small_hbm.at[pl.ds(first, group)], small_sems.at[part]))
        sends[-1].start()
    for send in sends:
        send.wait()


def ids_table(mine, info_ref):
    docs = info_ref.shape[1]
    quota = info_ref[3:4, :].astype(jnp.float32)
    lanes = (iota((LANES, docs), 0) == info_ref[1:2, :]).astype(jnp.float32).astype(jnp.bfloat16)
    return dot_nt(jnp.where(mine, quota, 0.0).astype(jnp.bfloat16), lanes)


def sort_big_kernel(shards, blocks, cap_big, docs_at, rows_ref, info_ref, *big_refs):
    devices = shards * blocks
    for shift, ref in enumerate(big_refs):
        to = modulo(docs_at[0] + shift, shards)
        ref[0:cap_big, :] = picked_rows(rows_ref, info_ref[2:3, :], to * cap_big, cap_big)
        spare = ref.shape[0] - cap_big
        mine = (iota((spare, info_ref.shape[1]), 0) == 0) & (info_ref[4:5, :] == devices + to)
        ref[cap_big:, 0:LANES] = ids_table(mine, info_ref).astype(jnp.bfloat16)
        ref[cap_big:, LANES:] = jnp.zeros((spare, ref.shape[1] - LANES), jnp.bfloat16)


def group_kernel(cap_big, *refs):
    held, group_ref = refs[:-1], refs[-1]
    total = len(held) * cap_big
    spare = group_ref.shape[0] - total
    own = jnp.zeros((spare, LANES), jnp.float32)
    for shift, ref in enumerate(held):
        group_ref[shift * cap_big:(shift + 1) * cap_big, :] = ref[0:cap_big, :]
        table = ref[cap_big:, 0:LANES].astype(jnp.float32)
        own = jnp.where(iota(own.shape, 0) == shift, table[0:1, :], own)
    group_ref[total:, 0:LANES] = own.astype(jnp.bfloat16)
    group_ref[total:, LANES:] = jnp.zeros((spare, group_ref.shape[1] - LANES), jnp.bfloat16)


def turn(tables, at, count, outs):
    for step, out in enumerate(outs):
        to = modulo(at + step, count)
        out[...] = jnp.zeros(out.shape, jnp.float32)
        for place, table in enumerate(tables):
            out[place:place + 1, :] = jnp.sum(
                jnp.where(iota(table.shape, 0) == to, table, 0.0), axis=0, keepdims=True)


def turn_kernel(count, at_ref, *refs):
    held, outs = refs[:-count], refs[-count:]
    turn([ref[...] for ref in held], at_ref[0], count, outs)


def rows_up(count, to=8):
    return -(-count // to) * to


def small_sources(total, blocks, cap_small):
    at = iota((1, total), 1)
    source = at // cap_small
    return source // blocks, modulo(source, blocks), lax.rem(at, jnp.int32(cap_small))


def big_steps(blocks):
    return [0] + list(range(2, blocks)) + ([1] if blocks > 1 else [])


def big_sources(total, shards, cap_big, cap_small):
    at = iota((1, total), 1)
    return (at // (shards * cap_big), modulo(at // cap_big, shards),
            cap_small + lax.rem(at, jnp.int32(cap_big)))


def big_ids(held, sources):
    part, shift, lane = sources
    spare = held[0].shape[0] - part.shape[1] // len(held)
    values = jnp.concatenate([ref[ref.shape[0] - spare:, 0:LANES] for ref in held], axis=0)
    return ids_from(values, part * spare + shift, lane)


def big_pairs(held, row_ids, col_ids, bests, pairs):
    size = row_ids.shape[1] // len(held)
    for row, col in pairs:
        same = 0 if row == col else None
        bests[col] = jnp.maximum(bests[col], block_best(
            held[row][0:size, :], col_ids[row * size:(row + 1) * size], same,
            held[col][0:size, :], row_ids[:, col * size:(col + 1) * size], same))
    return bests


def ids_from(values, row, lane):
    pick = (iota((LANES, lane.shape[1]), 0) == lane).astype(jnp.float32).astype(jnp.bfloat16)
    found = jnp.dot(values, pick, preferred_element_type=jnp.float32)
    return jnp.sum(jnp.where(iota(found.shape, 0) == row, found, 0.0), axis=0, keepdims=True)


def as_column(row):
    return jnp.broadcast_to(row, (8, row.shape[1])).T[:, 0:1]


def block_best(queries, col_ids, first_row, others, row_ids, first_col):
    scores = dot_nt(queries, others)
    allowed = (col_ids == row_ids) & (row_ids > 0.0)
    if first_row is not None:
        allowed &= (iota(scores.shape, 0) + first_row) != (iota(scores.shape, 1) + first_col)
    return jnp.max(jnp.where(allowed, scores, -1.0), axis=0, keepdims=True)


def spread(best, row, lane, rows):
    total = best.shape[1]
    mine = jnp.where(iota((rows, total), 0) == row, best, 0.0)
    place = (iota((LANES, total), 0) == lane).astype(jnp.float32).astype(jnp.bfloat16)
    found = dot_nt(thirds(mine), place)
    return found[:rows] + found[rows:2 * rows] + found[2 * rows:]


def thirds(values):
    high = values.astype(jnp.bfloat16)
    rest = values - high.astype(jnp.float32)
    middle = rest.astype(jnp.bfloat16)
    low = (rest - middle.astype(jnp.float32)).astype(jnp.bfloat16)
    return jnp.concatenate([high, middle, low], axis=0)


def big_kernel(shards, cap_big, cap_small, *refs):
    held, best_ref = refs[:-1], refs[-1]
    size = shards * cap_big
    row_ids = big_ids(held, big_sources(len(held) * size, shards, cap_big, cap_small))
    col_ids = as_column(row_ids)
    pairs = [(row, col) for row in range(len(held)) for col in range(len(held))]
    bests = big_pairs(held, row_ids, col_ids, [jnp.full((1, size), -1.0, jnp.float32)] * len(held), pairs)
    best_ref[...] = jnp.concatenate(bests, axis=1)


def big_last_kernel(shards, blocks, cap_big, cap_small, docs_at, small_ref, best_ref, *refs):
    held, back_refs = refs[:blocks], refs[blocks:]
    size = shards * cap_big
    high = back_refs[0].shape[0]
    part, shift, lane = big_sources(blocks * size, shards, cap_big, cap_small)
    row_ids = big_ids(held, (part, shift, lane))
    col_ids = as_column(row_ids)
    last = blocks - 1
    pairs = [(row, last) for row in range(blocks)] + [(last, col) for col in range(last)]
    bests = [best_ref[:, col * size:(col + 1) * size] for col in range(last)]
    bests = big_pairs(held, row_ids, col_ids, bests + [jnp.full((1, size), -1.0, jnp.float32)], pairs)
    docs = modulo(docs_at[0] + shards - shift, shards)
    step = jnp.where(part == 0, 0, jnp.where(part == last, 1, part + 1))
    back = small_ref[...] + spread(jnp.concatenate(bests, axis=1), step * high + docs, lane, small_ref.shape[0])
    for at, ref in enumerate(back_refs):
        ref[...] = back[at * high:(at + 1) * high, :]


def small_kernel(shards, blocks, cap_small, blk_at, got_ref, back_ref, rows_ref):
    total, feature = rows_ref.shape
    high = back_ref.shape[0] // blocks
    slabs = feature // LANES
    values = []
    for device in range(got_ref.shape[0]):
        for slab in range(slabs):
            rows_ref[device * cap_small:(device + 1) * cap_small, slab * LANES:(slab + 1) * LANES] = got_ref[
                device, slab * cap_small:(slab + 1) * cap_small, :]
        values.append(got_ref[device, slabs * cap_small:, :].astype(jnp.float32)[0:1, :])
    docs, blk, lane = small_sources(total, blocks, cap_small)
    row_ids = ids_from(jnp.concatenate(values, axis=0).astype(jnp.bfloat16), docs * blocks + blk, lane)
    col_ids = as_column(row_ids)
    tile = tile_of(total)
    best = jnp.full((1, total), -1.0, jnp.float32)
    for at in range(0, total, tile):
        best = jnp.maximum(best, block_best(
            rows_ref[at:at + tile, :], col_ids[at:at + tile], at, rows_ref[...], row_ids, 0))
    row = modulo(blk + blocks - blk_at[0], blocks) * high + docs
    back_ref[...] = spread(best, row, lane, back_ref.shape[0])


def masks_kernel(shards, blocks, docs_at, blk_at, info_ref, row_ref, lane_ref):
    device = info_ref[0:1, :]
    high = row_ref.shape[0] // (3 * shards)
    row = (modulo(docs_at[0] + shards - device // blocks, shards) * high
           + modulo(blk_at[0] + blocks - modulo(device, blocks), blocks))
    mask = (iota((shards * high, row_ref.shape[1]), 0) == row).astype(jnp.float32)
    row_ref[...] = jnp.concatenate([mask] * 3, axis=0).astype(jnp.bfloat16)
    lane_ref[...] = (iota(lane_ref.shape, 0) == info_ref[1:2, :]).astype(jnp.float32)


def finish_kernel(*refs):
    held, (row_ref, lane_ref, out_ref) = refs[:-3], refs[-3:]
    values = thirds(jnp.concatenate([ref[...] for ref in held], axis=0))
    found = lax.dot_general(values, row_ref[...], (((0,), (0,)), ((), ())), preferred_element_type=jnp.float32)
    out_ref[...] = jnp.sum(jnp.where(lane_ref[...] > 0.0, found, 0.0), axis=0, keepdims=True)


def call(kernel, outs, ins, flops, moved, limit=16, scratch=()):
    specs = [pl.BlockSpec(memory_space=space) for _, _, space in outs]
    return pl.pallas_call(
        kernel,
        out_shape=[space(shape, dtype) if space is pltpu.HBM else jax.ShapeDtypeStruct(shape, dtype)
                   for shape, dtype, space in outs],
        in_specs=[pl.BlockSpec(memory_space=space) for space in ins],
        out_specs=specs,
        scratch_shapes=scratch,
        cost_estimate=pl.CostEstimate(flops=flops, bytes_accessed=moved, transcendentals=0),
        compiler_params=pltpu.CompilerParams(vmem_limit_bytes=limit << 20),
    )


def body(pooled, proj_weight, cluster):
    shards = lax.axis_size("docs")
    blocks = lax.axis_size("blk")
    devices = shards * blocks
    docs = pooled.shape[0]
    feature = proj_weight.shape[1]
    big_count = docs // 4
    small_count = docs - big_count
    cap_big = 2 * big_count // shards
    cap_small = rows_up(2 * small_count // devices, 16)
    small_slots = devices * cap_small
    big_slots = shards * cap_big
    big_total = blocks * big_slots
    sizes = (shards, blocks, cap_big, cap_small)
    f32, bf16, i32 = jnp.float32, jnp.bfloat16, jnp.int32
    vmem, hbm, smem, dma = pltpu.VMEM, pltpu.HBM, pltpu.SMEM, pltpu.SemaphoreType.DMA

    docs_at, blk_at = (lax.axis_index(axis).astype(i32).reshape(1) for axis in ("docs", "blk"))

    def along(x, axis, count, by):
        return lax.ppermute(x, axis, [(i, (i + by) % count) for i in range(count)])

    small_rows = feature // LANES * cap_small + 16
    small_sent, rows, info = call(
        functools.partial(sort_kernel, *sizes),
        [((devices, small_rows, LANES), bf16, hbm), ((docs, feature), bf16, hbm), ((8, docs), i32, hbm)],
        [hbm, hbm, hbm],
        2 * docs * feature * (pooled.shape[1] + small_slots), 4 << 20, 60,
        [vmem(pooled.shape, bf16), vmem(proj_weight.shape, bf16), vmem((1, docs), i32),
         vmem((devices, small_rows, LANES), bf16), vmem((docs, feature), bf16), vmem((8, docs), i32),
         dma((5,)), dma((4,))],
    )(pooled, proj_weight, cluster.reshape(1, docs))

    got_small = lax.all_to_all(small_sent, ("docs", "blk"), split_axis=0, concat_axis=0, tiled=True)

    big_sent = call(
        functools.partial(sort_big_kernel, shards, blocks, cap_big),
        [((cap_big + 16, feature), bf16, vmem)] * shards,
        [smem, vmem, vmem],
        2 * docs * feature * big_slots, 2 << 20,
    )(docs_at, rows, info)
    held = [big_sent[0]] + [along(big_sent[by], "docs", shards, by) for by in range(1, shards)]
    group, = call(
        functools.partial(group_kernel, cap_big),
        [((big_slots + rows_up(shards, 16), feature), bf16, vmem)], [vmem] * shards,
        big_slots * feature, 1 << 20,
    )(*held)
    parts = [group]
    for step in big_steps(blocks)[1:]:
        pairs = [(d * blocks + (home_of(d, blocks) + step) % blocks, d * blocks + home_of(d, blocks))
                 for d in range(shards)]
        parts.append(lax.ppermute(group, ("docs", "blk"), pairs))

    back_small, = call(
        functools.partial(small_kernel, shards, blocks, cap_small),
        [((blocks * rows_up(shards), LANES), f32, vmem)], [smem, vmem],
        2 * small_slots * small_slots * feature, 2 << 20, 16,
        [vmem((small_slots, feature), bf16)],
    )(blk_at, got_small)
    early, = call(
        functools.partial(big_kernel, shards, cap_big, cap_small),
        [((1, big_total - big_slots), f32, vmem)], [vmem] * (blocks - 1),
        2 * (big_total - big_slots) ** 2 * feature, 2 << 20,
    )(*parts[:-1])
    back = call(
        functools.partial(big_last_kernel, *sizes),
        [((rows_up(shards), LANES), f32, vmem)] * blocks, [smem] + [vmem] * (blocks + 2),
        2 * (2 * big_total - big_slots) * big_slots * feature, 2 << 20,
    )(docs_at, back_small, early, *parts)
    back = [back[0]] + [along(back[by], "blk", blocks, by) for by in range(1, blocks)]
    back = call(
        functools.partial(turn_kernel, shards),
        [((rows_up(blocks), LANES), f32, vmem)] * shards, [smem] + [vmem] * blocks,
        shards * blocks * LANES, 1 << 16,
    )(docs_at, *back)
    back = [back[0]] + [along(back[by], "docs", shards, by) for by in range(1, shards)]

    masks = call(
        functools.partial(masks_kernel, shards, blocks),
        [((3 * shards * rows_up(blocks), docs), bf16, vmem), ((LANES, docs), f32, vmem)], [smem, smem, vmem],
        docs * LANES, 1 << 18,
    )(docs_at, blk_at, info)
    out, = call(
        finish_kernel, [((1, docs), f32, vmem)], [vmem] * (shards + 2),
        6 * docs * LANES * devices, 1 << 18,
    )(*back, *masks)
    return out.reshape(docs)


def solution(mesh):
    in_specs = (P(("slab", "docs", "blk"), None), P(), P(("slab", "docs", "blk")))
    out_specs = P(("slab", "docs", "blk"))
    return jax.shard_map(body, mesh=mesh, in_specs=in_specs, out_specs=out_specs, check_vma=False)
```

```python
import functools

import jax
import jax.numpy as jnp
from jax import lax
from jax.experimental import pallas as pl
from jax.experimental.pallas import tpu as pltpu
from jax.sharding import PartitionSpec as P

BIG_OWN = 4
LANES = 128


def modulo(x, n):
    return x & (n - 1) if n & (n - 1) == 0 else lax.rem(x, jnp.int32(n))


def quotient(x, n):
    if n & (n - 1) == 0:
        return lax.shift_right_logical(x, jnp.int32(n.bit_length() - 1))
    return lax.div(x, jnp.int32(n))


def iota(shape, axis):
    return lax.broadcasted_iota(jnp.int32, shape, axis)


def dot_nt(a, b):
    return lax.dot_general(a, b, (((1,), (1,)), ((), ())), preferred_element_type=jnp.float32)


def tile_of(rows, most=256):
    tile = most
    while rows % tile:
        tile //= 2
    return tile


def home_of(docs, blocks):
    return max(blocks // 2 - 1, 0) + (docs & min(blocks - 1, 1))


def picked_rows(rows_ref, slot, first, count):
    pick = (iota((count, rows_ref.shape[0]), 0) + first == slot).astype(jnp.float32).astype(jnp.bfloat16)
    return jnp.dot(pick, rows_ref[...], preferred_element_type=jnp.float32).astype(jnp.bfloat16)


def sort_kernel(shards, blocks, cap_big, cap_small, docs_at, pooled_hbm, weight_hbm, cluster_hbm, small_hbm, info_hbm,
                *refs):
    big_hbm = refs[:shards]
    (pooled_ref, weight_ref, cluster_ref, small_ref, big_ref, rows_ref, info_ref, sems, small_sems,
     big_sems) = refs[shards:]
    docs, feature = rows_ref.shape
    devices = shards * blocks
    limit = BIG_OWN * shards
    buckets = devices + shards

    fetches = [pltpu.make_async_copy(source, target, sems.at[n]) for n, (source, target) in enumerate(
        ((cluster_hbm, cluster_ref), (weight_hbm, weight_ref), (pooled_hbm, pooled_ref)))]
    for fetch in fetches:
        fetch.start()
    fetches[0].wait()

    cluster = cluster_ref[...]
    is_big = cluster < limit
    owner = modulo(cluster, shards)
    past = jnp.maximum(cluster - limit, 0)
    target = modulo(past, devices)
    bucket = jnp.where(is_big, devices + owner, target)

    padded = -(-buckets // 16) * 16
    hot = (iota((padded, docs), 0) == bucket).astype(jnp.float32)
    earlier = (iota((docs, docs), 0) < iota((docs, docs), 1)).astype(jnp.float32).astype(jnp.bfloat16)
    before = jnp.dot(hot.astype(jnp.bfloat16), earlier, preferred_element_type=jnp.float32)
    rank = jnp.sum(before * hot, axis=0, keepdims=True).astype(jnp.int32)

    info_ref[0:1, :] = jnp.where(is_big, owner * blocks + home_of(owner, blocks), target)
    info_ref[1:2, :] = jnp.where(is_big, cap_small + rank, rank)
    info_ref[2:3, :] = jnp.where(is_big, quotient(cluster, shards), quotient(past, devices)) + 1
    info_ref[3:8, :] = jnp.zeros((5, docs), jnp.int32)
    sends = [pltpu.make_async_copy(info_ref, info_hbm, sems.at[3])]
    sends[0].start()
    small_slot = jnp.where(is_big, -1, target * cap_small + rank)
    ids = ids_table(iota((devices, docs), 0) == bucket, info_ref)
    shift = modulo(owner + shards - docs_at[0], shards)
    big_slot = jnp.where(is_big, shift * cap_big + rank, -1)
    for by in range(shards):
        mine = (iota((16, docs), 0) == 0) & is_big & (shift == by)
        big_ref[by, cap_big:, 0:LANES] = ids_table(mine, info_ref).astype(jnp.bfloat16)
        big_ref[by, cap_big:, LANES:] = jnp.zeros((16, feature - LANES), jnp.bfloat16)

    for fetch in fetches[1:]:
        fetch.wait()
    projected = jnp.dot(pooled_ref[...], weight_ref[...], preferred_element_type=jnp.float32)
    squares = jnp.sum(projected * projected, axis=1, keepdims=True)
    rows_ref[...] = (projected * lax.rsqrt(squares + 1e-06)).astype(jnp.bfloat16)
    picked = picked_rows(rows_ref, big_slot, 0, shards * cap_big)
    for by, out in enumerate(big_hbm):
        big_ref[by, 0:cap_big, :] = picked[by * cap_big:(by + 1) * cap_big, :]
        sends.append(pltpu.make_async_copy(big_ref.at[by], out, big_sems.at[by]))
        sends[-1].start()

    slabs = feature // LANES
    group = devices // small_sems.shape[0]
    for part in range(small_sems.shape[0]):
        first = part * group
        picked = picked_rows(rows_ref, small_slot, first * cap_small, group * cap_small)
        for device in range(group):
            for slab in range(slabs):
                small_ref[first + device, slab * cap_small:(slab + 1) * cap_small, :] = picked[
                    device * cap_small:(device + 1) * cap_small, slab * LANES:(slab + 1) * LANES]
            small_ref[first + device, slabs * cap_small:, :] = jnp.broadcast_to(
                ids[first + device:first + device + 1, :], (8, LANES)).astype(jnp.bfloat16)
        sends.append(pltpu.make_async_copy(
            small_ref.at[pl.ds(first, group)], small_hbm.at[pl.ds(first, group)], small_sems.at[part]))
        sends[-1].start()
    for send in sends:
        send.wait()


def ids_table(mine, info_ref):
    docs = info_ref.shape[1]
    quota = info_ref[2:3, :].astype(jnp.float32)
    lanes = (iota((LANES, docs), 0) == info_ref[1:2, :]).astype(jnp.float32).astype(jnp.bfloat16)
    return dot_nt(jnp.where(mine, quota, 0.0).astype(jnp.bfloat16), lanes)


def group_kernel(cap_big, *refs):
    held, group_ref = refs[:-1], refs[-1]
    total = len(held) * cap_big
    spare = group_ref.shape[0] - total
    own = jnp.zeros((spare, LANES), jnp.float32)
    for shift, ref in enumerate(held):
        group_ref[shift * cap_big:(shift + 1) * cap_big, :] = ref[0:cap_big, :]
        table = ref[cap_big:, 0:LANES].astype(jnp.float32)
        own = jnp.where(iota(own.shape, 0) == shift, table[0:1, :], own)
    group_ref[total:, 0:LANES] = own.astype(jnp.bfloat16)
    group_ref[total:, LANES:] = jnp.zeros((spare, group_ref.shape[1] - LANES), jnp.bfloat16)


def turn(tables, at, count, outs):
    for step, out in enumerate(outs):
        to = modulo(at + step, count)
        out[...] = jnp.zeros(out.shape, jnp.float32)
        for place, table in enumerate(tables):
            out[place:place + 1, :] = jnp.sum(
                jnp.where(iota(table.shape, 0) == to, table, 0.0), axis=0, keepdims=True)


def turn_kernel(count, at_ref, *refs):
    held, outs = refs[:-count], refs[-count:]
    turn([ref[...] for ref in held], at_ref[0], count, outs)


def rows_up(count, to=8):
    return -(-count // to) * to


def small_sources(total, blocks, cap_small):
    at = iota((1, total), 1)
    source = at // cap_small
    return source // blocks, modulo(source, blocks), lax.rem(at, jnp.int32(cap_small))


def big_steps(blocks):
    return [0] + list(range(2, blocks)) + ([1] if blocks > 1 else [])


def big_sources(total, shards, cap_big, cap_small):
    at = iota((1, total), 1)
    return (at // (shards * cap_big), modulo(at // cap_big, shards),
            cap_small + lax.rem(at, jnp.int32(cap_big)))


def big_ids(held, sources):
    part, shift, lane = sources
    spare = held[0].shape[0] - part.shape[1] // len(held)
    values = jnp.concatenate([ref[ref.shape[0] - spare:, 0:LANES] for ref in held], axis=0)
    return ids_from(values, part * spare + shift, lane)


def big_pairs(held, row_ids, col_ids, bests, pairs):
    size = row_ids.shape[1] // len(held)
    for row, col in pairs:
        same = 0 if row == col else None
        bests[col] = jnp.maximum(bests[col], block_best(
            held[row][0:size, :], col_ids[row * size:(row + 1) * size], same,
            held[col][0:size, :], row_ids[:, col * size:(col + 1) * size], same))
    return bests


def ids_from(values, row, lane):
    pick = (iota((LANES, lane.shape[1]), 0) == lane).astype(jnp.float32).astype(jnp.bfloat16)
    found = jnp.dot(values, pick, preferred_element_type=jnp.float32)
    return jnp.sum(jnp.where(iota(found.shape, 0) == row, found, 0.0), axis=0, keepdims=True)


def as_column(row):
    return jnp.broadcast_to(row, (8, row.shape[1])).T[:, 0:1]


def block_best(queries, col_ids, first_row, others, row_ids, first_col):
    scores = dot_nt(queries, others)
    allowed = (col_ids == row_ids) & (row_ids > 0.0)
    if first_row is not None:
        allowed &= (iota(scores.shape, 0) + first_row) != (iota(scores.shape, 1) + first_col)
    return jnp.max(jnp.where(allowed, scores, -1.0), axis=0, keepdims=True)


def spread(best, row, lane, rows):
    total = best.shape[1]
    mine = jnp.where(iota((rows, total), 0) == row, best, 0.0)
    place = (iota((LANES, total), 0) == lane).astype(jnp.float32).astype(jnp.bfloat16)
    found = dot_nt(thirds(mine), place)
    return found[:rows] + found[rows:2 * rows] + found[2 * rows:]


def thirds(values):
    high = values.astype(jnp.bfloat16)
    rest = values - high.astype(jnp.float32)
    middle = rest.astype(jnp.bfloat16)
    low = (rest - middle.astype(jnp.float32)).astype(jnp.bfloat16)
    return jnp.concatenate([high, middle, low], axis=0)


def big_kernel(shards, cap_big, cap_small, *refs):
    held, best_ref = refs[:-1], refs[-1]
    size = shards * cap_big
    row_ids = big_ids(held, big_sources(len(held) * size, shards, cap_big, cap_small))
    col_ids = as_column(row_ids)
    pairs = [(row, col) for row in range(len(held)) for col in range(len(held))]
    bests = big_pairs(held, row_ids, col_ids, [jnp.full((1, size), -1.0, jnp.float32)] * len(held), pairs)
    best_ref[...] = jnp.concatenate(bests, axis=1)


def big_last_kernel(shards, blocks, cap_big, cap_small, docs_at, small_ref, best_ref, *refs):
    held, back_refs = refs[:blocks], refs[blocks:]
    size = shards * cap_big
    high = back_refs[0].shape[0]
    part, shift, lane = big_sources(blocks * size, shards, cap_big, cap_small)
    row_ids = big_ids(held, (part, shift, lane))
    col_ids = as_column(row_ids)
    last = blocks - 1
    pairs = [(row, last) for row in range(blocks)] + [(last, col) for col in range(last)]
    bests = [best_ref[:, col * size:(col + 1) * size] for col in range(last)]
    bests = big_pairs(held, row_ids, col_ids, bests + [jnp.full((1, size), -1.0, jnp.float32)], pairs)
    docs = modulo(docs_at[0] + shards - shift, shards)
    step = jnp.where(part == 0, 0, jnp.where(part == last, 1, part + 1))
    back = small_ref[...] + spread(jnp.concatenate(bests, axis=1), step * high + docs, lane, small_ref.shape[0])
    for at, ref in enumerate(back_refs):
        ref[...] = back[at * high:(at + 1) * high, :]


def small_kernel(shards, blocks, cap_small, blk_at, got_ref, back_ref, rows_ref):
    total, feature = rows_ref.shape
    high = back_ref.shape[0] // blocks
    slabs = feature // LANES
    values = []
    for device in range(got_ref.shape[0]):
        for slab in range(slabs):
            rows_ref[device * cap_small:(device + 1) * cap_small, slab * LANES:(slab + 1) * LANES] = got_ref[
                device, slab * cap_small:(slab + 1) * cap_small, :]
        values.append(got_ref[device, slabs * cap_small:, :].astype(jnp.float32)[0:1, :])
    docs, blk, lane = small_sources(total, blocks, cap_small)
    row_ids = ids_from(jnp.concatenate(values, axis=0).astype(jnp.bfloat16), docs * blocks + blk, lane)
    col_ids = as_column(row_ids)
    tile = tile_of(total)
    best = jnp.full((1, total), -1.0, jnp.float32)
    for at in range(0, total, tile):
        best = jnp.maximum(best, block_best(
            rows_ref[at:at + tile, :], col_ids[at:at + tile], at, rows_ref[...], row_ids, 0))
    row = modulo(blk + blocks - blk_at[0], blocks) * high + docs
    back_ref[...] = spread(best, row, lane, back_ref.shape[0])


def masks_kernel(shards, blocks, docs_at, blk_at, info_ref, row_ref, lane_ref):
    device = info_ref[0:1, :]
    high = row_ref.shape[0] // (3 * shards)
    row = (modulo(docs_at[0] + shards - device // blocks, shards) * high
           + modulo(blk_at[0] + blocks - modulo(device, blocks), blocks))
    mask = (iota((shards * high, row_ref.shape[1]), 0) == row).astype(jnp.float32)
    row_ref[...] = jnp.concatenate([mask] * 3, axis=0).astype(jnp.bfloat16)
    lane_ref[...] = (iota(lane_ref.shape, 0) == info_ref[1:2, :]).astype(jnp.float32)


def finish_kernel(*refs):
    held, (row_ref, lane_ref, out_ref) = refs[:-3], refs[-3:]
    values = thirds(jnp.concatenate([ref[...] for ref in held], axis=0))
    found = lax.dot_general(values, row_ref[...], (((0,), (0,)), ((), ())), preferred_element_type=jnp.float32)
    out_ref[...] = jnp.sum(jnp.where(lane_ref[...] > 0.0, found, 0.0), axis=0, keepdims=True)


def call(kernel, outs, ins, flops, moved, limit=16, scratch=()):
    specs = [pl.BlockSpec(memory_space=space) for _, _, space in outs]
    return pl.pallas_call(
        kernel,
        out_shape=[space(shape, dtype) if space is pltpu.HBM else jax.ShapeDtypeStruct(shape, dtype)
                   for shape, dtype, space in outs],
        in_specs=[pl.BlockSpec(memory_space=space) for space in ins],
        out_specs=specs,
        scratch_shapes=scratch,
        cost_estimate=pl.CostEstimate(flops=flops, bytes_accessed=moved, transcendentals=0),
        compiler_params=pltpu.CompilerParams(vmem_limit_bytes=limit << 20),
    )


def body(pooled, proj_weight, cluster):
    shards = lax.axis_size("docs")
    blocks = lax.axis_size("blk")
    devices = shards * blocks
    docs = pooled.shape[0]
    feature = proj_weight.shape[1]
    big_count = docs // 4
    small_count = docs - big_count
    cap_big = 2 * big_count // shards
    cap_small = rows_up(2 * small_count // devices, 16)
    small_slots = devices * cap_small
    big_slots = shards * cap_big
    big_total = blocks * big_slots
    sizes = (shards, blocks, cap_big, cap_small)
    f32, bf16, i32 = jnp.float32, jnp.bfloat16, jnp.int32
    vmem, hbm, smem, dma = pltpu.VMEM, pltpu.HBM, pltpu.SMEM, pltpu.SemaphoreType.DMA

    docs_at, blk_at = (lax.axis_index(axis).astype(i32).reshape(1) for axis in ("docs", "blk"))

    def along(x, axis, count, by):
        return lax.ppermute(x, axis, [(i, (i + by) % count) for i in range(count)])

    small_rows = feature // LANES * cap_small + 8
    small_sent, info, *big_sent = call(
        functools.partial(sort_kernel, *sizes),
        [((devices, small_rows, LANES), bf16, hbm), ((8, docs), i32, hbm)] + [((cap_big + 16, feature), bf16, hbm)] * shards,
        [smem, hbm, hbm, hbm],
        2 * docs * feature * (pooled.shape[1] + small_slots), 4 << 20, 60,
        [vmem(pooled.shape, bf16), vmem(proj_weight.shape, bf16), vmem((1, docs), i32),
         vmem((devices, small_rows, LANES), bf16), vmem((shards, cap_big + 16, feature), bf16),
         vmem((docs, feature), bf16), vmem((8, docs), i32), dma((4,)), dma((4,)), dma((shards,))],
    )(docs_at, pooled, proj_weight, cluster.reshape(1, docs))

    got_small = lax.all_to_all(small_sent, ("docs", "blk"), split_axis=0, concat_axis=0, tiled=True)

    held = [big_sent[0]] + [along(big_sent[by], "docs", shards, by) for by in range(1, shards)]
    group, = call(
        functools.partial(group_kernel, cap_big),
        [((big_slots + rows_up(shards, 16), feature), bf16, vmem)], [vmem] * shards,
        big_slots * feature, 64 << 20,
    )(*held)
    parts = [group]
    for step in big_steps(blocks)[1:]:
        pairs = [(d * blocks + (home_of(d, blocks) + step) % blocks, d * blocks + home_of(d, blocks))
                 for d in range(shards)]
        parts.append(lax.ppermute(group, ("docs", "blk"), pairs))

    back_small, = call(
        functools.partial(small_kernel, shards, blocks, cap_small),
        [((blocks * rows_up(shards), LANES), f32, vmem)], [smem, vmem],
        2 * small_slots * small_slots * feature, 2 << 20, 16,
        [vmem((small_slots, feature), bf16)],
    )(blk_at, got_small)
    early, = call(
        functools.partial(big_kernel, shards, cap_big, cap_small),
        [((1, big_total - big_slots), f32, vmem)], [vmem] * (blocks - 1),
        2 * (big_total - big_slots) ** 2 * feature, 2 << 20,
    )(*parts[:-1])
    back = call(
        functools.partial(big_last_kernel, *sizes),
        [((rows_up(shards), LANES), f32, vmem)] * blocks, [smem] + [vmem] * (blocks + 2),
        2 * (2 * big_total - big_slots) * big_slots * feature, 2 << 20,
    )(docs_at, back_small, early, *parts)
    back = [back[0]] + [along(back[by], "blk", blocks, by) for by in range(1, blocks)]
    back = call(
        functools.partial(turn_kernel, shards),
        [((rows_up(blocks), LANES), f32, vmem)] * shards, [smem] + [vmem] * blocks,
        shards * blocks * LANES, 1 << 16,
    )(docs_at, *back)
    back = [back[0]] + [along(back[by], "docs", shards, by) for by in range(1, shards)]

    masks = call(
        functools.partial(masks_kernel, shards, blocks),
        [((3 * shards * rows_up(blocks), docs), bf16, vmem), ((LANES, docs), f32, vmem)], [smem, smem, vmem],
        docs * LANES, 1 << 18,
    )(docs_at, blk_at, info)
    out, = call(
        finish_kernel, [((1, docs), f32, vmem)], [vmem] * (shards + 2),
        6 * docs * LANES * devices, 1 << 18,
    )(*back, *masks)
    return out.reshape(docs)


def solution(mesh):
    in_specs = (P(("slab", "docs", "blk"), None), P(), P(("slab", "docs", "blk")))
    out_specs = P(("slab", "docs", "blk"))
    return jax.shard_map(body, mesh=mesh, in_specs=in_specs, out_specs=out_specs, check_vma=False)
```

```python
import functools

import jax
import jax.numpy as jnp
from jax import lax
from jax.experimental import pallas as pl
from jax.experimental.pallas import tpu as pltpu
from jax.sharding import PartitionSpec as P

BIG_OWN = 4
LANES = 128


def modulo(x, n):
    return x & (n - 1) if n & (n - 1) == 0 else lax.rem(x, jnp.int32(n))


def quotient(x, n):
    if n & (n - 1) == 0:
        return lax.shift_right_logical(x, jnp.int32(n.bit_length() - 1))
    return lax.div(x, jnp.int32(n))


def iota(shape, axis):
    return lax.broadcasted_iota(jnp.int32, shape, axis)


def dot_nt(a, b):
    return lax.dot_general(a, b, (((1,), (1,)), ((), ())), preferred_element_type=jnp.float32)


def tile_of(rows, most=256):
    tile = most
    while rows % tile:
        tile //= 2
    return tile


def home_of(docs, blocks):
    return max(blocks // 2 - 1, 0) + (docs & min(blocks - 1, 1))


def picked_rows(rows_ref, slot, first, count):
    pick = (iota((count, rows_ref.shape[0]), 0) + first == slot).astype(jnp.float32).astype(jnp.bfloat16)
    return jnp.dot(pick, rows_ref[...], preferred_element_type=jnp.float32).astype(jnp.bfloat16)


def sort_kernel(shards, blocks, cap_big, cap_small, docs_at, pooled_hbm, weight_hbm, cluster_hbm, small_hbm, info_hbm,
                *refs):
    big_hbm = refs[:shards]
    (pooled_ref, weight_ref, cluster_ref, small_ref, big_ref, rows_ref, info_ref, sems, small_sems,
     big_sems) = refs[shards:]
    docs, feature = rows_ref.shape
    devices = shards * blocks
    limit = BIG_OWN * shards
    buckets = devices + shards

    fetches = [pltpu.make_async_copy(source, target, sems.at[n]) for n, (source, target) in enumerate(
        ((cluster_hbm, cluster_ref), (weight_hbm, weight_ref), (pooled_hbm, pooled_ref)))]
    for fetch in fetches:
        fetch.start()
    fetches[0].wait()

    cluster = cluster_ref[...]
    is_big = cluster < limit
    owner = modulo(cluster, shards)
    past = jnp.maximum(cluster - limit, 0)
    target = modulo(past, devices)
    bucket = jnp.where(is_big, devices + owner, target)

    padded = -(-buckets // 16) * 16
    hot = (iota((padded, docs), 0) == bucket).astype(jnp.float32)
    earlier = (iota((docs, docs), 0) < iota((docs, docs), 1)).astype(jnp.float32).astype(jnp.bfloat16)
    before = jnp.dot(hot.astype(jnp.bfloat16), earlier, preferred_element_type=jnp.float32)
    rank = jnp.sum(before * hot, axis=0, keepdims=True).astype(jnp.int32)

    info_ref[0:1, :] = jnp.where(is_big, owner * blocks + home_of(owner, blocks), target)
    info_ref[1:2, :] = jnp.where(is_big, cap_small + rank, rank)
    info_ref[2:3, :] = jnp.where(is_big, quotient(cluster, shards), quotient(past, devices)) + 1
    info_ref[3:8, :] = jnp.zeros((5, docs), jnp.int32)
    sends = [pltpu.make_async_copy(info_ref, info_hbm, sems.at[3])]
    sends[0].start()
    small_slot = jnp.where(is_big, -1, target * cap_small + rank)
    ids = ids_table(iota((devices, docs), 0) == bucket, info_ref)
    shift = modulo(owner + shards - docs_at[0], shards)
    big_slot = jnp.where(is_big, shift * cap_big + rank, -1)
    for by in range(shards):
        mine = (iota((16, docs), 0) == 0) & is_big & (shift == by)
        big_ref[by, cap_big:, 0:LANES] = ids_table(mine, info_ref).astype(jnp.bfloat16)
        big_ref[by, cap_big:, LANES:] = jnp.zeros((16, feature - LANES), jnp.bfloat16)

    for fetch in fetches[1:]:
        fetch.wait()
    projected = jnp.dot(pooled_ref[...], weight_ref[...], preferred_element_type=jnp.float32)
    squares = jnp.sum(projected * projected, axis=1, keepdims=True)
    rows_ref[...] = (projected * lax.rsqrt(squares + 1e-06)).astype(jnp.bfloat16)
    picked = picked_rows(rows_ref, big_slot, 0, shards * cap_big)
    for by, out in enumerate(big_hbm):
        big_ref[by, 0:cap_big, :] = picked[by * cap_big:(by + 1) * cap_big, :]
        sends.append(pltpu.make_async_copy(big_ref.at[by], out, big_sems.at[by]))
        sends[-1].start()

    slabs = feature // LANES
    group = devices // small_sems.shape[0]
    for part in range(small_sems.shape[0]):
        first = part * group
        picked = picked_rows(rows_ref, small_slot, first * cap_small, group * cap_small)
        for device in range(group):
            for slab in range(slabs):
                small_ref[first + device, slab * cap_small:(slab + 1) * cap_small, :] = picked[
                    device * cap_small:(device + 1) * cap_small, slab * LANES:(slab + 1) * LANES]
            small_ref[first + device, slabs * cap_small:, :] = jnp.broadcast_to(
                ids[first + device:first + device + 1, :], (8, LANES)).astype(jnp.bfloat16)
        sends.append(pltpu.make_async_copy(
            small_ref.at[pl.ds(first, group)], small_hbm.at[pl.ds(first, group)], small_sems.at[part]))
        sends[-1].start()
    for send in sends:
        send.wait()


def ids_table(mine, info_ref):
    docs = info_ref.shape[1]
    quota = info_ref[2:3, :].astype(jnp.float32)
    lanes = (iota((LANES, docs), 0) == info_ref[1:2, :]).astype(jnp.float32).astype(jnp.bfloat16)
    return dot_nt(jnp.where(mine, quota, 0.0).astype(jnp.bfloat16), lanes)


def group_kernel(cap_big, *refs):
    held, group_ref = refs[:-1], refs[-1]
    total = len(held) * cap_big
    spare = group_ref.shape[0] - total
    own = jnp.zeros((spare, LANES), jnp.float32)
    for shift, ref in enumerate(held):
        group_ref[shift * cap_big:(shift + 1) * cap_big, :] = ref[0:cap_big, :]
        table = ref[cap_big:, 0:LANES].astype(jnp.float32)
        own = jnp.where(iota(own.shape, 0) == shift, table[0:1, :], own)
    group_ref[total:, 0:LANES] = own.astype(jnp.bfloat16)
    group_ref[total:, LANES:] = jnp.zeros((spare, group_ref.shape[1] - LANES), jnp.bfloat16)


def turn(tables, at, count, outs):
    for step, out in enumerate(outs):
        to = modulo(at + step, count)
        out[...] = jnp.zeros(out.shape, jnp.float32)
        for place, table in enumerate(tables):
            out[place:place + 1, :] = jnp.sum(
                jnp.where(iota(table.shape, 0) == to, table, 0.0), axis=0, keepdims=True)


def turn_kernel(count, at_ref, *refs):
    held, outs = refs[:-count], refs[-count:]
    turn([ref[...] for ref in held], at_ref[0], count, outs)


def rows_up(count, to=8):
    return -(-count // to) * to


def small_sources(total, blocks, cap_small):
    at = iota((1, total), 1)
    source = at // cap_small
    return source // blocks, modulo(source, blocks), lax.rem(at, jnp.int32(cap_small))


def big_steps(blocks):
    return [0] + list(range(2, blocks)) + ([1] if blocks > 1 else [])


def big_sources(total, shards, cap_big, cap_small):
    at = iota((1, total), 1)
    return (at // (shards * cap_big), modulo(at // cap_big, shards),
            cap_small + lax.rem(at, jnp.int32(cap_big)))


def big_ids(held, sources):
    part, shift, lane = sources
    spare = held[0].shape[0] - part.shape[1] // len(held)
    values = jnp.concatenate([ref[ref.shape[0] - spare:, 0:LANES] for ref in held], axis=0)
    return ids_from(values, part * spare + shift, lane)


def big_pairs(held, row_ids, col_ids, bests, pairs):
    size = row_ids.shape[1] // len(held)
    for row, col in pairs:
        same = 0 if row == col else None
        bests[col] = jnp.maximum(bests[col], block_best(
            held[row][0:size, :], col_ids[row * size:(row + 1) * size], same,
            held[col][0:size, :], row_ids[:, col * size:(col + 1) * size], same))
    return bests


def ids_from(values, row, lane):
    pick = (iota((LANES, lane.shape[1]), 0) == lane).astype(jnp.float32).astype(jnp.bfloat16)
    found = jnp.dot(values, pick, preferred_element_type=jnp.float32)
    return jnp.sum(jnp.where(iota(found.shape, 0) == row, found, 0.0), axis=0, keepdims=True)


def as_column(row):
    return jnp.broadcast_to(row, (8, row.shape[1])).T[:, 0:1]


def block_best(queries, col_ids, first_row, others, row_ids, first_col):
    scores = dot_nt(queries, others)
    allowed = (col_ids == row_ids) & (row_ids > 0.0)
    if first_row is not None:
        allowed &= (iota(scores.shape, 0) + first_row) != (iota(scores.shape, 1) + first_col)
    return jnp.max(jnp.where(allowed, scores, -1.0), axis=0, keepdims=True)


def spread(best, row, lane, rows):
    total = best.shape[1]
    mine = jnp.where(iota((rows, total), 0) == row, best, 0.0)
    place = (iota((LANES, total), 0) == lane).astype(jnp.float32).astype(jnp.bfloat16)
    found = dot_nt(thirds(mine), place)
    return found[:rows] + found[rows:2 * rows] + found[2 * rows:]


def thirds(values):
    high = values.astype(jnp.bfloat16)
    rest = values - high.astype(jnp.float32)
    middle = rest.astype(jnp.bfloat16)
    low = (rest - middle.astype(jnp.float32)).astype(jnp.bfloat16)
    return jnp.concatenate([high, middle, low], axis=0)


def big_kernel(shards, cap_big, cap_small, *refs):
    held, best_ref = refs[:-1], refs[-1]
    size = shards * cap_big
    row_ids = big_ids(held, big_sources(len(held) * size, shards, cap_big, cap_small))
    col_ids = as_column(row_ids)
    pairs = [(row, col) for row in range(len(held)) for col in range(len(held))]
    bests = big_pairs(held, row_ids, col_ids, [jnp.full((1, size), -1.0, jnp.float32)] * len(held), pairs)
    best_ref[...] = jnp.concatenate(bests, axis=1)


def big_last_kernel(shards, blocks, cap_big, cap_small, docs_at, small_ref, best_ref, *refs):
    held, back_refs = refs[:blocks], refs[blocks:]
    size = shards * cap_big
    high = back_refs[0].shape[0]
    part, shift, lane = big_sources(blocks * size, shards, cap_big, cap_small)
    row_ids = big_ids(held, (part, shift, lane))
    col_ids = as_column(row_ids)
    last = blocks - 1
    pairs = [(row, last) for row in range(blocks)] + [(last, col) for col in range(last)]
    bests = [best_ref[:, col * size:(col + 1) * size] for col in range(last)]
    bests = big_pairs(held, row_ids, col_ids, bests + [jnp.full((1, size), -1.0, jnp.float32)], pairs)
    docs = modulo(docs_at[0] + shards - shift, shards)
    step = jnp.where(part == 0, 0, jnp.where(part == last, 1, part + 1))
    back = small_ref[...] + spread(jnp.concatenate(bests, axis=1), step * high + docs, lane, small_ref.shape[0])
    for at, ref in enumerate(back_refs):
        ref[...] = back[at * high:(at + 1) * high, :]


def small_kernel(shards, blocks, cap_small, blk_at, got_ref, back_ref, rows_ref):
    total, feature = rows_ref.shape
    high = back_ref.shape[0] // blocks
    slabs = feature // LANES
    values = []
    for device in range(got_ref.shape[0]):
        for slab in range(slabs):
            rows_ref[device * cap_small:(device + 1) * cap_small, slab * LANES:(slab + 1) * LANES] = got_ref[
                device, slab * cap_small:(slab + 1) * cap_small, :]
        values.append(got_ref[device, slabs * cap_small:, :].astype(jnp.float32)[0:1, :])
    docs, blk, lane = small_sources(total, blocks, cap_small)
    row_ids = ids_from(jnp.concatenate(values, axis=0).astype(jnp.bfloat16), docs * blocks + blk, lane)
    col_ids = as_column(row_ids)
    tile = tile_of(total)
    best = jnp.full((1, total), -1.0, jnp.float32)
    for at in range(0, total, tile):
        best = jnp.maximum(best, block_best(
            rows_ref[at:at + tile, :], col_ids[at:at + tile], at, rows_ref[...], row_ids, 0))
    row = modulo(blk + blocks - blk_at[0], blocks) * high + docs
    back_ref[...] = spread(best, row, lane, back_ref.shape[0])


def masks_kernel(shards, blocks, docs_at, blk_at, info_ref, row_ref, lane_ref):
    device = info_ref[0:1, :]
    high = row_ref.shape[0] // (3 * shards)
    row = (modulo(docs_at[0] + shards - device // blocks, shards) * high
           + modulo(blk_at[0] + blocks - modulo(device, blocks), blocks))
    mask = (iota((shards * high, row_ref.shape[1]), 0) == row).astype(jnp.float32)
    row_ref[...] = jnp.concatenate([mask] * 3, axis=0).astype(jnp.bfloat16)
    lane_ref[...] = (iota(lane_ref.shape, 0) == info_ref[1:2, :]).astype(jnp.float32)


def finish_kernel(*refs):
    held, (row_ref, lane_ref, out_ref) = refs[:-3], refs[-3:]
    values = thirds(jnp.concatenate([ref[...] for ref in held], axis=0))
    found = lax.dot_general(values, row_ref[...], (((0,), (0,)), ((), ())), preferred_element_type=jnp.float32)
    out_ref[...] = jnp.sum(jnp.where(lane_ref[...] > 0.0, found, 0.0), axis=0, keepdims=True)


def call(kernel, outs, ins, flops, moved, limit=16, scratch=()):
    specs = [pl.BlockSpec(memory_space=space) for _, _, space in outs]
    return pl.pallas_call(
        kernel,
        out_shape=[space(shape, dtype) if space is pltpu.HBM else jax.ShapeDtypeStruct(shape, dtype)
                   for shape, dtype, space in outs],
        in_specs=[pl.BlockSpec(memory_space=space) for space in ins],
        out_specs=specs,
        scratch_shapes=scratch,
        cost_estimate=pl.CostEstimate(flops=flops, bytes_accessed=moved, transcendentals=0),
        compiler_params=pltpu.CompilerParams(vmem_limit_bytes=limit << 20),
    )


def body(pooled, proj_weight, cluster):
    shards = lax.axis_size("docs")
    blocks = lax.axis_size("blk")
    devices = shards * blocks
    docs = pooled.shape[0]
    feature = proj_weight.shape[1]
    big_count = docs // 4
    small_count = docs - big_count
    cap_big = 2 * big_count // shards
    cap_small = rows_up(2 * small_count // devices, 16)
    small_slots = devices * cap_small
    big_slots = shards * cap_big
    big_total = blocks * big_slots
    sizes = (shards, blocks, cap_big, cap_small)
    f32, bf16, i32 = jnp.float32, jnp.bfloat16, jnp.int32
    vmem, hbm, smem, dma = pltpu.VMEM, pltpu.HBM, pltpu.SMEM, pltpu.SemaphoreType.DMA

    docs_at, blk_at = (lax.axis_index(axis).astype(i32).reshape(1) for axis in ("docs", "blk"))

    def along(x, axis, count, by):
        return lax.ppermute(x, axis, [(i, (i + by) % count) for i in range(count)])

    small_rows = feature // LANES * cap_small + 8
    small_sent, info, *big_sent = call(
        functools.partial(sort_kernel, *sizes),
        [((devices, small_rows, LANES), bf16, hbm), ((8, docs), i32, hbm)] + [((cap_big + 16, feature), bf16, hbm)] * shards,
        [smem, hbm, hbm, hbm],
        2 * docs * feature * (pooled.shape[1] + small_slots), 4 << 20, 60,
        [vmem(pooled.shape, bf16), vmem(proj_weight.shape, bf16), vmem((1, docs), i32),
         vmem((devices, small_rows, LANES), bf16), vmem((shards, cap_big + 16, feature), bf16),
         vmem((docs, feature), bf16), vmem((8, docs), i32), dma((4,)), dma((4,)), dma((shards,))],
    )(docs_at, pooled, proj_weight, cluster.reshape(1, docs))

    got_small = lax.all_to_all(small_sent, ("docs", "blk"), split_axis=0, concat_axis=0, tiled=True)

    held = [big_sent[0]] + [along(big_sent[by], "docs", shards, by) for by in range(1, shards)]
    group, = call(
        functools.partial(group_kernel, cap_big),
        [((big_slots + rows_up(shards, 16), feature), bf16, vmem)], [vmem] * shards,
        big_slots * feature, 1 << 30,
    )(*held)
    parts = [group]
    for step in big_steps(blocks)[1:]:
        pairs = [(d * blocks + (home_of(d, blocks) + step) % blocks, d * blocks + home_of(d, blocks))
                 for d in range(shards)]
        parts.append(lax.ppermute(group, ("docs", "blk"), pairs))

    back_small, = call(
        functools.partial(small_kernel, shards, blocks, cap_small),
        [((blocks * rows_up(shards), LANES), f32, vmem)], [smem, vmem],
        2 * small_slots * small_slots * feature, 2 << 20, 16,
        [vmem((small_slots, feature), bf16)],
    )(blk_at, got_small)
    early, = call(
        functools.partial(big_kernel, shards, cap_big, cap_small),
        [((1, big_total - big_slots), f32, vmem)], [vmem] * (blocks - 1),
        2 * (big_total - big_slots) ** 2 * feature, 2 << 20,
    )(*parts[:-1])
    back = call(
        functools.partial(big_last_kernel, *sizes),
        [((rows_up(shards), LANES), f32, vmem)] * blocks, [smem] + [vmem] * (blocks + 2),
        2 * (2 * big_total - big_slots) * big_slots * feature, 2 << 20,
    )(docs_at, back_small, early, *parts)
    back = [back[0]] + [along(back[by], "blk", blocks, by) for by in range(1, blocks)]
    back = call(
        functools.partial(turn_kernel, shards),
        [((rows_up(blocks), LANES), f32, vmem)] * shards, [smem] + [vmem] * blocks,
        shards * blocks * LANES, 1 << 16,
    )(docs_at, *back)
    back = [back[0]] + [along(back[by], "docs", shards, by) for by in range(1, shards)]

    masks = call(
        functools.partial(masks_kernel, shards, blocks),
        [((3 * shards * rows_up(blocks), docs), bf16, vmem), ((LANES, docs), f32, vmem)], [smem, smem, vmem],
        docs * LANES, 1 << 18,
    )(docs_at, blk_at, info)
    out, = call(
        finish_kernel, [((1, docs), f32, vmem)], [vmem] * (shards + 2),
        6 * docs * LANES * devices, 1 << 18,
    )(*back, *masks)
    return out.reshape(docs)


def solution(mesh):
    in_specs = (P(("slab", "docs", "blk"), None), P(), P(("slab", "docs", "blk")))
    out_specs = P(("slab", "docs", "blk"))
    return jax.shard_map(body, mesh=mesh, in_specs=in_specs, out_specs=out_specs, check_vma=False)
```

```python
import functools

import jax
import jax.numpy as jnp
from jax import lax
from jax.experimental import pallas as pl
from jax.experimental.pallas import tpu as pltpu
from jax.sharding import PartitionSpec as P

BIG_OWN = 4
LANES = 128


def modulo(x, n):
    return x & (n - 1) if n & (n - 1) == 0 else lax.rem(x, jnp.int32(n))


def quotient(x, n):
    if n & (n - 1) == 0:
        return lax.shift_right_logical(x, jnp.int32(n.bit_length() - 1))
    return lax.div(x, jnp.int32(n))


def iota(shape, axis):
    return lax.broadcasted_iota(jnp.int32, shape, axis)


def dot_nt(a, b):
    return lax.dot_general(a, b, (((1,), (1,)), ((), ())), preferred_element_type=jnp.float32)


def tile_of(rows, most=256):
    tile = most
    while rows % tile:
        tile //= 2
    return tile


def home_of(docs, blocks):
    return max(blocks // 2 - 1, 0) + (docs & min(blocks - 1, 1))


def picked_rows(rows_ref, slot, first, count):
    pick = (iota((count, rows_ref.shape[0]), 0) + first == slot).astype(jnp.float32).astype(jnp.bfloat16)
    return jnp.dot(pick, rows_ref[...], preferred_element_type=jnp.float32).astype(jnp.bfloat16)


def sort_kernel(shards, blocks, cap_big, cap_small, docs_at, pooled_hbm, weight_hbm, cluster_hbm, small_hbm, info_hbm,
                *refs):
    big_hbm = refs[:shards]
    (pooled_ref, weight_ref, cluster_ref, small_ref, big_ref, rows_ref, info_ref, sems, small_sems,
     big_sems) = refs[shards:]
    docs, feature = rows_ref.shape
    devices = shards * blocks
    limit = BIG_OWN * shards
    buckets = devices + shards

    fetches = [pltpu.make_async_copy(source, target, sems.at[n]) for n, (source, target) in enumerate(
        ((cluster_hbm, cluster_ref), (weight_hbm, weight_ref), (pooled_hbm, pooled_ref)))]
    for fetch in fetches:
        fetch.start()
    earlier = (iota((docs, docs), 0) < iota((docs, docs), 1)).astype(jnp.float32).astype(jnp.bfloat16)
    for fetch in fetches:
        fetch.wait()

    cluster = cluster_ref[...]
    is_big = cluster < limit
    owner = modulo(cluster, shards)
    past = jnp.maximum(cluster - limit, 0)
    target = modulo(past, devices)
    bucket = jnp.where(is_big, devices + owner, target)

    padded = -(-buckets // 16) * 16
    hot = (iota((padded, docs), 0) == bucket).astype(jnp.float32)
    before = jnp.dot(hot.astype(jnp.bfloat16), earlier, preferred_element_type=jnp.float32)
    rank = jnp.sum(before * hot, axis=0, keepdims=True).astype(jnp.int32)

    info_ref[0:1, :] = jnp.where(is_big, owner * blocks + home_of(owner, blocks), target)
    info_ref[1:2, :] = jnp.where(is_big, cap_small + rank, rank)
    info_ref[2:3, :] = jnp.where(is_big, quotient(cluster, shards), quotient(past, devices)) + 1
    info_ref[3:8, :] = jnp.zeros((5, docs), jnp.int32)
    sends = [pltpu.make_async_copy(info_ref, info_hbm, sems.at[3])]
    sends[0].start()
    small_slot = jnp.where(is_big, -1, target * cap_small + rank)
    quota = info_ref[2:3, :].astype(jnp.float32)
    lanes = (iota((LANES, docs), 0) == info_ref[1:2, :]).astype(jnp.float32).astype(jnp.bfloat16)

    def ids_table(mine):
        return dot_nt(jnp.where(mine, quota, 0.0).astype(jnp.bfloat16), lanes)

    ids = ids_table(iota((devices, docs), 0) == bucket)
    slabs = feature // LANES
    shift = modulo(owner + shards - docs_at[0], shards)
    big_slot = jnp.where(is_big, shift * cap_big + rank, -1)
    for by in range(shards):
        mine = (iota((16, docs), 0) == 0) & is_big & (shift == by)
        big_ref[by, slabs * cap_big:, :] = ids_table(mine).astype(jnp.bfloat16)

    projected = jnp.dot(pooled_ref[...], weight_ref[...], preferred_element_type=jnp.float32)
    squares = jnp.sum(projected * projected, axis=1, keepdims=True)
    rows_ref[...] = (projected * lax.rsqrt(squares + 1e-06)).astype(jnp.bfloat16)
    picked = picked_rows(rows_ref, big_slot, 0, shards * cap_big)
    for by, out in enumerate(big_hbm):
        for slab in range(slabs):
            big_ref[by, slab * cap_big:(slab + 1) * cap_big, :] = picked[
                by * cap_big:(by + 1) * cap_big, slab * LANES:(slab + 1) * LANES]
        sends.append(pltpu.make_async_copy(big_ref.at[by], out, big_sems.at[by]))
        sends[-1].start()

    group = devices // small_sems.shape[0]
    for part in range(small_sems.shape[0]):
        first = part * group
        picked = picked_rows(rows_ref, small_slot, first * cap_small, group * cap_small)
        for device in range(group):
            for slab in range(slabs):
                small_ref[first + device, slab * cap_small:(slab + 1) * cap_small, :] = picked[
                    device * cap_small:(device + 1) * cap_small, slab * LANES:(slab + 1) * LANES]
            small_ref[first + device, slabs * cap_small:, :] = jnp.broadcast_to(
                ids[first + device:first + device + 1, :], (8, LANES)).astype(jnp.bfloat16)
        sends.append(pltpu.make_async_copy(
            small_ref.at[pl.ds(first, group)], small_hbm.at[pl.ds(first, group)], small_sems.at[part]))
        sends[-1].start()
    for send in sends:
        send.wait()


def group_kernel(slabs, cap_big, *refs):
    held, group_ref = refs[:-1], refs[-1]
    total = len(held) * cap_big
    spare = group_ref.shape[0] - slabs * total
    own = jnp.zeros((spare, LANES), jnp.float32)
    for shift, ref in enumerate(held):
        for slab in range(slabs):
            at = slab * total + shift * cap_big
            group_ref[at:at + cap_big, :] = ref[slab * cap_big:(slab + 1) * cap_big, :]
        table = ref[slabs * cap_big:, :].astype(jnp.float32)
        own = jnp.where(iota(own.shape, 0) == shift, table[0:1, :], own)
    group_ref[slabs * total:, :] = own.astype(jnp.bfloat16)


def turn(tables, at, count, outs):
    for step, out in enumerate(outs):
        to = modulo(at + step, count)
        out[...] = jnp.zeros(out.shape, jnp.float32)
        for place, table in enumerate(tables):
            out[place:place + 1, :] = jnp.sum(
                jnp.where(iota(table.shape, 0) == to, table, 0.0), axis=0, keepdims=True)


def turn_kernel(count, at_ref, *refs):
    held, outs = refs[:-count], refs[-count:]
    turn([ref[...] for ref in held], at_ref[0], count, outs)


def rows_up(count, to=8):
    return -(-count // to) * to


def small_sources(total, blocks, cap_small):
    at = iota((1, total), 1)
    source = at // cap_small
    return source // blocks, modulo(source, blocks), lax.rem(at, jnp.int32(cap_small))


def big_steps(blocks):
    return [0] + list(range(2, blocks)) + ([1] if blocks > 1 else [])


def big_sources(total, shards, cap_big, cap_small):
    at = iota((1, total), 1)
    return (at // (shards * cap_big), modulo(at // cap_big, shards),
            cap_small + lax.rem(at, jnp.int32(cap_big)))


def big_ids(held, rows, sources):
    part, shift, lane = sources
    spare = held[0].shape[0] - rows
    values = jnp.concatenate([ref[rows:, :] for ref in held], axis=0)
    return ids_from(values, part * spare + shift, lane)


def assemble(held, rows_ref):
    size, slabs = rows_ref.shape[0] // len(held), rows_ref.shape[1] // LANES
    for part, ref in enumerate(held):
        for slab in range(slabs):
            rows_ref[part * size:(part + 1) * size, slab * LANES:(slab + 1) * LANES] = ref[
                slab * size:(slab + 1) * size, :]


def big_pairs(held, row_ids, col_ids, bests, pairs):
    size = row_ids.shape[1] // len(held)
    for row, col in pairs:
        same = 0 if row == col else None
        bests[col] = jnp.maximum(bests[col], block_best(
            held[row][...], col_ids[row * size:(row + 1) * size], same,
            held[col][...], row_ids[:, col * size:(col + 1) * size], same))
    return bests


def ids_from(values, row, lane):
    pick = (iota((LANES, lane.shape[1]), 0) == lane).astype(jnp.float32).astype(jnp.bfloat16)
    found = jnp.dot(values, pick, preferred_element_type=jnp.float32)
    return jnp.sum(jnp.where(iota(found.shape, 0) == row, found, 0.0), axis=0, keepdims=True)


def as_column(row):
    return jnp.broadcast_to(row, (8, row.shape[1])).T[:, 0:1]


def block_best(queries, col_ids, first_row, others, row_ids, first_col):
    scores = dot_nt(queries, others)
    allowed = (col_ids == row_ids) & (row_ids > 0.0)
    if first_row is not None:
        allowed &= (iota(scores.shape, 0) + first_row) != (iota(scores.shape, 1) + first_col)
    return jnp.max(jnp.where(allowed, scores, -1.0), axis=0, keepdims=True)


def spread(best, row, lane, rows):
    total = best.shape[1]
    mine = jnp.where(iota((rows, total), 0) == row, best, 0.0)
    place = (iota((LANES, total), 0) == lane).astype(jnp.float32).astype(jnp.bfloat16)
    found = dot_nt(thirds(mine), place)
    return found[:rows] + found[rows:2 * rows] + found[2 * rows:]


def thirds(values):
    high = values.astype(jnp.bfloat16)
    rest = values - high.astype(jnp.float32)
    middle = rest.astype(jnp.bfloat16)
    low = (rest - middle.astype(jnp.float32)).astype(jnp.bfloat16)
    return jnp.concatenate([high, middle, low], axis=0)


def big_kernel(shards, cap_big, cap_small, *refs):
    held, best_ref, rows_ref = refs[:-2], refs[-2], refs[-1]
    size, slabs = shards * cap_big, rows_ref.shape[1] // LANES
    assemble(held, rows_ref)
    row_ids = big_ids(held, slabs * size, big_sources(len(held) * size, shards, cap_big, cap_small))
    col_ids = as_column(row_ids)
    rows = [rows_ref.at[pl.ds(part * size, size)] for part in range(len(held))]
    pairs = [(row, col) for row in range(len(held)) for col in range(len(held))]
    bests = big_pairs(rows, row_ids, col_ids, [jnp.full((1, size), -1.0, jnp.float32)] * len(held), pairs)
    best_ref[...] = jnp.concatenate(bests, axis=1)


def big_last_kernel(shards, blocks, cap_big, cap_small, docs_at, small_ref, best_ref, rows_ref, *refs):
    held, back_refs, last_ref = refs[:blocks], refs[blocks:-1], refs[-1]
    size, slabs = shards * cap_big, rows_ref.shape[1] // LANES
    high = back_refs[0].shape[0]
    last = blocks - 1
    assemble(held[last:], last_ref)
    part, shift, lane = big_sources(blocks * size, shards, cap_big, cap_small)
    row_ids = big_ids(held, slabs * size, (part, shift, lane))
    col_ids = as_column(row_ids)
    rows = [rows_ref.at[pl.ds(at * size, size)] for at in range(last)] + [last_ref]
    pairs = [(row, last) for row in range(blocks)] + [(last, col) for col in range(last)]
    bests = [best_ref[:, col * size:(col + 1) * size] for col in range(last)]
    bests = big_pairs(rows, row_ids, col_ids, bests + [jnp.full((1, size), -1.0, jnp.float32)], pairs)
    docs = modulo(docs_at[0] + shards - shift, shards)
    step = jnp.where(part == 0, 0, jnp.where(part == last, 1, part + 1))
    back = small_ref[...] + spread(jnp.concatenate(bests, axis=1), step * high + docs, lane, small_ref.shape[0])
    for at, ref in enumerate(back_refs):
        ref[...] = back[at * high:(at + 1) * high, :]


def small_kernel(shards, blocks, cap_small, blk_at, got_ref, back_ref, rows_ref):
    total, feature = rows_ref.shape
    high = back_ref.shape[0] // blocks
    slabs = feature // LANES
    values = []
    for device in range(got_ref.shape[0]):
        for slab in range(slabs):
            rows_ref[device * cap_small:(device + 1) * cap_small, slab * LANES:(slab + 1) * LANES] = got_ref[
                device, slab * cap_small:(slab + 1) * cap_small, :]
        values.append(got_ref[device, slabs * cap_small:, :].astype(jnp.float32)[0:1, :])
    docs, blk, lane = small_sources(total, blocks, cap_small)
    row_ids = ids_from(jnp.concatenate(values, axis=0).astype(jnp.bfloat16), docs * blocks + blk, lane)
    col_ids = as_column(row_ids)
    tile = tile_of(total)
    best = jnp.full((1, total), -1.0, jnp.float32)
    for at in range(0, total, tile):
        best = jnp.maximum(best, block_best(
            rows_ref[at:at + tile, :], col_ids[at:at + tile], at, rows_ref[...], row_ids, 0))
    row = modulo(blk + blocks - blk_at[0], blocks) * high + docs
    back_ref[...] = spread(best, row, lane, back_ref.shape[0])


def masks_kernel(shards, blocks, docs_at, blk_at, info_ref, row_ref, lane_ref):
    device = info_ref[0:1, :]
    high = row_ref.shape[0] // (3 * shards)
    row = (modulo(docs_at[0] + shards - device // blocks, shards) * high
           + modulo(blk_at[0] + blocks - modulo(device, blocks), blocks))
    mask = (iota((shards * high, row_ref.shape[1]), 0) == row).astype(jnp.float32)
    row_ref[...] = jnp.concatenate([mask] * 3, axis=0).astype(jnp.bfloat16)
    lane_ref[...] = (iota(lane_ref.shape, 0) == info_ref[1:2, :]).astype(jnp.float32)


def finish_kernel(*refs):
    held, (row_ref, lane_ref, out_ref) = refs[:-3], refs[-3:]
    values = thirds(jnp.concatenate([ref[...] for ref in held], axis=0))
    found = lax.dot_general(values, row_ref[...], (((0,), (0,)), ((), ())), preferred_element_type=jnp.float32)
    out_ref[...] = jnp.sum(jnp.where(lane_ref[...] > 0.0, found, 0.0), axis=0, keepdims=True)


def call(kernel, outs, ins, flops, moved, limit=16, scratch=()):
    specs = [pl.BlockSpec(memory_space=space) for _, _, space in outs]
    return pl.pallas_call(
        kernel,
        out_shape=[space(shape, dtype) if space is pltpu.HBM else jax.ShapeDtypeStruct(shape, dtype)
                   for shape, dtype, space in outs],
        in_specs=[pl.BlockSpec(memory_space=space) for space in ins],
        out_specs=specs,
        scratch_shapes=scratch,
        cost_estimate=pl.CostEstimate(flops=flops, bytes_accessed=moved, transcendentals=0),
        compiler_params=pltpu.CompilerParams(vmem_limit_bytes=limit << 20),
    )


def body(pooled, proj_weight, cluster):
    shards = lax.axis_size("docs")
    blocks = lax.axis_size("blk")
    devices = shards * blocks
    docs = pooled.shape[0]
    feature = proj_weight.shape[1]
    big_count = docs // 4
    small_count = docs - big_count
    cap_big = 2 * big_count // shards
    cap_small = rows_up(2 * small_count // devices, 16)
    small_slots = devices * cap_small
    big_slots = shards * cap_big
    big_total = blocks * big_slots
    sizes = (shards, blocks, cap_big, cap_small)
    f32, bf16, i32 = jnp.float32, jnp.bfloat16, jnp.int32
    vmem, hbm, smem, dma = pltpu.VMEM, pltpu.HBM, pltpu.SMEM, pltpu.SemaphoreType.DMA

    docs_at, blk_at = (lax.axis_index(axis).astype(i32).reshape(1) for axis in ("docs", "blk"))

    def along(x, axis, count, by):
        return lax.ppermute(x, axis, [(i, (i + by) % count) for i in range(count)])

    slabs = feature // LANES
    small_rows = slabs * cap_small + 8
    big_rows = slabs * cap_big + 16
    group_rows = slabs * big_slots + rows_up(shards, 16)
    small_sent, info, *big_sent = call(
        functools.partial(sort_kernel, *sizes),
        [((devices, small_rows, LANES), bf16, hbm), ((8, docs), i32, hbm)] + [((big_rows, LANES), bf16, hbm)] * shards,
        [smem, hbm, hbm, hbm],
        2 * docs * feature * (pooled.shape[1] + small_slots), 4 << 20, 60,
        [vmem(pooled.shape, bf16), vmem(proj_weight.shape, bf16), vmem((1, docs), i32),
         vmem((devices, small_rows, LANES), bf16), vmem((shards, big_rows, LANES), bf16),
         vmem((docs, feature), bf16), vmem((8, docs), i32), dma((4,)), dma((4,)), dma((shards,))],
    )(docs_at, pooled, proj_weight, cluster.reshape(1, docs))

    got_small = lax.all_to_all(small_sent, ("docs", "blk"), split_axis=0, concat_axis=0, tiled=True)

    held = [big_sent[0]] + [along(big_sent[by], "docs", shards, by) for by in range(1, shards)]
    group, = call(
        functools.partial(group_kernel, slabs, cap_big),
        [((group_rows, LANES), bf16, vmem)], [vmem] * shards,
        big_slots * feature, 1 << 20,
    )(*held)
    parts = [group]
    for step in big_steps(blocks)[1:]:
        pairs = [(d * blocks + (home_of(d, blocks) + step) % blocks, d * blocks + home_of(d, blocks))
                 for d in range(shards)]
        parts.append(lax.ppermute(group, ("docs", "blk"), pairs))

    back_small, = call(
        functools.partial(small_kernel, shards, blocks, cap_small),
        [((blocks * rows_up(shards), LANES), f32, vmem)], [smem, vmem],
        2 * small_slots * small_slots * feature, 2 << 20, 16,
        [vmem((small_slots, feature), bf16)],
    )(blk_at, got_small)
    early, early_rows = call(
        functools.partial(big_kernel, shards, cap_big, cap_small),
        [((1, big_total - big_slots), f32, vmem), ((big_total - big_slots, feature), bf16, vmem)],
        [vmem] * (blocks - 1),
        2 * (big_total - big_slots) ** 2 * feature, 2 << 20,
    )(*parts[:-1])
    back = call(
        functools.partial(big_last_kernel, *sizes),
        [((rows_up(shards), LANES), f32, vmem)] * blocks, [smem] + [vmem] * (blocks + 3),
        2 * (2 * big_total - big_slots) * big_slots * feature, 2 << 20, 16,
        [vmem((big_slots, feature), bf16)],
    )(docs_at, back_small, early, early_rows, *parts)
    back = [back[0]] + [along(back[by], "blk", blocks, by) for by in range(1, blocks)]
    back = call(
        functools.partial(turn_kernel, shards),
        [((rows_up(blocks), LANES), f32, vmem)] * shards, [smem] + [vmem] * blocks,
        shards * blocks * LANES, 1 << 16,
    )(docs_at, *back)
    back = [back[0]] + [along(back[by], "docs", shards, by) for by in range(1, shards)]

    masks = call(
        functools.partial(masks_kernel, shards, blocks),
        [((3 * shards * rows_up(blocks), docs), bf16, vmem), ((LANES, docs), f32, vmem)], [smem, smem, vmem],
        docs * LANES, 1 << 18,
    )(docs_at, blk_at, info)
    out, = call(
        finish_kernel, [((1, docs), f32, vmem)], [vmem] * (shards + 2),
        6 * docs * LANES * devices, 1 << 18,
    )(*back, *masks)
    return out.reshape(docs)


def solution(mesh):
    in_specs = (P(("slab", "docs", "blk"), None), P(), P(("slab", "docs", "blk")))
    out_specs = P(("slab", "docs", "blk"))
    return jax.shard_map(body, mesh=mesh, in_specs=in_specs, out_specs=out_specs, check_vma=False)
```

```python
import functools

import jax
import jax.numpy as jnp
from jax import lax
from jax.experimental import pallas as pl
from jax.experimental.pallas import tpu as pltpu
from jax.sharding import PartitionSpec as P

BIG_OWN = 4
LANES = 128


def modulo(x, n):
    return x & (n - 1) if n & (n - 1) == 0 else lax.rem(x, jnp.int32(n))


def quotient(x, n):
    if n & (n - 1) == 0:
        return lax.shift_right_logical(x, jnp.int32(n.bit_length() - 1))
    return lax.div(x, jnp.int32(n))


def iota(shape, axis):
    return lax.broadcasted_iota(jnp.int32, shape, axis)


def dot_nt(a, b):
    return lax.dot_general(a, b, (((1,), (1,)), ((), ())), preferred_element_type=jnp.float32)


def tile_of(rows, most=256):
    tile = most
    while rows % tile:
        tile //= 2
    return tile


def home_of(docs, blocks):
    return max(blocks // 2 - 1, 0) + (docs & min(blocks - 1, 1))


def picked_rows(rows_ref, slot, first, count):
    pick = (iota((count, rows_ref.shape[0]), 0) + first == slot).astype(jnp.float32).astype(jnp.bfloat16)
    return jnp.dot(pick, rows_ref[...], preferred_element_type=jnp.float32).astype(jnp.bfloat16)


def sort_kernel(shards, blocks, cap_big, cap_small, docs_at, pooled_hbm, weight_hbm, cluster_hbm, small_hbm, info_hbm,
                *refs):
    big_hbm = refs[:shards]
    (pooled_ref, weight_ref, cluster_ref, small_ref, big_ref, rows_ref, info_ref, sems, small_sems,
     big_sems) = refs[shards:]
    docs, feature = rows_ref.shape
    devices = shards * blocks
    limit = BIG_OWN * shards
    buckets = devices + shards

    fetches = [pltpu.make_async_copy(source, target, sems.at[n]) for n, (source, target) in enumerate(
        ((cluster_hbm, cluster_ref), (weight_hbm, weight_ref), (pooled_hbm, pooled_ref)))]
    for fetch in fetches:
        fetch.start()
    earlier = (iota((docs, docs), 0) < iota((docs, docs), 1)).astype(jnp.float32).astype(jnp.bfloat16)
    fetches[0].wait()

    cluster = cluster_ref[...]
    is_big = cluster < limit
    owner = modulo(cluster, shards)
    past = jnp.maximum(cluster - limit, 0)
    target = modulo(past, devices)
    bucket = jnp.where(is_big, devices + owner, target)

    padded = -(-buckets // 16) * 16
    hot = (iota((padded, docs), 0) == bucket).astype(jnp.float32)
    before = jnp.dot(hot.astype(jnp.bfloat16), earlier, preferred_element_type=jnp.float32)
    rank = jnp.sum(before * hot, axis=0, keepdims=True).astype(jnp.int32)

    info_ref[0:1, :] = jnp.where(is_big, owner * blocks + home_of(owner, blocks), target)
    info_ref[1:2, :] = jnp.where(is_big, cap_small + rank, rank)
    info_ref[2:3, :] = jnp.where(is_big, quotient(cluster, shards), quotient(past, devices)) + 1
    info_ref[3:8, :] = jnp.zeros((5, docs), jnp.int32)
    sends = [pltpu.make_async_copy(info_ref, info_hbm, sems.at[3])]
    sends[0].start()
    small_slot = jnp.where(is_big, -1, target * cap_small + rank)
    quota = info_ref[2:3, :].astype(jnp.float32)
    lanes = (iota((LANES, docs), 0) == info_ref[1:2, :]).astype(jnp.float32).astype(jnp.bfloat16)

    def ids_table(mine):
        return dot_nt(jnp.where(mine, quota, 0.0).astype(jnp.bfloat16), lanes)

    ids = ids_table(iota((devices, docs), 0) == bucket)
    shift = modulo(owner + shards - docs_at[0], shards)
    big_slot = jnp.where(is_big, shift * cap_big + rank, -1)
    for by in range(shards):
        mine = (iota((16, docs), 0) == 0) & is_big & (shift == by)
        big_ref[by, cap_big:, 0:LANES] = ids_table(mine).astype(jnp.bfloat16)
        big_ref[by, cap_big:, LANES:] = jnp.zeros((16, feature - LANES), jnp.bfloat16)

    for fetch in fetches[1:]:
        fetch.wait()
    projected = jnp.dot(pooled_ref[...], weight_ref[...], preferred_element_type=jnp.float32)
    squares = jnp.sum(projected * projected, axis=1, keepdims=True)
    rows_ref[...] = (projected * lax.rsqrt(squares + 1e-06)).astype(jnp.bfloat16)
    picked = picked_rows(rows_ref, big_slot, 0, shards * cap_big)
    for by, out in enumerate(big_hbm):
        big_ref[by, 0:cap_big, :] = picked[by * cap_big:(by + 1) * cap_big, :]
        sends.append(pltpu.make_async_copy(big_ref.at[by], out, big_sems.at[by]))
        sends[-1].start()

    slabs = feature // LANES
    group = devices // small_sems.shape[0]
    for part in range(small_sems.shape[0]):
        first = part * group
        picked = picked_rows(rows_ref, small_slot, first * cap_small, group * cap_small)
        for device in range(group):
            for slab in range(slabs):
                small_ref[first + device, slab * cap_small:(slab + 1) * cap_small, :] = picked[
                    device * cap_small:(device + 1) * cap_small, slab * LANES:(slab + 1) * LANES]
            small_ref[first + device, slabs * cap_small:, :] = jnp.broadcast_to(
                ids[first + device:first + device + 1, :], (8, LANES)).astype(jnp.bfloat16)
        sends.append(pltpu.make_async_copy(
            small_ref.at[pl.ds(first, group)], small_hbm.at[pl.ds(first, group)], small_sems.at[part]))
        sends[-1].start()
    for send in sends:
        send.wait()


def group_kernel(cap_big, *refs):
    held, group_ref = refs[:-1], refs[-1]
    total = len(held) * cap_big
    spare = group_ref.shape[0] - total
    own = jnp.zeros((spare, LANES), jnp.float32)
    for shift, ref in enumerate(held):
        group_ref[shift * cap_big:(shift + 1) * cap_big, :] = ref[0:cap_big, :]
        table = ref[cap_big:, 0:LANES].astype(jnp.float32)
        own = jnp.where(iota(own.shape, 0) == shift, table[0:1, :], own)
    group_ref[total:, 0:LANES] = own.astype(jnp.bfloat16)
    group_ref[total:, LANES:] = jnp.zeros((spare, group_ref.shape[1] - LANES), jnp.bfloat16)


def halves_of(order, bit):
    return [index for index in order if not index >> bit & 1], [index for index in order if index >> bit & 1]


def halve_kernel(order, bit, kept_ref, moved_ref, *outs):
    half = kept_ref.shape[0]
    for out, rows in zip(outs, halves_of(order, bit)):
        for at, index in enumerate(rows):
            row = order.index(index)
            ref = kept_ref if row < half else moved_ref
            out[at:at + 1, :] = ref[row % half:row % half + 1, :]


def rows_up(count, to=8):
    return -(-count // to) * to


def small_sources(total, blocks, cap_small):
    at = iota((1, total), 1)
    source = at // cap_small
    return source // blocks, modulo(source, blocks), lax.rem(at, jnp.int32(cap_small))


def big_steps(blocks):
    return [0] + list(range(2, blocks)) + ([1] if blocks > 1 else [])


def big_sources(total, shards, cap_big, cap_small):
    at = iota((1, total), 1)
    return (at // (shards * cap_big), modulo(at // cap_big, shards),
            cap_small + lax.rem(at, jnp.int32(cap_big)))


def big_ids(held, sources):
    part, shift, lane = sources
    spare = held[0].shape[0] - part.shape[1] // len(held)
    values = jnp.concatenate([ref[ref.shape[0] - spare:, 0:LANES] for ref in held], axis=0)
    return ids_from(values, part * spare + shift, lane)


def big_pairs(held, row_ids, col_ids, bests, pairs):
    size = row_ids.shape[1] // len(held)
    for row, col in pairs:
        same = 0 if row == col else None
        bests[col] = jnp.maximum(bests[col], block_best(
            held[row][0:size, :], col_ids[row * size:(row + 1) * size], same,
            held[col][0:size, :], row_ids[:, col * size:(col + 1) * size], same))
    return bests


def ids_from(values, row, lane):
    pick = (iota((LANES, lane.shape[1]), 0) == lane).astype(jnp.float32).astype(jnp.bfloat16)
    found = jnp.dot(values, pick, preferred_element_type=jnp.float32)
    return jnp.sum(jnp.where(iota(found.shape, 0) == row, found, 0.0), axis=0, keepdims=True)


def as_column(row):
    return jnp.broadcast_to(row, (8, row.shape[1])).T[:, 0:1]


def block_best(queries, col_ids, first_row, others, row_ids, first_col):
    scores = dot_nt(queries, others)
    allowed = (col_ids == row_ids) & (row_ids > 0.0)
    if first_row is not None:
        allowed &= (iota(scores.shape, 0) + first_row) != (iota(scores.shape, 1) + first_col)
    return jnp.max(jnp.where(allowed, scores, -1.0), axis=0, keepdims=True)


def spread(best, row, lane, rows):
    total = best.shape[1]
    mine = jnp.where(iota((rows, total), 0) == row, best, 0.0)
    place = (iota((LANES, total), 0) == lane).astype(jnp.float32).astype(jnp.bfloat16)
    found = dot_nt(thirds(mine), place)
    return found[:rows] + found[rows:2 * rows] + found[2 * rows:]


def thirds(values):
    high = values.astype(jnp.bfloat16)
    rest = values - high.astype(jnp.float32)
    middle = rest.astype(jnp.bfloat16)
    low = (rest - middle.astype(jnp.float32)).astype(jnp.bfloat16)
    return jnp.concatenate([high, middle, low], axis=0)


def big_kernel(shards, cap_big, cap_small, *refs):
    held, best_ref = refs[:-1], refs[-1]
    size = shards * cap_big
    row_ids = big_ids(held, big_sources(len(held) * size, shards, cap_big, cap_small))
    col_ids = as_column(row_ids)
    pairs = [(row, col) for row in range(len(held)) for col in range(len(held))]
    bests = big_pairs(held, row_ids, col_ids, [jnp.full((1, size), -1.0, jnp.float32)] * len(held), pairs)
    best_ref[...] = jnp.concatenate(bests, axis=1)


def big_last_kernel(shards, blocks, cap_big, cap_small, docs_at, blk_at, small_ref, best_ref, *refs):
    held, (kept_ref, moved_ref) = refs[:blocks], refs[blocks:]
    size = shards * cap_big
    part, shift, lane = big_sources(blocks * size, shards, cap_big, cap_small)
    row_ids = big_ids(held, (part, shift, lane))
    col_ids = as_column(row_ids)
    last = blocks - 1
    pairs = [(row, last) for row in range(blocks)] + [(last, col) for col in range(last)]
    bests = [best_ref[:, col * size:(col + 1) * size] for col in range(last)]
    bests = big_pairs(held, row_ids, col_ids, bests + [jnp.full((1, size), -1.0, jnp.float32)], pairs)
    docs = modulo(docs_at[0] + shards - shift, shards)
    blk = modulo(blk_at[0] + jnp.where(part == 0, 0, jnp.where(part == last, 1, part + 1)), blocks)
    row = (blk ^ blk_at[0]) * shards + (docs ^ docs_at[0])
    back = small_ref[...] + spread(jnp.concatenate(bests, axis=1), row, lane, small_ref.shape[0])
    half = small_ref.shape[0] // 2
    kept_ref[...] = back[:half, :]
    moved_ref[...] = back[half:, :]


def small_kernel(shards, blocks, cap_small, docs_at, blk_at, got_ref, back_ref, rows_ref):
    total, feature = rows_ref.shape
    slabs = feature // LANES
    values = []
    for device in range(got_ref.shape[0]):
        for slab in range(slabs):
            rows_ref[device * cap_small:(device + 1) * cap_small, slab * LANES:(slab + 1) * LANES] = got_ref[
                device, slab * cap_small:(slab + 1) * cap_small, :]
        values.append(got_ref[device, slabs * cap_small:, :].astype(jnp.float32)[0:1, :])
    docs, blk, lane = small_sources(total, blocks, cap_small)
    row_ids = ids_from(jnp.concatenate(values, axis=0).astype(jnp.bfloat16), docs * blocks + blk, lane)
    col_ids = as_column(row_ids)
    tile = tile_of(total)
    best = jnp.full((1, total), -1.0, jnp.float32)
    for at in range(0, total, tile):
        best = jnp.maximum(best, block_best(
            rows_ref[at:at + tile, :], col_ids[at:at + tile], at, rows_ref[...], row_ids, 0))
    row = (blk ^ blk_at[0]) * shards + (docs ^ docs_at[0])
    back_ref[...] = spread(best, row, lane, back_ref.shape[0])


def masks_kernel(shards, blocks, order, docs_at, blk_at, info_ref, row_ref, lane_ref):
    device = info_ref[0:1, :]
    row = (modulo(device, blocks) ^ blk_at[0]) * shards + (device // blocks ^ docs_at[0])
    mask = jnp.concatenate([(row == index).astype(jnp.float32) for index in order], axis=0)
    row_ref[...] = jnp.concatenate([mask] * 3, axis=0).astype(jnp.bfloat16)
    lane_ref[...] = (iota(lane_ref.shape, 0) == info_ref[1:2, :]).astype(jnp.float32)


def finish_kernel(*refs):
    held, (row_ref, lane_ref, out_ref) = refs[:-3], refs[-3:]
    values = thirds(jnp.concatenate([ref[...] for ref in held], axis=0))
    found = lax.dot_general(values, row_ref[...], (((0,), (0,)), ((), ())), preferred_element_type=jnp.float32)
    out_ref[...] = jnp.sum(jnp.where(lane_ref[...] > 0.0, found, 0.0), axis=0, keepdims=True)


def call(kernel, outs, ins, flops, moved, limit=16, scratch=()):
    specs = [pl.BlockSpec(memory_space=space) for _, _, space in outs]
    return pl.pallas_call(
        kernel,
        out_shape=[space(shape, dtype) if space is pltpu.HBM else jax.ShapeDtypeStruct(shape, dtype)
                   for shape, dtype, space in outs],
        in_specs=[pl.BlockSpec(memory_space=space) for space in ins],
        out_specs=specs,
        scratch_shapes=scratch,
        cost_estimate=pl.CostEstimate(flops=flops, bytes_accessed=moved, transcendentals=0),
        compiler_params=pltpu.CompilerParams(vmem_limit_bytes=limit << 20),
    )


def body(pooled, proj_weight, cluster):
    shards = lax.axis_size("docs")
    blocks = lax.axis_size("blk")
    devices = shards * blocks
    docs = pooled.shape[0]
    feature = proj_weight.shape[1]
    big_count = docs // 4
    small_count = docs - big_count
    cap_big = 2 * big_count // shards
    cap_small = rows_up(2 * small_count // devices, 16)
    small_slots = devices * cap_small
    big_slots = shards * cap_big
    big_total = blocks * big_slots
    sizes = (shards, blocks, cap_big, cap_small)
    f32, bf16, i32 = jnp.float32, jnp.bfloat16, jnp.int32
    vmem, hbm, smem, dma = pltpu.VMEM, pltpu.HBM, pltpu.SMEM, pltpu.SemaphoreType.DMA

    docs_at, blk_at = (lax.axis_index(axis).astype(i32).reshape(1) for axis in ("docs", "blk"))

    def along(x, axis, count, by):
        return lax.ppermute(x, axis, [(i, (i + by) % count) for i in range(count)])

    small_rows = feature // LANES * cap_small + 8
    small_sent, info, *big_sent = call(
        functools.partial(sort_kernel, *sizes),
        [((devices, small_rows, LANES), bf16, hbm), ((8, docs), i32, hbm)] + [((cap_big + 16, feature), bf16, hbm)] * shards,
        [smem, hbm, hbm, hbm],
        2 * docs * feature * (pooled.shape[1] + small_slots), 4 << 20, 60,
        [vmem(pooled.shape, bf16), vmem(proj_weight.shape, bf16), vmem((1, docs), i32),
         vmem((devices, small_rows, LANES), bf16), vmem((shards, cap_big + 16, feature), bf16),
         vmem((docs, feature), bf16), vmem((8, docs), i32), dma((4,)), dma((4,)), dma((shards,))],
    )(docs_at, pooled, proj_weight, cluster.reshape(1, docs))

    got_small = lax.all_to_all(small_sent, ("docs", "blk"), split_axis=0, concat_axis=0, tiled=True)

    held = [big_sent[0]] + [along(big_sent[by], "docs", shards, by) for by in range(1, shards)]
    group, = call(
        functools.partial(group_kernel, cap_big),
        [((big_slots + rows_up(shards, 16), feature), bf16, vmem)], [vmem] * shards,
        big_slots * feature, 1 << 20,
    )(*held)
    parts = [group]
    for step in big_steps(blocks)[1:]:
        pairs = [(d * blocks + (home_of(d, blocks) + step) % blocks, d * blocks + home_of(d, blocks))
                 for d in range(shards)]
        parts.append(lax.ppermute(group, ("docs", "blk"), pairs))

    back_small, = call(
        functools.partial(small_kernel, shards, blocks, cap_small),
        [((devices, LANES), f32, vmem)], [smem, smem, vmem],
        2 * small_slots * small_slots * feature, 2 << 20, 16,
        [vmem((small_slots, feature), bf16)],
    )(docs_at, blk_at, got_small)
    early, = call(
        functools.partial(big_kernel, shards, cap_big, cap_small),
        [((1, big_total - big_slots), f32, vmem)], [vmem] * (blocks - 1),
        2 * (big_total - big_slots) ** 2 * feature, 2 << 20,
    )(*parts[:-1])
    back = call(
        functools.partial(big_last_kernel, *sizes),
        [((devices // 2, LANES), f32, vmem)] * 2, [smem, smem] + [vmem] * (blocks + 2),
        2 * (2 * big_total - big_slots) * big_slots * feature, 2 << 20,
    )(docs_at, blk_at, back_small, early, *parts)
    order = list(range(devices))
    for bit in reversed(range(devices.bit_length() - 1)):
        if bit < devices.bit_length() - 2:
            back = call(
                functools.partial(halve_kernel, order, bit),
                [((devices // 2, LANES), f32, vmem)] * 2, [vmem, vmem], devices * LANES, 1 << 14,
            )(*back)
        order = sum(halves_of(order, bit), [])
        far_docs, far_blk = (1 << bit) % shards, (1 << bit) // shards
        pairs = [(d * blocks + b, (d ^ far_docs) * blocks + (b ^ far_blk)) for d in range(shards) for b in range(blocks)]
        back = [back[0], lax.ppermute(back[1], ("docs", "blk"), pairs)]

    masks = call(
        functools.partial(masks_kernel, shards, blocks, order),
        [((3 * devices, docs), bf16, vmem), ((LANES, docs), f32, vmem)], [smem, smem, vmem],
        docs * LANES, 1 << 18,
    )(docs_at, blk_at, info)
    out, = call(
        finish_kernel, [((1, docs), f32, vmem)], [vmem] * 4,
        6 * docs * LANES * devices, 1 << 18,
    )(*back, *masks)
    return out.reshape(docs)


def solution(mesh):
    in_specs = (P(("slab", "docs", "blk"), None), P(), P(("slab", "docs", "blk")))
    out_specs = P(("slab", "docs", "blk"))
    return jax.shard_map(body, mesh=mesh, in_specs=in_specs, out_specs=out_specs, check_vma=False)
```

```python
import functools

import jax
import jax.numpy as jnp
from jax import lax
from jax.experimental import pallas as pl
from jax.experimental.pallas import tpu as pltpu
from jax.sharding import PartitionSpec as P

BIG_OWN = 4
LANES = 128


def modulo(x, n):
    return x & (n - 1) if n & (n - 1) == 0 else lax.rem(x, jnp.int32(n))


def quotient(x, n):
    if n & (n - 1) == 0:
        return lax.shift_right_logical(x, jnp.int32(n.bit_length() - 1))
    return lax.div(x, jnp.int32(n))


def iota(shape, axis):
    return lax.broadcasted_iota(jnp.int32, shape, axis)


def dot_nt(a, b):
    return lax.dot_general(a, b, (((1,), (1,)), ((), ())), preferred_element_type=jnp.float32)


def tile_of(rows, most=256):
    tile = most
    while rows % tile:
        tile //= 2
    return tile


def home_of(docs, blocks):
    return max(blocks // 2 - 1, 0) + (docs & min(blocks - 1, 1))


def picked_rows(rows_ref, slot, first, count):
    pick = (iota((count, rows_ref.shape[0]), 0) + first == slot).astype(jnp.float32).astype(jnp.bfloat16)
    return jnp.dot(pick, rows_ref[...], preferred_element_type=jnp.float32).astype(jnp.bfloat16)


def sort_kernel(shards, blocks, cap_big, cap_small, docs_at, pooled_hbm, weight_hbm, cluster_hbm, small_hbm, info_hbm,
                *refs):
    big_hbm = refs[:shards]
    (pooled_ref, weight_ref, cluster_ref, small_ref, big_ref, rows_ref, info_ref, sems, small_sems,
     big_sems) = refs[shards:]
    docs, feature = rows_ref.shape
    devices = shards * blocks
    limit = BIG_OWN * shards
    buckets = devices + shards

    fetches = [pltpu.make_async_copy(source, target, sems.at[n]) for n, (source, target) in enumerate(
        ((cluster_hbm, cluster_ref), (weight_hbm, weight_ref), (pooled_hbm, pooled_ref)))]
    for fetch in fetches:
        fetch.start()
    fetches[0].wait()

    cluster = cluster_ref[...]
    is_big = cluster < limit
    owner = modulo(cluster, shards)
    past = jnp.maximum(cluster - limit, 0)
    target = modulo(past, devices)
    bucket = jnp.where(is_big, devices + owner, target)

    padded = -(-buckets // 16) * 16
    hot = (iota((padded, docs), 0) == bucket).astype(jnp.float32)
    earlier = (iota((docs, docs), 0) < iota((docs, docs), 1)).astype(jnp.float32).astype(jnp.bfloat16)
    before = jnp.dot(hot.astype(jnp.bfloat16), earlier, preferred_element_type=jnp.float32)
    rank = jnp.sum(before * hot, axis=0, keepdims=True).astype(jnp.int32)

    info_ref[0:1, :] = jnp.where(is_big, owner * blocks + home_of(owner, blocks), target)
    info_ref[1:2, :] = jnp.where(is_big, cap_small + rank, rank)
    info_ref[2:3, :] = jnp.where(is_big, quotient(cluster, shards), quotient(past, devices)) + 1
    info_ref[3:8, :] = jnp.zeros((5, docs), jnp.int32)
    sends = [pltpu.make_async_copy(info_ref, info_hbm, sems.at[3])]
    sends[0].start()
    small_slot = jnp.where(is_big, -1, target * cap_small + rank)
    ids = ids_table(iota((devices, docs), 0) == bucket, info_ref)
    shift = modulo(owner + shards - docs_at[0], shards)
    big_slot = jnp.where(is_big, shift * cap_big + rank, -1)
    for by in range(shards):
        mine = (iota((16, docs), 0) == 0) & is_big & (shift == by)
        big_ref[by, cap_big:, 0:LANES] = ids_table(mine, info_ref).astype(jnp.bfloat16)
        big_ref[by, cap_big:, LANES:] = jnp.zeros((16, feature - LANES), jnp.bfloat16)

    for fetch in fetches[1:]:
        fetch.wait()
    projected = jnp.dot(pooled_ref[...], weight_ref[...], preferred_element_type=jnp.float32)
    squares = jnp.sum(projected * projected, axis=1, keepdims=True)
    rows_ref[...] = (projected * lax.rsqrt(squares + 1e-06)).astype(jnp.bfloat16)
    picked = picked_rows(rows_ref, big_slot, 0, shards * cap_big)
    for by, out in enumerate(big_hbm):
        big_ref[by, 0:cap_big, :] = picked[by * cap_big:(by + 1) * cap_big, :]
        sends.append(pltpu.make_async_copy(big_ref.at[by], out, big_sems.at[by]))
        sends[-1].start()

    slabs = feature // LANES
    group = devices // small_sems.shape[0]
    for part in range(small_sems.shape[0]):
        first = part * group
        picked = picked_rows(rows_ref, small_slot, first * cap_small, group * cap_small)
        for device in range(group):
            for slab in range(slabs):
                small_ref[first + device, slab * cap_small:(slab + 1) * cap_small, :] = picked[
                    device * cap_small:(device + 1) * cap_small, slab * LANES:(slab + 1) * LANES]
            small_ref[first + device, slabs * cap_small:, :] = jnp.broadcast_to(
                ids[first + device:first + device + 1, :], (8, LANES)).astype(jnp.bfloat16)
        sends.append(pltpu.make_async_copy(
            small_ref.at[pl.ds(first, group)], small_hbm.at[pl.ds(first, group)], small_sems.at[part]))
        sends[-1].start()
    for send in sends:
        send.wait()


def ids_table(mine, info_ref):
    docs = info_ref.shape[1]
    quota = info_ref[2:3, :].astype(jnp.float32)
    lanes = (iota((LANES, docs), 0) == info_ref[1:2, :]).astype(jnp.float32).astype(jnp.bfloat16)
    return dot_nt(jnp.where(mine, quota, 0.0).astype(jnp.bfloat16), lanes)


def group_kernel(cap_big, *refs):
    held, group_ref = refs[:-1], refs[-1]
    total = len(held) * cap_big
    spare = group_ref.shape[0] - total
    own = jnp.zeros((spare, LANES), jnp.float32)
    for shift, ref in enumerate(held):
        group_ref[shift * cap_big:(shift + 1) * cap_big, :] = ref[0:cap_big, :]
        table = ref[cap_big:, 0:LANES].astype(jnp.float32)
        own = jnp.where(iota(own.shape, 0) == shift, table[0:1, :], own)
    group_ref[total:, 0:LANES] = own.astype(jnp.bfloat16)
    group_ref[total:, LANES:] = jnp.zeros((spare, group_ref.shape[1] - LANES), jnp.bfloat16)


def turn(tables, at, count, outs):
    for step, out in enumerate(outs):
        to = modulo(at + step, count)
        out[...] = jnp.zeros(out.shape, jnp.float32)
        for place, table in enumerate(tables):
            out[place:place + 1, :] = jnp.sum(
                jnp.where(iota(table.shape, 0) == to, table, 0.0), axis=0, keepdims=True)


def turn_kernel(count, at_ref, *refs):
    held, outs = refs[:-count], refs[-count:]
    turn([ref[...] for ref in held], at_ref[0], count, outs)


def rows_up(count, to=8):
    return -(-count // to) * to


def small_sources(total, blocks, cap_small):
    at = iota((1, total), 1)
    source = at // cap_small
    return source // blocks, modulo(source, blocks), lax.rem(at, jnp.int32(cap_small))


def big_steps(blocks):
    return [0] + list(range(2, blocks)) + ([1] if blocks > 1 else [])


def big_sources(total, shards, cap_big, cap_small):
    at = iota((1, total), 1)
    return (at // (shards * cap_big), modulo(at // cap_big, shards),
            cap_small + lax.rem(at, jnp.int32(cap_big)))


def big_ids(held, sources):
    part, shift, lane = sources
    spare = held[0].shape[0] - part.shape[1] // len(held)
    values = jnp.concatenate([ref[ref.shape[0] - spare:, 0:LANES] for ref in held], axis=0)
    return ids_from(values, part * spare + shift, lane)


def big_pairs(held, row_ids, col_ids, bests, pairs):
    size = row_ids.shape[1] // len(held)
    for row, col in pairs:
        same = 0 if row == col else None
        bests[col] = jnp.maximum(bests[col], block_best(
            held[row][0:size, :], col_ids[row * size:(row + 1) * size], same,
            held[col][0:size, :], row_ids[:, col * size:(col + 1) * size], same))
    return bests


def ids_from(values, row, lane):
    pick = (iota((LANES, lane.shape[1]), 0) == lane).astype(jnp.float32).astype(jnp.bfloat16)
    found = jnp.dot(values, pick, preferred_element_type=jnp.float32)
    return jnp.sum(jnp.where(iota(found.shape, 0) == row, found, 0.0), axis=0, keepdims=True)


def as_column(row):
    return jnp.broadcast_to(row, (8, row.shape[1])).T[:, 0:1]


def block_best(queries, col_ids, first_row, others, row_ids, first_col):
    scores = dot_nt(queries, others)
    allowed = (col_ids == row_ids) & (row_ids > 0.0)
    if first_row is not None:
        allowed &= (iota(scores.shape, 0) + first_row) != (iota(scores.shape, 1) + first_col)
    return jnp.max(jnp.where(allowed, scores, -1.0), axis=0, keepdims=True)


def spread(best, row, lane, rows):
    total = best.shape[1]
    mine = jnp.where(iota((rows, total), 0) == row, best, 0.0)
    place = (iota((LANES, total), 0) == lane).astype(jnp.float32).astype(jnp.bfloat16)
    found = dot_nt(thirds(mine), place)
    return found[:rows] + found[rows:2 * rows] + found[2 * rows:]


def thirds(values):
    high = values.astype(jnp.bfloat16)
    rest = values - high.astype(jnp.float32)
    middle = rest.astype(jnp.bfloat16)
    low = (rest - middle.astype(jnp.float32)).astype(jnp.bfloat16)
    return jnp.concatenate([high, middle, low], axis=0)


def big_kernel(shards, cap_big, cap_small, *refs):
    held, best_ref = refs[:-1], refs[-1]
    size = shards * cap_big
    row_ids = big_ids(held, big_sources(len(held) * size, shards, cap_big, cap_small))
    col_ids = as_column(row_ids)
    pairs = [(row, col) for row in range(len(held)) for col in range(len(held))]
    bests = big_pairs(held, row_ids, col_ids, [jnp.full((1, size), -1.0, jnp.float32)] * len(held), pairs)
    best_ref[...] = jnp.concatenate(bests, axis=1)


def big_last_kernel(shards, blocks, cap_big, cap_small, docs_at, small_ref, best_ref, *refs):
    held, back_refs = refs[:blocks], refs[blocks:]
    size = shards * cap_big
    high = back_refs[0].shape[0]
    part, shift, lane = big_sources(blocks * size, shards, cap_big, cap_small)
    row_ids = big_ids(held, (part, shift, lane))
    col_ids = as_column(row_ids)
    last = blocks - 1
    pairs = [(row, last) for row in range(blocks)] + [(last, col) for col in range(last)]
    bests = [best_ref[:, col * size:(col + 1) * size] for col in range(last)]
    bests = big_pairs(held, row_ids, col_ids, bests + [jnp.full((1, size), -1.0, jnp.float32)], pairs)
    docs = modulo(docs_at[0] + shards - shift, shards)
    step = jnp.where(part == 0, 0, jnp.where(part == last, 1, part + 1))
    back = small_ref[...] + spread(jnp.concatenate(bests, axis=1), step * high + docs, lane, small_ref.shape[0])
    for at, ref in enumerate(back_refs):
        ref[...] = back[at * high:(at + 1) * high, :]


def small_kernel(shards, blocks, cap_small, blk_at, got_ref, back_ref, rows_ref):
    total, feature = rows_ref.shape
    high = back_ref.shape[0] // blocks
    slabs = feature // LANES
    values = []
    for device in range(got_ref.shape[0]):
        for slab in range(slabs):
            rows_ref[device * cap_small:(device + 1) * cap_small, slab * LANES:(slab + 1) * LANES] = got_ref[
                device, slab * cap_small:(slab + 1) * cap_small, :]
        values.append(got_ref[device, slabs * cap_small:, :].astype(jnp.float32)[0:1, :])
    docs, blk, lane = small_sources(total, blocks, cap_small)
    row_ids = ids_from(jnp.concatenate(values, axis=0).astype(jnp.bfloat16), docs * blocks + blk, lane)
    col_ids = as_column(row_ids)
    tile = tile_of(total)
    best = jnp.full((1, total), -1.0, jnp.float32)
    for at in range(0, total, tile):
        best = jnp.maximum(best, block_best(
            rows_ref[at:at + tile, :], col_ids[at:at + tile], at, rows_ref[...], row_ids, 0))
    row = modulo(blk + blocks - blk_at[0], blocks) * high + docs
    back_ref[...] = spread(best, row, lane, back_ref.shape[0])


def masks_kernel(shards, blocks, docs_at, blk_at, info_ref, row_ref, lane_ref):
    device = info_ref[0:1, :]
    high = row_ref.shape[0] // (3 * shards)
    row = (modulo(docs_at[0] + shards - device // blocks, shards) * high
           + modulo(blk_at[0] + blocks - modulo(device, blocks), blocks))
    mask = (iota((shards * high, row_ref.shape[1]), 0) == row).astype(jnp.float32)
    row_ref[...] = jnp.concatenate([mask] * 3, axis=0).astype(jnp.bfloat16)
    lane_ref[...] = (iota(lane_ref.shape, 0) == info_ref[1:2, :]).astype(jnp.float32)


def finish_kernel(*refs):
    held, (row_ref, lane_ref, out_ref) = refs[:-3], refs[-3:]
    values = thirds(jnp.concatenate([ref[...] for ref in held], axis=0))
    found = lax.dot_general(values, row_ref[...], (((0,), (0,)), ((), ())), preferred_element_type=jnp.float32)
    out_ref[...] = jnp.sum(jnp.where(lane_ref[...] > 0.0, found, 0.0), axis=0, keepdims=True)


def call(kernel, outs, ins, flops, moved, limit=16, scratch=()):
    specs = [pl.BlockSpec(memory_space=space) for _, _, space in outs]
    return pl.pallas_call(
        kernel,
        out_shape=[space(shape, dtype) if space is pltpu.HBM else jax.ShapeDtypeStruct(shape, dtype)
                   for shape, dtype, space in outs],
        in_specs=[pl.BlockSpec(memory_space=space) for space in ins],
        out_specs=specs,
        scratch_shapes=scratch,
        cost_estimate=pl.CostEstimate(flops=flops, bytes_accessed=moved, transcendentals=0),
        compiler_params=pltpu.CompilerParams(vmem_limit_bytes=limit << 20),
    )


def body(pooled, proj_weight, cluster):
    shards = lax.axis_size("docs")
    blocks = lax.axis_size("blk")
    devices = shards * blocks
    docs = pooled.shape[0]
    feature = proj_weight.shape[1]
    big_count = docs // 4
    small_count = docs - big_count
    cap_big = 2 * big_count // shards
    cap_small = rows_up(2 * small_count // devices, 16)
    small_slots = devices * cap_small
    big_slots = shards * cap_big
    big_total = blocks * big_slots
    sizes = (shards, blocks, cap_big, cap_small)
    f32, bf16, i32 = jnp.float32, jnp.bfloat16, jnp.int32
    vmem, hbm, smem, dma = pltpu.VMEM, pltpu.HBM, pltpu.SMEM, pltpu.SemaphoreType.DMA

    docs_at, blk_at = (lax.axis_index(axis).astype(i32).reshape(1) for axis in ("docs", "blk"))

    def along(x, axis, count, by):
        return lax.ppermute(x, axis, [(i, (i + by) % count) for i in range(count)])

    small_rows = feature // LANES * cap_small + 8
    small_sent, info, *big_sent = call(
        functools.partial(sort_kernel, *sizes),
        [((devices, small_rows, LANES), bf16, hbm), ((8, docs), i32, hbm)] + [((cap_big + 16, feature), bf16, hbm)] * shards,
        [smem, hbm, hbm, hbm],
        2 * docs * feature * (pooled.shape[1] + small_slots), 4 << 20, 60,
        [vmem(pooled.shape, bf16), vmem(proj_weight.shape, bf16), vmem((1, docs), i32),
         vmem((devices, small_rows, LANES), bf16), vmem((shards, cap_big + 16, feature), bf16),
         vmem((docs, feature), bf16), vmem((8, docs), i32), dma((4,)), dma((2,)), dma((shards,))],
    )(docs_at, pooled, proj_weight, cluster.reshape(1, docs))

    got_small = lax.all_to_all(small_sent, ("docs", "blk"), split_axis=0, concat_axis=0, tiled=True)

    held = [big_sent[0]] + [along(big_sent[by], "docs", shards, by) for by in range(1, shards)]
    group, = call(
        functools.partial(group_kernel, cap_big),
        [((big_slots + rows_up(shards, 16), feature), bf16, vmem)], [vmem] * shards,
        big_slots * feature, 1 << 20,
    )(*held)
    parts = [group]
    for step in big_steps(blocks)[1:]:
        pairs = [(d * blocks + (home_of(d, blocks) + step) % blocks, d * blocks + home_of(d, blocks))
                 for d in range(shards)]
        parts.append(lax.ppermute(group, ("docs", "blk"), pairs))

    back_small, = call(
        functools.partial(small_kernel, shards, blocks, cap_small),
        [((blocks * rows_up(shards), LANES), f32, vmem)], [smem, vmem],
        2 * small_slots * small_slots * feature, 2 << 20, 16,
        [vmem((small_slots, feature), bf16)],
    )(blk_at, got_small)
    early, = call(
        functools.partial(big_kernel, shards, cap_big, cap_small),
        [((1, big_total - big_slots), f32, vmem)], [vmem] * (blocks - 1),
        2 * (big_total - big_slots) ** 2 * feature, 2 << 20,
    )(*parts[:-1])
    back = call(
        functools.partial(big_last_kernel, *sizes),
        [((rows_up(shards), LANES), f32, vmem)] * blocks, [smem] + [vmem] * (blocks + 2),
        2 * (2 * big_total - big_slots) * big_slots * feature, 2 << 20,
    )(docs_at, back_small, early, *parts)
    back = [back[0]] + [along(back[by], "blk", blocks, by) for by in range(1, blocks)]
    back = call(
        functools.partial(turn_kernel, shards),
        [((rows_up(blocks), LANES), f32, vmem)] * shards, [smem] + [vmem] * blocks,
        shards * blocks * LANES, 1 << 16,
    )(docs_at, *back)
    back = [back[0]] + [along(back[by], "docs", shards, by) for by in range(1, shards)]

    masks = call(
        functools.partial(masks_kernel, shards, blocks),
        [((3 * shards * rows_up(blocks), docs), bf16, vmem), ((LANES, docs), f32, vmem)], [smem, smem, vmem],
        docs * LANES, 1 << 18,
    )(docs_at, blk_at, info)
    out, = call(
        finish_kernel, [((1, docs), f32, vmem)], [vmem] * (shards + 2),
        6 * docs * LANES * devices, 1 << 18,
    )(*back, *masks)
    return out.reshape(docs)


def solution(mesh):
    in_specs = (P(("slab", "docs", "blk"), None), P(), P(("slab", "docs", "blk")))
    out_specs = P(("slab", "docs", "blk"))
    return jax.shard_map(body, mesh=mesh, in_specs=in_specs, out_specs=out_specs, check_vma=False)
```

```python
import functools

import jax
import jax.numpy as jnp
from jax import lax
from jax.experimental import pallas as pl
from jax.experimental.pallas import tpu as pltpu
from jax.sharding import PartitionSpec as P

BIG_OWN = 4
LANES = 128


def modulo(x, n):
    return x & (n - 1) if n & (n - 1) == 0 else lax.rem(x, jnp.int32(n))


def quotient(x, n):
    if n & (n - 1) == 0:
        return lax.shift_right_logical(x, jnp.int32(n.bit_length() - 1))
    return lax.div(x, jnp.int32(n))


def iota(shape, axis):
    return lax.broadcasted_iota(jnp.int32, shape, axis)


def dot_nt(a, b):
    return lax.dot_general(a, b, (((1,), (1,)), ((), ())), preferred_element_type=jnp.float32)


def tile_of(rows, most=256):
    tile = most
    while rows % tile:
        tile //= 2
    return tile


def home_of(docs, blocks):
    return max(blocks // 2 - 1, 0) + (docs & min(blocks - 1, 1))


def picked_rows(rows_ref, slot, first, count):
    pick = (iota((count, rows_ref.shape[0]), 0) + first == slot).astype(jnp.float32).astype(jnp.bfloat16)
    return jnp.dot(pick, rows_ref[...], preferred_element_type=jnp.float32).astype(jnp.bfloat16)


def sort_kernel(shards, blocks, cap_big, cap_small, docs_at, pooled_hbm, weight_hbm, cluster_hbm, small_hbm, info_hbm,
                *refs):
    big_hbm = refs[:shards]
    (pooled_ref, weight_ref, cluster_ref, small_ref, big_ref, rows_ref, info_ref, sems, small_sems,
     big_sems) = refs[shards:]
    docs, feature = rows_ref.shape
    devices = shards * blocks
    limit = BIG_OWN * shards
    buckets = devices + shards

    fetches = [pltpu.make_async_copy(source, target, sems.at[n]) for n, (source, target) in enumerate(
        ((cluster_hbm, cluster_ref), (weight_hbm, weight_ref), (pooled_hbm, pooled_ref)))]
    for fetch in fetches:
        fetch.start()
    fetches[0].wait()

    cluster = cluster_ref[...]
    is_big = cluster < limit
    owner = modulo(cluster, shards)
    past = jnp.maximum(cluster - limit, 0)
    target = modulo(past, devices)
    bucket = jnp.where(is_big, devices + owner, target)

    padded = -(-buckets // 16) * 16
    hot = (iota((padded, docs), 0) == bucket).astype(jnp.float32)
    earlier = (iota((docs, docs), 0) < iota((docs, docs), 1)).astype(jnp.float32).astype(jnp.bfloat16)
    before = jnp.dot(hot.astype(jnp.bfloat16), earlier, preferred_element_type=jnp.float32)
    rank = jnp.sum(before * hot, axis=0, keepdims=True).astype(jnp.int32)

    info_ref[0:1, :] = jnp.where(is_big, owner * blocks + home_of(owner, blocks), target)
    info_ref[1:2, :] = jnp.where(is_big, cap_small + rank, rank)
    info_ref[2:3, :] = jnp.where(is_big, quotient(cluster, shards), quotient(past, devices)) + 1
    info_ref[3:8, :] = jnp.zeros((5, docs), jnp.int32)
    sends = [pltpu.make_async_copy(info_ref, info_hbm, sems.at[3])]
    sends[0].start()
    small_slot = jnp.where(is_big, -1, target * cap_small + rank)
    ids = ids_table(iota((devices, docs), 0) == bucket, info_ref)
    shift = modulo(owner + shards - docs_at[0], shards)
    big_slot = jnp.where(is_big, shift * cap_big + rank, -1)
    for by in range(shards):
        mine = (iota((16, docs), 0) == 0) & is_big & (shift == by)
        big_ref[by, cap_big:, 0:LANES] = ids_table(mine, info_ref).astype(jnp.bfloat16)
        big_ref[by, cap_big:, LANES:] = jnp.zeros((16, feature - LANES), jnp.bfloat16)

    for fetch in fetches[1:]:
        fetch.wait()
    projected = jnp.dot(pooled_ref[...], weight_ref[...], preferred_element_type=jnp.float32)
    squares = jnp.sum(projected * projected, axis=1, keepdims=True)
    rows_ref[...] = (projected * lax.rsqrt(squares + 1e-06)).astype(jnp.bfloat16)
    picked = picked_rows(rows_ref, big_slot, 0, shards * cap_big)
    for by, out in enumerate(big_hbm):
        big_ref[by, 0:cap_big, :] = picked[by * cap_big:(by + 1) * cap_big, :]
        sends.append(pltpu.make_async_copy(big_ref.at[by], out, big_sems.at[by]))
        sends[-1].start()

    slabs = feature // LANES
    group = devices // small_sems.shape[0]
    for part in range(small_sems.shape[0]):
        first = part * group
        picked = picked_rows(rows_ref, small_slot, first * cap_small, group * cap_small)
        for device in range(group):
            for slab in range(slabs):
                small_ref[first + device, slab * cap_small:(slab + 1) * cap_small, :] = picked[
                    device * cap_small:(device + 1) * cap_small, slab * LANES:(slab + 1) * LANES]
            small_ref[first + device, slabs * cap_small:, :] = jnp.broadcast_to(
                ids[first + device:first + device + 1, :], (8, LANES)).astype(jnp.bfloat16)
        sends.append(pltpu.make_async_copy(
            small_ref.at[pl.ds(first, group)], small_hbm.at[pl.ds(first, group)], small_sems.at[part]))
        sends[-1].start()
    for send in sends:
        send.wait()


def ids_table(mine, info_ref):
    docs = info_ref.shape[1]
    quota = info_ref[2:3, :].astype(jnp.float32)
    lanes = (iota((LANES, docs), 0) == info_ref[1:2, :]).astype(jnp.float32).astype(jnp.bfloat16)
    return dot_nt(jnp.where(mine, quota, 0.0).astype(jnp.bfloat16), lanes)


def group_kernel(cap_big, *refs):
    held, group_ref = refs[:-1], refs[-1]
    total = len(held) * cap_big
    spare = group_ref.shape[0] - total
    own = jnp.zeros((spare, LANES), jnp.float32)
    for shift, ref in enumerate(held):
        group_ref[shift * cap_big:(shift + 1) * cap_big, :] = ref[0:cap_big, :]
        table = ref[cap_big:, 0:LANES].astype(jnp.float32)
        own = jnp.where(iota(own.shape, 0) == shift, table[0:1, :], own)
    group_ref[total:, 0:LANES] = own.astype(jnp.bfloat16)
    group_ref[total:, LANES:] = jnp.zeros((spare, group_ref.shape[1] - LANES), jnp.bfloat16)


def turn(tables, at, count, outs):
    for step, out in enumerate(outs):
        to = modulo(at + step, count)
        out[...] = jnp.zeros(out.shape, jnp.float32)
        for place, table in enumerate(tables):
            out[place:place + 1, :] = jnp.sum(
                jnp.where(iota(table.shape, 0) == to, table, 0.0), axis=0, keepdims=True)


def turn_kernel(count, at_ref, *refs):
    held, outs = refs[:-count], refs[-count:]
    turn([ref[...] for ref in held], at_ref[0], count, outs)


def rows_up(count, to=8):
    return -(-count // to) * to


def small_sources(total, blocks, cap_small):
    at = iota((1, total), 1)
    source = at // cap_small
    return source // blocks, modulo(source, blocks), lax.rem(at, jnp.int32(cap_small))


def big_steps(blocks):
    return [step for step in range(blocks) if step != blocks // 2] + ([blocks // 2] if blocks > 1 else [])


def big_sources(total, shards, cap_big, cap_small):
    at = iota((1, total), 1)
    return (at // (shards * cap_big), modulo(at // cap_big, shards),
            cap_small + lax.rem(at, jnp.int32(cap_big)))


def big_ids(held, sources):
    part, shift, lane = sources
    spare = held[0].shape[0] - part.shape[1] // len(held)
    values = jnp.concatenate([ref[ref.shape[0] - spare:, 0:LANES] for ref in held], axis=0)
    return ids_from(values, part * spare + shift, lane)


def big_pairs(held, row_ids, col_ids, bests, pairs):
    size = row_ids.shape[1] // len(held)
    for row, col in pairs:
        same = 0 if row == col else None
        bests[col] = jnp.maximum(bests[col], block_best(
            held[row][0:size, :], col_ids[row * size:(row + 1) * size], same,
            held[col][0:size, :], row_ids[:, col * size:(col + 1) * size], same))
    return bests


def ids_from(values, row, lane):
    pick = (iota((LANES, lane.shape[1]), 0) == lane).astype(jnp.float32).astype(jnp.bfloat16)
    found = jnp.dot(values, pick, preferred_element_type=jnp.float32)
    return jnp.sum(jnp.where(iota(found.shape, 0) == row, found, 0.0), axis=0, keepdims=True)


def as_column(row):
    return jnp.broadcast_to(row, (8, row.shape[1])).T[:, 0:1]


def block_best(queries, col_ids, first_row, others, row_ids, first_col):
    scores = dot_nt(queries, others)
    allowed = (col_ids == row_ids) & (row_ids > 0.0)
    if first_row is not None:
        allowed &= (iota(scores.shape, 0) + first_row) != (iota(scores.shape, 1) + first_col)
    return jnp.max(jnp.where(allowed, scores, -1.0), axis=0, keepdims=True)


def spread(best, row, lane, rows):
    total = best.shape[1]
    mine = jnp.where(iota((rows, total), 0) == row, best, 0.0)
    place = (iota((LANES, total), 0) == lane).astype(jnp.float32).astype(jnp.bfloat16)
    found = dot_nt(thirds(mine), place)
    return found[:rows] + found[rows:2 * rows] + found[2 * rows:]


def thirds(values):
    high = values.astype(jnp.bfloat16)
    rest = values - high.astype(jnp.float32)
    middle = rest.astype(jnp.bfloat16)
    low = (rest - middle.astype(jnp.float32)).astype(jnp.bfloat16)
    return jnp.concatenate([high, middle, low], axis=0)


def big_kernel(shards, cap_big, cap_small, *refs):
    held, best_ref = refs[:-1], refs[-1]
    size = shards * cap_big
    row_ids = big_ids(held, big_sources(len(held) * size, shards, cap_big, cap_small))
    col_ids = as_column(row_ids)
    pairs = [(row, col) for row in range(len(held)) for col in range(len(held))]
    bests = big_pairs(held, row_ids, col_ids, [jnp.full((1, size), -1.0, jnp.float32)] * len(held), pairs)
    best_ref[...] = jnp.concatenate(bests, axis=1)


def big_last_kernel(shards, blocks, cap_big, cap_small, docs_at, small_ref, best_ref, *refs):
    held, back_refs = refs[:blocks], refs[blocks:]
    size = shards * cap_big
    high = back_refs[0].shape[0]
    part, shift, lane = big_sources(blocks * size, shards, cap_big, cap_small)
    row_ids = big_ids(held, (part, shift, lane))
    col_ids = as_column(row_ids)
    last = blocks - 1
    pairs = [(row, last) for row in range(blocks)] + [(last, col) for col in range(last)]
    bests = [best_ref[:, col * size:(col + 1) * size] for col in range(last)]
    bests = big_pairs(held, row_ids, col_ids, bests + [jnp.full((1, size), -1.0, jnp.float32)], pairs)
    docs = modulo(docs_at[0] + shards - shift, shards)
    step = jnp.where(part == last, blocks // 2, jnp.where(part < blocks // 2, part, part + 1))
    back = small_ref[...] + spread(jnp.concatenate(bests, axis=1), step * high + docs, lane, small_ref.shape[0])
    for at, ref in enumerate(back_refs):
        ref[...] = back[at * high:(at + 1) * high, :]


def small_kernel(shards, blocks, cap_small, blk_at, got_ref, back_ref, rows_ref):
    total, feature = rows_ref.shape
    high = back_ref.shape[0] // blocks
    slabs = feature // LANES
    values = []
    for device in range(got_ref.shape[0]):
        for slab in range(slabs):
            rows_ref[device * cap_small:(device + 1) * cap_small, slab * LANES:(slab + 1) * LANES] = got_ref[
                device, slab * cap_small:(slab + 1) * cap_small, :]
        values.append(got_ref[device, slabs * cap_small:, :].astype(jnp.float32)[0:1, :])
    docs, blk, lane = small_sources(total, blocks, cap_small)
    row_ids = ids_from(jnp.concatenate(values, axis=0).astype(jnp.bfloat16), docs * blocks + blk, lane)
    col_ids = as_column(row_ids)
    tile = tile_of(total)
    best = jnp.full((1, total), -1.0, jnp.float32)
    for at in range(0, total, tile):
        best = jnp.maximum(best, block_best(
            rows_ref[at:at + tile, :], col_ids[at:at + tile], at, rows_ref[...], row_ids, 0))
    row = modulo(blk + blocks - blk_at[0], blocks) * high + docs
    back_ref[...] = spread(best, row, lane, back_ref.shape[0])


def masks_kernel(shards, blocks, docs_at, blk_at, info_ref, row_ref, lane_ref):
    device = info_ref[0:1, :]
    high = row_ref.shape[0] // (3 * shards)
    row = (modulo(docs_at[0] + shards - device // blocks, shards) * high
           + modulo(blk_at[0] + blocks - modulo(device, blocks), blocks))
    mask = (iota((shards * high, row_ref.shape[1]), 0) == row).astype(jnp.float32)
    row_ref[...] = jnp.concatenate([mask] * 3, axis=0).astype(jnp.bfloat16)
    lane_ref[...] = (iota(lane_ref.shape, 0) == info_ref[1:2, :]).astype(jnp.float32)


def finish_kernel(*refs):
    held, (row_ref, lane_ref, out_ref) = refs[:-3], refs[-3:]
    values = thirds(jnp.concatenate([ref[...] for ref in held], axis=0))
    found = lax.dot_general(values, row_ref[...], (((0,), (0,)), ((), ())), preferred_element_type=jnp.float32)
    out_ref[...] = jnp.sum(jnp.where(lane_ref[...] > 0.0, found, 0.0), axis=0, keepdims=True)


def call(kernel, outs, ins, flops, moved, limit=16, scratch=()):
    specs = [pl.BlockSpec(memory_space=space) for _, _, space in outs]
    return pl.pallas_call(
        kernel,
        out_shape=[space(shape, dtype) if space is pltpu.HBM else jax.ShapeDtypeStruct(shape, dtype)
                   for shape, dtype, space in outs],
        in_specs=[pl.BlockSpec(memory_space=space) for space in ins],
        out_specs=specs,
        scratch_shapes=scratch,
        cost_estimate=pl.CostEstimate(flops=flops, bytes_accessed=moved, transcendentals=0),
        compiler_params=pltpu.CompilerParams(vmem_limit_bytes=limit << 20),
    )


def body(pooled, proj_weight, cluster):
    shards = lax.axis_size("docs")
    blocks = lax.axis_size("blk")
    devices = shards * blocks
    docs = pooled.shape[0]
    feature = proj_weight.shape[1]
    big_count = docs // 4
    small_count = docs - big_count
    cap_big = 2 * big_count // shards
    cap_small = rows_up(2 * small_count // devices, 16)
    small_slots = devices * cap_small
    big_slots = shards * cap_big
    big_total = blocks * big_slots
    sizes = (shards, blocks, cap_big, cap_small)
    f32, bf16, i32 = jnp.float32, jnp.bfloat16, jnp.int32
    vmem, hbm, smem, dma = pltpu.VMEM, pltpu.HBM, pltpu.SMEM, pltpu.SemaphoreType.DMA

    docs_at, blk_at = (lax.axis_index(axis).astype(i32).reshape(1) for axis in ("docs", "blk"))

    def along(x, axis, count, by):
        return lax.ppermute(x, axis, [(i, (i + by) % count) for i in range(count)])

    small_rows = feature // LANES * cap_small + 8
    small_sent, info, *big_sent = call(
        functools.partial(sort_kernel, *sizes),
        [((devices, small_rows, LANES), bf16, hbm), ((8, docs), i32, hbm)] + [((cap_big + 16, feature), bf16, hbm)] * shards,
        [smem, hbm, hbm, hbm],
        2 * docs * feature * (pooled.shape[1] + small_slots), 4 << 20, 60,
        [vmem(pooled.shape, bf16), vmem(proj_weight.shape, bf16), vmem((1, docs), i32),
         vmem((devices, small_rows, LANES), bf16), vmem((shards, cap_big + 16, feature), bf16),
         vmem((docs, feature), bf16), vmem((8, docs), i32), dma((4,)), dma((4,)), dma((shards,))],
    )(docs_at, pooled, proj_weight, cluster.reshape(1, docs))

    got_small = lax.all_to_all(small_sent, ("docs", "blk"), split_axis=0, concat_axis=0, tiled=True)

    held = [big_sent[0]] + [along(big_sent[by], "docs", shards, by) for by in range(1, shards)]
    group, = call(
        functools.partial(group_kernel, cap_big),
        [((big_slots + rows_up(shards, 16), feature), bf16, vmem)], [vmem] * shards,
        big_slots * feature, 64 << 20,
    )(*held)
    parts = [group]
    for step in big_steps(blocks)[1:]:
        pairs = [(d * blocks + (home_of(d, blocks) + step) % blocks, d * blocks + home_of(d, blocks))
                 for d in range(shards)]
        parts.append(lax.ppermute(group, ("docs", "blk"), pairs))

    back_small, = call(
        functools.partial(small_kernel, shards, blocks, cap_small),
        [((blocks * rows_up(shards), LANES), f32, vmem)], [smem, vmem],
        2 * small_slots * small_slots * feature, 2 << 20, 16,
        [vmem((small_slots, feature), bf16)],
    )(blk_at, got_small)
    early, = call(
        functools.partial(big_kernel, shards, cap_big, cap_small),
        [((1, big_total - big_slots), f32, vmem)], [vmem] * (blocks - 1),
        2 * (big_total - big_slots) ** 2 * feature, 2 << 20,
    )(*parts[:-1])
    back = call(
        functools.partial(big_last_kernel, *sizes),
        [((rows_up(shards), LANES), f32, vmem)] * blocks, [smem] + [vmem] * (blocks + 2),
        2 * (2 * big_total - big_slots) * big_slots * feature, 2 << 20,
    )(docs_at, back_small, early, *parts)
    back = [back[0]] + [along(back[by], "blk", blocks, by) for by in range(1, blocks)]
    back = call(
        functools.partial(turn_kernel, shards),
        [((rows_up(blocks), LANES), f32, vmem)] * shards, [smem] + [vmem] * blocks,
        shards * blocks * LANES, 1 << 16,
    )(docs_at, *back)
    back = [back[0]] + [along(back[by], "docs", shards, by) for by in range(1, shards)]

    masks = call(
        functools.partial(masks_kernel, shards, blocks),
        [((3 * shards * rows_up(blocks), docs), bf16, vmem), ((LANES, docs), f32, vmem)], [smem, smem, vmem],
        docs * LANES, 1 << 18,
    )(docs_at, blk_at, info)
    out, = call(
        finish_kernel, [((1, docs), f32, vmem)], [vmem] * (shards + 2),
        6 * docs * LANES * devices, 1 << 18,
    )(*back, *masks)
    return out.reshape(docs)


def solution(mesh):
    in_specs = (P(("slab", "docs", "blk"), None), P(), P(("slab", "docs", "blk")))
    out_specs = P(("slab", "docs", "blk"))
    return jax.shard_map(body, mesh=mesh, in_specs=in_specs, out_specs=out_specs, check_vma=False)
```
